32 devices in a mesh: dp: 16 (over z, y, x), seq: 2 (over core).
Axes of the slice: x: 2, y: 2, z: 4, core: 2. Of those that a mesh axis runs over, the one named last changes fastest.
Arguments:
- source: bfloat16 [32, 1024, 512], P('dp', 'seq'), may hold values from -6 to 6
- canvas: bfloat16 [32, 1024, 512], P('dp', 'seq'), may hold values from -6 to 6
- source_len: int32 [32], P('dp'), may hold values from 256 to 1024, as said below
- canvas_len: int32 [32], P('dp'), may hold values from 256 to 1024, as said below
- cotangent: bfloat16 [32, 1024, 512], P('dp', 'seq'), may hold values from -6 to 6
- enc_attn: bfloat16 [4, 512, 512], P(None, ('dp', 'seq'))
- enc_up: bfloat16 [512, 2048], P(('dp', 'seq')), may hold values from -0.25 to 0.25
- enc_down: bfloat16 [2048, 512], P(('dp', 'seq')), may hold values from -0.125 to 0.125
- dec_attn: bfloat16 [4, 512, 512], P(None, ('dp', 'seq'))
- cross_attn: bfloat16 [4, 512, 512], P(None, ('dp', 'seq'))
- dec_up: bfloat16 [512, 2048], P(('dp', 'seq')), may hold values from -0.25 to 0.25
- dec_down: bfloat16 [2048, 512], P(('dp', 'seq')), may hold values from -0.125 to 0.125
- slot_proj: bfloat16 [1024, 512], P(('dp', 'seq')), may hold values from -0.1875 to 0.1875
- norm_gains: bfloat16 [5, 512], P(None, ('dp', 'seq')), may hold values from 0.25 to 1.75
Outputs:
- slot_out: bfloat16 [32, 1024, 512], P('dp', 'seq')
- source_grad: float32 [32, 1024, 512], P('dp', 'seq')
- canvas_grad: float32 [32, 1024, 512], P('dp', 'seq')
- enc_attn_grad: float32 [4, 512, 512], P(None, ('dp', 'seq'))
- enc_up_grad: float32 [512, 2048], P(('dp', 'seq'))
- enc_down_grad: float32 [2048, 512], P(('dp', 'seq'))
- dec_attn_grad: float32 [4, 512, 512], P(None, ('dp', 'seq'))
- cross_attn_grad: float32 [4, 512, 512], P(None, ('dp', 'seq'))
- dec_up_grad: float32 [512, 2048], P(('dp', 'seq'))
- dec_down_grad: float32 [2048, 512], P(('dp', 'seq'))
- slot_proj_grad: float32 [1024, 512], P(('dp', 'seq'))
- norm_gains_grad: float32 [5, 512], P(None, ('dp', 'seq'))
The draws below stay inside these ranges and needn't reach their ends.
Inputs may be any that keep to these rules, and one draw needn't show every extreme that they name: `source_len`: in the examples of each index of dp one source is 1024 long. `canvas_len`: in the examples of each index of dp one canvas is 1024 long.
All inputs are finite; a program needn't handle non-finite values.
Results may differ from the reference program's by a relative error of at most 0.02.
Values may be sent and summed in bfloat16 or wider, within the bound.
No kernel may reach another device: no remote copies, remote signals or barrier semaphores. Data moves between devices by JAX's collectives and lax.ppermute only.
A program may use at most 256 MiB of HBM per device.

```python
import math
import jax
import jax.numpy as jnp
from jax import lax

D = 512
H = 8
FF = 2048
HD = 64
SRC = 1024
CAN = 1024
MB = 2
EXM = 1
EX = 32


def lengths_for(key, longest):
    group_size = MB * EXM
    first_key, second_key = jax.random.split(key)
    spread = jax.random.randint(first_key, (EX,), longest // 4, longest + 1)
    picked = jax.random.randint(second_key, (EX // group_size,), 0, group_size)
    position = jnp.arange(EX) % group_size
    chosen = jnp.repeat(picked, group_size)
    return jnp.where(position == chosen, longest, spread).astype(jnp.int32)


def attention_stack(key, keys_seen):
    stacked = jax.random.normal(key, (4, D, D), jnp.float32)
    factor = jnp.array([1.0, 1.0, 1.0, math.sqrt(keys_seen) / 4.0], jnp.float32) * D ** (-0.5)
    return stacked * factor[:, None, None]


def draw_source_len(key, part):
    key = jax.random.fold_in(key, 1)
    return lengths_for(key, SRC)


def draw_canvas_len(key, part):
    key = jax.random.fold_in(key, 2)
    return lengths_for(key, CAN)


def draw_enc_attn(key, part):
    key = jax.random.fold_in(key, 3)
    return attention_stack(key, SRC).astype(jnp.bfloat16)


def draw_dec_attn(key, part):
    key = jax.random.fold_in(key, 4)
    return attention_stack(key, CAN).astype(jnp.bfloat16)


def draw_cross_attn(key, part):
    key = jax.random.fold_in(key, 5)
    return attention_stack(key, SRC).astype(jnp.bfloat16)


def level_of(own_key, extent, shards, smallest, high):
    def one(dim, blocks):
        steps = jax.random.uniform(jax.random.fold_in(jax.random.fold_in(own_key, 6), dim), (blocks,), jnp.float32, smallest / len(shards), high / len(shards))
        return jnp.repeat(jnp.exp(steps), extent[dim] // blocks).reshape((-1,) + (1,) * (len(extent) - dim - 1))

    level = one(*shards[0])
    for cut in shards[1:]:
        level = level * one(*cut)
    return level


def gaussian(rng, extent, scale, most, shards=(), dtype=jnp.bfloat16):
    values = jax.random.normal(rng, extent, jnp.float32) * scale
    if len(shards) > 0:
        values = level_of(rng, extent, shards, -0.22, 0.18) * values
    return jnp.clip(values, min=-most, max=most).astype(dtype)


def setup_inputs(seed: int = 0) -> dict:
    arg_keys = jax.random.split(jax.random.key(seed), 15)
    return {
        "source": gaussian(arg_keys[0], (EX, SRC, D), 1.0, 6.0, ((0, 16), (1, 2))),
        "canvas": gaussian(arg_keys[1], (EX, CAN, D), 1.0, 6.0, ((0, 16), (1, 2))),
        "source_len": draw_source_len(jax.random.fold_in(arg_keys[14], 71), 0),
        "canvas_len": draw_canvas_len(jax.random.fold_in(arg_keys[14], 71), 0),
        "cotangent": gaussian(arg_keys[4], (EX, CAN, D), 1.0, 6.0, ((0, 16), (1, 2))),
        "enc_attn": draw_enc_attn(jax.random.fold_in(arg_keys[14], 71), 0),
        "enc_up": gaussian(arg_keys[6], (D, FF), D ** -0.5, 0.25, ((0, 32),)),
        "enc_down": gaussian(arg_keys[7], (FF, D), FF ** -0.5, 0.125, ((0, 32),)),
        "dec_attn": draw_dec_attn(jax.random.fold_in(arg_keys[14], 71), 0),
        "cross_attn": draw_cross_attn(jax.random.fold_in(arg_keys[14], 71), 0),
        "dec_up": gaussian(arg_keys[10], (D, FF), D ** -0.5, 0.25, ((0, 32),)),
        "dec_down": gaussian(arg_keys[11], (FF, D), FF ** -0.5, 0.125, ((0, 32),)),
        "slot_proj": gaussian(arg_keys[12], (2 * D, D), (2 * D) ** -0.5, 0.1875, ((0, 32),)),
        "norm_gains": jnp.clip(1.0 + 0.15 * jax.random.normal(arg_keys[13], (5, D), jnp.float32), 0.25, 1.75).astype(jnp.bfloat16),
    }


HIGHEST = lax.Precision.HIGHEST

@jax.custom_vjp
def low(v):
    return lax.optimization_barrier(v.astype(jnp.bfloat16)).astype(jnp.float32)

@jax.custom_vjp
def low_back(v):
    return v

def low_keep(v):
    return (low(v), None)

def low_pass(kept, grad):
    return (grad,)

def back_keep(v):
    return (v, None)

def back_low(kept, grad):
    return (low(grad),)
low.defvjp(low_keep, low_pass)
low_back.defvjp(back_keep, back_low)

def round_both(value):
    return low_back(low(value))

def matmul(left, right):
    return jnp.dot(left, right, precision=HIGHEST)

def layer_norm(residual, gain_row):
    centre = residual - lax.optimization_barrier(jnp.mean(residual, axis=-1, keepdims=True))
    spread = lax.optimization_barrier(jnp.mean(centre * centre, axis=-1, keepdims=True))
    return centre * lax.rsqrt(spread + 1e-05) * gain_row

def attention(query_in, key_in, weights, length):
    query_rows = query_in.shape[0]
    key_count = key_in.shape[0]
    queries = round_both(matmul(query_in, weights[0]))
    key_proj = round_both(matmul(key_in, weights[1]))
    values = round_both(matmul(key_in, weights[2]))
    q_heads = queries.reshape(query_rows, H, HD)
    k_heads = key_proj.reshape(key_count, H, HD)
    v_heads = values.reshape(key_count, H, HD)
    scores = low_back(jnp.einsum('qhd,khd->hqk', q_heads, k_heads, precision=HIGHEST) * 0.125)
    visible = jnp.arange(key_count) < length
    scores = jnp.where(visible[None, None, :], scores, -1e+30)
    highest = lax.optimization_barrier(jnp.max(scores, axis=-1, keepdims=True))
    exponent = jnp.exp(scores - highest)
    softmax_w = low(exponent / lax.optimization_barrier(jnp.sum(exponent, axis=-1, keepdims=True)))
    blended = jnp.einsum('hqk,khd->qhd', softmax_w, v_heads, precision=HIGHEST)
    blended = round_both(blended.reshape(query_rows, D))
    return low_back(matmul(blended, weights[3]))

def feed_forward(hidden, up_weight, down_weight):
    inner = low_back(matmul(low(hidden), up_weight))
    activated = low(jax.nn.gelu(inner, approximate=False))
    return low_back(matmul(activated, down_weight))

def forward(source_x, canvas_x, enc_attn, enc_up, enc_down, dec_attn, cross_attn, dec_up, dec_down, slot_proj, norm_gains, source_count, canvas_count):
    hidden_one = layer_norm(source_x + attention(source_x, source_x, enc_attn, source_count), norm_gains[0])
    encoded = layer_norm(hidden_one + feed_forward(hidden_one, enc_up, enc_down), norm_gains[1])
    dec_one = layer_norm(canvas_x + attention(canvas_x, canvas_x, dec_attn, canvas_count), norm_gains[2])
    dec_two = layer_norm(dec_one + attention(low(dec_one), low(encoded), cross_attn, source_count), norm_gains[3])
    dec_three = layer_norm(dec_two + feed_forward(dec_two, dec_up, dec_down), norm_gains[4])
    rounded = low(dec_three)
    following = jnp.concatenate([rounded[1:], jnp.zeros((1, D), jnp.float32)], axis=0)
    paired = jnp.concatenate([rounded, following], axis=1)
    slot_values = matmul(paired, slot_proj)
    slot_mask = jnp.arange(CAN) < canvas_count - 1
    return jnp.where(slot_mask[:, None], slot_values, 0.0)

def reference(source, canvas, source_len, canvas_len, cotangent, enc_attn, enc_up, enc_down, dec_attn, cross_attn, dec_up, dec_down, slot_proj, norm_gains):
    weights = tuple((w.astype(jnp.float32) for w in (enc_attn, enc_up, enc_down, dec_attn, cross_attn, dec_up, dec_down, slot_proj, norm_gains)))

    def one_example(running, example):
        source_x, canvas_x, source_count, canvas_count, incoming = example

        def closed(src_in, can_in, *params):
            return forward(src_in, can_in, *params, source_count, canvas_count)
        result, pullback = jax.vjp(closed, source_x.astype(jnp.float32), canvas_x.astype(jnp.float32), *weights)
        gradients = pullback(incoming.astype(jnp.float32))
        running = tuple((a + b for a, b in zip(running, gradients[2:])))
        return (running, (result.astype(jnp.bfloat16), gradients[0], gradients[1]))
    zeroed = tuple((jnp.zeros_like(w) for w in weights))
    totals, stacked = lax.scan(one_example, zeroed, (source, canvas, source_len, canvas_len, cotangent))
    slot_out, source_grad, canvas_grad = stacked
    return (slot_out, source_grad, canvas_grad, totals[0], totals[1], totals[2], totals[3], totals[4], totals[5], totals[6], totals[7], totals[8])
```

```python
import functools
import math

import jax
import jax.numpy as jnp
from jax import lax
from jax.experimental import pallas as pl
from jax.experimental.pallas import tpu as pltpu
from jax.sharding import PartitionSpec as P

F32 = jnp.float32
BF16 = jnp.bfloat16
H = 8
HD = 64
PAIR = 2 * HD
LOG2E = math.log2(math.e)
Q_SCALE = LOG2E / 8.0
K_BACK = 1.0 / LOG2E
MASKED = -1e30
VMEM_LIMIT = 58 * 1024 * 1024
PARAMS = pltpu.CompilerParams(vmem_limit_bytes=VMEM_LIMIT)


def nn(a, b):
    return lax.dot_general(a, b, (((1,), (0,)), ((), ())), preferred_element_type=F32)


def nt(a, b):
    return lax.dot_general(a, b, (((1,), (1,)), ((), ())), preferred_element_type=F32)


def tn(a, b):
    return lax.dot_general(a, b, (((0,), (0,)), ((), ())), preferred_element_type=F32)


def norm_parts(r):
    centre = r - jnp.mean(r, axis=-1, keepdims=True)
    rs = lax.rsqrt(jnp.mean(centre * centre, axis=-1, keepdims=True) + 1e-5)
    return centre * rs, rs


def norm(r, gain):
    return norm_parts(r)[0] * gain


def norm_back(r, gain, dy):
    z, rs = norm_parts(r)
    t = dy * gain
    dr = (t - jnp.mean(t, axis=-1, keepdims=True) - z * jnp.mean(t * z, axis=-1, keepdims=True)) * rs
    return dr, jnp.sum(dy * z, axis=0, keepdims=True)


def lanes(rows):
    return lax.broadcasted_iota(jnp.int32, (rows, PAIR), 1)


def key_extras(length, count):
    row = lax.broadcasted_iota(jnp.int32, (count, PAIR), 0)
    lane = lanes(count)
    bias = jnp.where(row < length, 0.0, MASKED)
    return jnp.where(lane == 3, bias, jnp.where(lane < 3, 1.0, 0.0)).astype(BF16)


def three_parts(v):
    hi = v.astype(BF16)
    rest = v - hi.astype(F32)
    mid = rest.astype(BF16)
    low = rest - mid.astype(F32)
    return hi.astype(F32), mid.astype(F32), low


def spread_parts(v, last):
    lane = lanes(v.shape[0])
    hi, mid, low = three_parts(v)
    tail = jnp.where(lane == 3, last, 0.0)
    return jnp.where(lane == 0, hi, jnp.where(lane == 1, mid, jnp.where(lane == 2, low, tail))).astype(BF16)


def whole(shape):
    return pl.BlockSpec(shape, lambda i: (0,) * len(shape))


def smem():
    return pl.BlockSpec(memory_space=pltpu.SMEM)


def cost(flops, nbytes, exps=0):
    return pl.CostEstimate(flops=int(flops), bytes_accessed=int(nbytes), transcendentals=int(exps))


def attn_fwd_kernel(cross, *refs):
    if cross:
        (len_ref, rq_ref, rk_ref, gq_ref, gk_ref, w_ref,
         xq_ref, xk_ref, q_ref, k_ref, v_ref, o_ref, qx_ref, r_ref, kaug, vaug) = refs
    else:
        len_ref, xq_ref, xk_ref, w_ref, q_ref, k_ref, v_ref, o_ref, qx_ref, r_ref, kaug, vaug = refs
    count = kaug.shape[1]
    rows = r_ref.shape[0]

    @pl.when(pl.program_id(0) == 0)
    def _():
        if cross:
            xk_ref[...] = norm(rk_ref[...], gk_ref[...]).astype(BF16)
        xk = xk_ref[...]
        k = nn(xk, w_ref[1]).astype(BF16)
        v = nn(xk, w_ref[2]).astype(BF16)
        k_ref[...] = k
        v_ref[...] = v
        extras = key_extras(len_ref[0], count)
        ones = jnp.ones((count, PAIR), BF16)
        for p in range(H // 2):
            kaug[p, :, :PAIR] = k[:, p * PAIR:(p + 1) * PAIR]
            kaug[p, :, PAIR:] = extras
            vaug[p, :, :PAIR] = v[:, p * PAIR:(p + 1) * PAIR]
            vaug[p, :, PAIR:] = ones

    if cross:
        resid = norm(rq_ref[...], gq_ref[...])
        xq = resid.astype(BF16)
        xq_ref[...] = xq
    else:
        xq = xq_ref[...]
        resid = xq.astype(F32)
    q = nn(xq, w_ref[0]) * Q_SCALE
    q_ref[...] = q.astype(BF16)
    lane = lanes(rows)
    first = lane < HD
    extra = jnp.where(lane == 3, 1.0, 0.0).astype(BF16)
    blended = []
    for p in range(H // 2):
        qp = q[:, p * PAIR:(p + 1) * PAIR]
        halves = []
        for h in range(2):
            qm = jnp.where(first if h == 0 else lane >= HD, qp, 0.0).astype(BF16)
            s = nt(jnp.concatenate([qm, extra], axis=1), kaug[p])
            m = jnp.max(s, axis=1, keepdims=True)
            e = jnp.exp2(s - m).astype(BF16)
            o = nn(e, vaug[p])
            total = o[:, PAIR:]
            halves.append(o[:, :PAIR] / total)
            qx_ref[2 * p + h] = spread_parts(-(m + jnp.log2(total)), 1.0)
        blended.append(jnp.where(first, halves[0], halves[1]).astype(BF16))
    o_all = jnp.concatenate(blended, axis=1)
    o_ref[...] = o_all
    r_ref[...] = resid + nn(o_all, w_ref[3])


def attn_forward(length, w, xq=None, xk=None, rq=None, rk=None, gq=None, gk=None):
    cross = rq is not None
    rows, width = (rq if cross else xq).shape
    count = (rk if cross else xk).shape[0]
    blk = math.gcd(rows, 256)
    sds = jax.ShapeDtypeStruct
    by_rows = pl.BlockSpec((blk, width), lambda i: (i, 0))
    outs = [
        sds((rows, width), BF16), sds((count, width), BF16), sds((count, width), BF16),
        sds((rows, width), BF16), sds((H, rows, PAIR), BF16), sds((rows, width), F32),
    ]
    out_specs = [
        by_rows, whole((count, width)), whole((count, width)),
        by_rows, pl.BlockSpec((H, blk, PAIR), lambda i: (0, i, 0)), by_rows,
    ]
    if cross:
        args = (length, rq, rk, gq, gk, w)
        in_specs = [smem(), by_rows, whole((count, width)), whole((1, width)), whole((1, width)), whole(w.shape)]
        outs = [sds((rows, width), BF16), sds((count, width), BF16)] + outs
        out_specs = [by_rows, whole((count, width))] + out_specs
    else:
        args = (length, xq, xk, w)
        in_specs = [smem(), by_rows, whole((count, width)), whole(w.shape)]
    return pl.pallas_call(
        functools.partial(attn_fwd_kernel, cross),
        grid=(rows // blk,),
        in_specs=in_specs,
        out_specs=out_specs,
        out_shape=outs,
        scratch_shapes=[pltpu.VMEM((H // 2, count, 2 * PAIR), BF16), pltpu.VMEM((H // 2, count, 2 * PAIR), BF16)],
        compiler_params=PARAMS,
        cost_estimate=cost(rows * count * 2 * 512 * H, 14 << 20, rows * count * H),
        name="cross_fwd" if cross else "self_fwd",
    )(*args)


def attn_bwd_kernel(same, len_ref, dy_ref, r_ref, g_ref, w_ref, q_ref, k_ref, v_ref, o_ref, qx_ref, xq_ref, xk_ref,
                    *refs):
    if same:
        dw_ref, dg_ref, dxq_ref = refs[:3]
        dxk_ref = None
        scratch = refs[3:]
    else:
        dw_ref, dg_ref, dxq_ref, dxk_ref = refs[:4]
        scratch = refs[4:]
    dr, dab, kaug, vaug, qaug, oaug, kt, dqt, dq, dk, dv = scratch
    count = kaug.shape[0]
    rows = dr.shape[0]
    blk = math.gcd(count, 256)
    p = pl.program_id(0)

    @pl.when(p == 0)
    def _():
        grad, dg = norm_back(r_ref[...], g_ref[...], dy_ref[...])
        dg_ref[...] = dg
        dr[...] = grad
        dab[...] = grad.astype(BF16)
        kaug[:, PAIR:] = key_extras(len_ref[0], count)
        vaug[:, PAIR:] = jnp.where(lanes(count) < 3, 1.0, 0.0).astype(BF16)

    cols = pl.ds(pl.multiple_of(p * PAIR, PAIR), PAIR)
    out_rows = w_ref[3, cols, :]
    do = nt(dab[...], out_rows).astype(BF16).astype(F32)
    o = o_ref[...]
    dw_ref[3, cols, :] = tn(o, dab[...]).astype(BF16)
    inner = do * o.astype(F32)
    kaug[:, :PAIR] = k_ref[...]
    vaug[:, :PAIR] = v_ref[...]
    kt[...] = k_ref[...].T
    lane = lanes(rows)
    q = q_ref[...].astype(F32)
    for h in range(2):
        mine = lane < HD if h == 0 else lane >= HD
        qaug[h, :, :PAIR] = jnp.where(mine, q, 0.0).astype(BF16)
        qaug[h, :, PAIR:] = qx_ref[h]
        oaug[h, :, :PAIR] = jnp.where(mine, do, 0.0).astype(BF16)
        d = jnp.sum(jnp.where(mine, inner, 0.0), axis=1, keepdims=True)
        oaug[h, :, PAIR:] = spread_parts(jnp.broadcast_to(-d, (rows, PAIR)), 0.0)
    for j in range(count // blk):
        keys = slice(j * blk, (j + 1) * blk)
        dv_sum = dk_sum = None
        for h in range(2):
            st = nt(kaug[keys, :], qaug[h])
            pt = jnp.exp2(st)
            dpt = nt(vaug[keys, :], oaug[h])
            ptb = pt.astype(BF16)
            dst = (pt * dpt).astype(BF16)
            dv_h = nn(ptb, oaug[h, :, :PAIR])
            dk_h = nn(dst, qaug[h, :, :PAIR])
            dq_h = nn(kt[h * HD:(h + 1) * HD, keys], dst)
            dv_sum = dv_h if h == 0 else dv_sum + dv_h
            dk_sum = dk_h if h == 0 else dk_sum + dk_h
            if j == 0:
                dqt[h * HD:(h + 1) * HD, :] = dq_h
            else:
                dqt[h * HD:(h + 1) * HD, :] += dq_h
        dv[keys, cols] = dv_sum.astype(BF16)
        dk[keys, cols] = (dk_sum * K_BACK).astype(BF16)
    dq[:, cols] = (dqt[...].T * 0.125).astype(BF16)

    @pl.when(p == pl.num_programs(0) - 1)
    def _():
        xqt = xq_ref[...].T
        xkt = xk_ref[...].T
        dw_ref[0] = nn(xqt, dq[...]).astype(BF16)
        dw_ref[1] = nn(xkt, dk[...]).astype(BF16)
        dw_ref[2] = nn(xkt, dv[...]).astype(BF16)
        dxq = dr[...] + nt(dq[...], w_ref[0])
        dxk = nt(dk[...], w_ref[1]) + nt(dv[...], w_ref[2])
        if same:
            dxq_ref[...] = dxq + dxk
        else:
            dxq_ref[...] = dxq
            dxk_ref[...] = dxk


def attn_backward(same, length, dy, r, gain, w, q, k, v, o, qx, xq, xk):
    rows, width = r.shape
    count = k.shape[0]
    sds = jax.ShapeDtypeStruct
    pair_of = lambda n: pl.BlockSpec((n, PAIR), lambda i: (0, i))
    in_specs = [
        smem(), whole((rows, width)), whole((rows, width)), whole((1, width)), whole(w.shape),
        pair_of(rows), pair_of(count), pair_of(count), pair_of(rows),
        pl.BlockSpec((2, rows, PAIR), lambda i: (i, 0, 0)), whole((rows, width)), whole((count, width)),
    ]
    outs = [sds(w.shape, BF16), sds((1, width), F32), sds((rows, width), F32)]
    if not same:
        outs.append(sds((count, width), F32))
    vm = pltpu.VMEM
    return pl.pallas_call(
        functools.partial(attn_bwd_kernel, same),
        grid=(H // 2,),
        in_specs=in_specs,
        out_specs=[whole(s.shape) for s in outs],
        out_shape=outs,
        scratch_shapes=[
            vm((rows, width), F32), vm((rows, width), BF16), vm((count, 2 * PAIR), BF16), vm((count, 2 * PAIR), BF16),
            vm((2, rows, 2 * PAIR), BF16), vm((2, rows, 2 * PAIR), BF16), vm((PAIR, count), BF16),
            vm((PAIR, rows), F32), vm((rows, width), BF16), vm((count, width), BF16), vm((count, width), BF16),
        ],
        compiler_params=PARAMS,
        cost_estimate=cost(rows * count * 5 * 512 * H, 20 << 20, rows * count * H),
        name="self_bwd" if same else "cross_bwd",
    )(length, dy, r, gain, w, q, k, v, o, qx, xq, xk)


def gelu_parts(u):
    au = jnp.abs(u)
    t = 1.0 / (1.0 + (0.3275911 * math.sqrt(0.5)) * au)
    e = jnp.exp2(u * u * (-0.5 * LOG2E))
    c = [0.5 * x for x in (0.254829592, -0.284496736, 1.421413741, -1.453152027, 1.061405429)]
    tail = t * (c[0] + t * (c[1] + t * (c[2] + t * (c[3] + t * c[4])))) * e
    phi = jnp.where(u >= 0.0, 1.0 - tail, tail)
    return u * phi, phi + u * e * (1.0 / math.sqrt(2.0 * math.pi))


def ffn_fwd_kernel(r_ref, g_ref, up_ref, down_ref, h_ref, a_ref, d_ref, out_ref):
    hidden = norm(r_ref[...], g_ref[...])
    low = hidden.astype(BF16)
    h_ref[...] = low
    total = hidden
    span = up_ref.shape[1] // 4
    for c in range(4):
        cols = slice(c * span, (c + 1) * span)
        act, slope = gelu_parts(nn(low, up_ref[:, cols]))
        act = act.astype(BF16)
        a_ref[:, cols] = act
        d_ref[:, cols] = slope.astype(BF16)
        total = total + nn(act, down_ref[cols, :])
    out_ref[...] = total


def ffn_forward(r, gain, up, down):
    rows, width = r.shape
    inner = up.shape[1]
    blk = math.gcd(rows, 256)
    sds = jax.ShapeDtypeStruct
    by_rows = lambda n: pl.BlockSpec((blk, n), lambda i: (i, 0))
    return pl.pallas_call(
        ffn_fwd_kernel,
        grid=(rows // blk,),
        in_specs=[by_rows(width), whole((1, width)), whole(up.shape), whole(down.shape)],
        out_specs=[by_rows(width), by_rows(inner), by_rows(inner), by_rows(width)],
        out_shape=[sds((rows, width), BF16), sds((rows, inner), BF16), sds((rows, inner), BF16), sds((rows, width), F32)],
        compiler_params=PARAMS,
        cost_estimate=cost(4 * rows * width * inner * 2, 17 << 20, rows * inner * 2),
        name="ffn_fwd",
    )(r, gain, up, down)


def ffn_bwd_kernel(dy_ref, r_ref, g_ref, h_ref, a_ref, d_ref, up_ref, down_ref,
                   dup_ref, ddown_ref, dg_ref, dh_ref, low, ht):
    @pl.when(pl.program_id(0) == 0)
    def _():
        grad, dg = norm_back(r_ref[...], g_ref[...], dy_ref[...])
        dg_ref[...] = dg
        dh_ref[...] = grad
        low[...] = grad.astype(BF16)
        ht[...] = h_ref[...].T

    grad = low[...]
    ddown_ref[...] = tn(a_ref[...], grad).astype(BF16)
    du = (nt(grad, down_ref[...]) * d_ref[...].astype(F32)).astype(BF16)
    dup_ref[...] = nn(ht[...], du).astype(BF16)
    dh_ref[...] += nt(du, up_ref[...])


def ffn_backward(dy, r, gain, hidden, act, slope, up, down):
    rows, width = r.shape
    inner = up.shape[1]
    span = inner // 4
    sds = jax.ShapeDtypeStruct
    by_cols = lambda n: pl.BlockSpec((n, span), lambda i: (0, i))
    by_span = pl.BlockSpec((span, width), lambda i: (i, 0))
    return pl.pallas_call(
        ffn_bwd_kernel,
        grid=(inner // span,),
        in_specs=[whole((rows, width)), whole((rows, width)), whole((1, width)), whole((rows, width)),
                  by_cols(rows), by_cols(rows), by_cols(width), by_span],
        out_specs=[by_cols(width), by_span, whole((1, width)), whole((rows, width))],
        out_shape=[sds((width, inner), BF16), sds((inner, width), BF16), sds((1, width), F32), sds((rows, width), F32)],
        scratch_shapes=[pltpu.VMEM((rows, width), BF16), pltpu.VMEM((width, rows), BF16)],
        compiler_params=PARAMS,
        cost_estimate=cost(8 * rows * width * inner * 2, 25 << 20),
        name="ffn_bwd",
    )(dy, r, gain, hidden, act, slope, up, down)


def slot_kernel(len_ref, base_ref, r_ref, g_ref, w_ref, cot_ref, next_ref, prev_ref, out_ref, dw_ref, dy_ref):
    rows, width = r_ref.shape
    gain = g_ref[...]
    low = norm(r_ref[...], gain).astype(BF16)
    after = norm(next_ref[...], gain).astype(BF16)
    row = lax.broadcasted_iota(jnp.int32, (rows, width), 0)
    place = row + base_ref[0]
    live = place < len_ref[0] - 1
    second = nn(low, w_ref[width:, :])
    halo = nn(after, w_ref[width:, :])[:1, :]
    shifted = jnp.where(row == rows - 1, halo * base_ref[1].astype(F32), pltpu.roll(second, rows - 1, 0))
    out_ref[...] = jnp.where(live, nn(low, w_ref[:width, :]) + shifted, 0.0).astype(BF16)
    g = jnp.where(live, cot_ref[...].astype(F32), 0.0)
    g_before = prev_ref[...].astype(F32)[:1, :]
    g_before = jnp.where(base_ref[0] - 1 < len_ref[0] - 1, g_before, 0.0)
    before = jnp.where(row == 0, g_before, pltpu.roll(g, 1, 0)).astype(BF16)
    g = g.astype(BF16)
    low_t = low.T
    dw_ref[:width, :] = nn(low_t, g).astype(BF16)
    dw_ref[width:, :] = nn(low_t, before).astype(BF16)
    dy_ref[...] = nt(g, w_ref[:width, :]) + nt(before, w_ref[width:, :])


def slot_step(length, base, r, gain, w, cot, after, before):
    rows, width = r.shape
    sds = jax.ShapeDtypeStruct
    vm = lambda: pl.BlockSpec(memory_space=pltpu.VMEM)
    return pl.pallas_call(
        slot_kernel,
        in_specs=[smem(), smem()] + [vm() for _ in range(6)],
        out_specs=[vm() for _ in range(3)],
        out_shape=[sds((rows, width), BF16), sds(w.shape, BF16), sds((rows, width), F32)],
        compiler_params=PARAMS,
        cost_estimate=cost(12 * rows * width * width, 9 << 20),
        name="slot",
    )(length, base, r, gain, w, cot, after, before)


def to_examples(x, count):
    examples, rows, width = x.shape
    me = lax.axis_index("seq")
    if count == examples:
        buf = jnp.zeros((count, rows, width), x.dtype)
        for k in range(count):
            piece = lax.dynamic_index_in_dim(x, (me + k) % count, 0, keepdims=False)
            if k:
                piece = lax.ppermute(piece, "seq", [(s, (s + k) % count) for s in range(count)])
            buf = lax.dynamic_update_index_in_dim(buf, piece, (me - k) % count, 0)
        return buf.reshape(count * rows, width)
    group = count // examples
    all_rows = lax.all_gather(x, "seq", axis=1, tiled=True)
    one = lax.dynamic_index_in_dim(all_rows, me // group, 0, keepdims=False)
    return lax.dynamic_slice_in_dim(one, (me % group) * examples * rows, examples * rows, 0)


def to_positions(x, examples, count):
    me = lax.axis_index("seq")
    width = x.shape[1]
    if count == examples:
        x = x.reshape(count, -1, width)
        buf = jnp.zeros_like(x)
        for k in range(count):
            piece = lax.dynamic_index_in_dim(x, (me + k) % count, 0, keepdims=False)
            if k:
                piece = lax.ppermute(piece, "seq", [(s, (s + k) % count) for s in range(count)])
            buf = lax.dynamic_update_index_in_dim(buf, piece, (me - k) % count, 0)
        return buf
    rows = x.shape[0] // examples
    all_rows = lax.all_gather(x, "seq", axis=0, tiled=True).reshape(examples, count * rows, width)
    return lax.dynamic_slice_in_dim(all_rows, me * rows, rows, 1)


def gather_weights(parts):
    return [lax.all_gather(x, ("dp", "seq"), axis=dim, tiled=True) for x, dim in parts]


def per_device(source, canvas, source_len, canvas_len, cotangent, enc_attn, enc_up, enc_down, dec_attn, cross_attn,
               dec_up, dec_down, slot_proj, norm_gains):
    examples, _, width = source.shape
    seq = lax.axis_size("seq")
    group = seq // examples
    me = lax.axis_index("seq")
    groups = [[e * group + t for t in range(group)] for e in range(examples)]

    def whole_keys(x):
        return lax.all_gather(x, "seq", axis=0, tiled=True, axis_index_groups=groups) if group > 1 else x

    def own_keys(x):
        if group == 1:
            return x
        return lax.psum_scatter(x, "seq", scatter_dimension=0, tiled=True, axis_index_groups=groups)

    def neighbour(x, step):
        if group == 1:
            return jnp.zeros_like(x)
        pairs = [(s, s + step) for s in range(seq) if 0 <= s % group + step < group]
        return lax.ppermute(x, "seq", pairs)

    flat = [enc_attn, enc_up, enc_down, dec_attn, cross_attn, dec_up, dec_down, slot_proj]
    sizes = [x.size for x in flat] + [norm_gains.size]
    packed = jnp.concatenate([x.reshape(-1) for x in flat] + [norm_gains.reshape(-1)])
    packed = jnp.pad(packed, (0, -packed.size % width)).reshape(1, -1, width)
    gathered = lax.all_gather(packed, ("dp", "seq"), axis=0, tiled=True).reshape(lax.axis_size("dp") * seq, -1)
    shards = []
    at = 0
    for size in sizes:
        shards.append(gathered[:, at:at + size])
        at += size
    devices = gathered.shape[0]

    def stack_of(x, like):
        return x.reshape(devices, 4, -1, width).transpose(1, 0, 2, 3).reshape(4, -1, width)

    w_enc = stack_of(shards[0], enc_attn)
    w_eup = shards[1].reshape(width, -1)
    w_edown = shards[2].reshape(-1, width)
    w_dec = stack_of(shards[3], dec_attn)
    w_cross = stack_of(shards[4], cross_attn)
    w_dup = shards[5].reshape(width, -1)
    w_ddown = shards[6].reshape(-1, width)
    w_slot = shards[7].reshape(-1, width)
    gains = shards[8].reshape(devices, 5, -1).transpose(1, 0, 2).reshape(5, width).astype(F32)
    gain = [gains[i:i + 1] for i in range(5)]

    example = me // group
    s_len = lax.dynamic_slice_in_dim(source_len, example, 1)
    c_len = lax.dynamic_slice_in_dim(canvas_len, example, 1)
    src = to_examples(source, seq)
    can = to_examples(canvas, seq)
    cot = to_examples(cotangent, seq)
    rows = src.shape[0]
    base = (me % group) * rows
    has_next = (me % group) < group - 1
    place = jnp.stack([base, has_next.astype(jnp.int32)]).astype(jnp.int32)

    src_all = whole_keys(src)
    can_all = whole_keys(can)
    q_a, k_a, v_a, o_a, x_a, r_a = attn_forward(s_len, w_enc, xq=src, xk=src_all)
    h_a, act_a, slope_a, r_b = ffn_forward(r_a, gain[0], w_eup, w_edown)
    q_b, k_b, v_b, o_b, x_b, r_c = attn_forward(c_len, w_dec, xq=can, xk=can_all)
    low_one, low_enc, q_c, k_c, v_c, o_c, x_c, r_d = attn_forward(
        s_len, w_cross, rq=r_c, rk=whole_keys(r_b), gq=gain[2], gk=gain[1])
    h_b, act_b, slope_b, r_e = ffn_forward(r_d, gain[3], w_dup, w_ddown)
    slot_out, d_slot, dy = slot_step(
        c_len, place, r_e, gain[4], w_slot, cot, neighbour(r_e[:8], -1), neighbour(cot[-8:][::-1], 1))
    d_dup, d_ddown, dg4, dy = ffn_backward(dy, r_e, gain[4], h_b, act_b, slope_b, w_dup, w_ddown)
    d_cross, dg3, dy, d_enc = attn_backward(
        False, s_len, dy, r_d, gain[3], w_cross, q_c, k_c, v_c, o_c, x_c, low_one, low_enc)
    alone = group == 1
    d_dec, dg2, *d_can = attn_backward(alone, c_len, dy, r_c, gain[2], w_dec, q_b, k_b, v_b, o_b, x_b, can, can_all)
    d_eup, d_edown, dg1, dy = ffn_backward(own_keys(d_enc), r_b, gain[1], h_a, act_a, slope_a, w_eup, w_edown)
    d_encw, dg0, *d_src = attn_backward(alone, s_len, dy, r_a, gain[0], w_enc, q_a, k_a, v_a, o_a, x_a, src, src_all)
    canvas_grad = d_can[0] if alone else d_can[0] + own_keys(d_can[1])
    source_grad = d_src[0] if alone else d_src[0] + own_keys(d_src[1])

    d_gains = jnp.concatenate([dg0, dg1, dg2, dg3, dg4], axis=0).astype(BF16)
    rowwise = lambda x: x.reshape(devices, -1)
    stacked = lambda x: x.reshape(4, devices, -1).transpose(1, 0, 2).reshape(devices, -1)
    grads = jnp.concatenate(
        [stacked(d_encw), rowwise(d_eup), rowwise(d_edown), stacked(d_dec), stacked(d_cross), rowwise(d_dup),
         rowwise(d_ddown), rowwise(d_slot), d_gains.reshape(5, devices, -1).transpose(1, 0, 2).reshape(devices, -1)],
        axis=1)
    total = grads.shape[1]
    grads = jnp.pad(grads, ((0, 0), (0, -total % width))).reshape(devices, -1, width)
    mine = lax.psum_scatter(grads, ("dp", "seq"), scatter_dimension=0, tiled=True).reshape(-1).astype(F32)
    results = []
    at = 0
    for like in flat + [norm_gains]:
        results.append(mine[at:at + like.size].reshape(like.shape))
        at += like.size

    return (
        to_positions(slot_out, examples, seq),
        to_positions(source_grad, examples, seq),
        to_positions(canvas_grad, examples, seq),
        *results,
    )


def solution(mesh):
    by_seq = P("dp", "seq", None)
    stack = P(None, ("dp", "seq"), None)
    by_row = P(("dp", "seq"), None)
    gains = P(None, ("dp", "seq"))
    in_specs = (by_seq, by_seq, P("dp"), P("dp"), by_seq, stack, by_row, by_row, stack, stack, by_row, by_row, by_row,
                gains)
    out_specs = (by_seq, by_seq, by_seq, stack, by_row, by_row, stack, stack, by_row, by_row, by_row, gains)
    return jax.shard_map(per_device, mesh=mesh, in_specs=in_specs, out_specs=out_specs, check_vma=False)
```

```python
import functools
import math

import jax
import jax.numpy as jnp
from jax import lax
from jax.experimental import pallas as pl
from jax.experimental.pallas import tpu as pltpu
from jax.sharding import PartitionSpec as P

F32 = jnp.float32
BF16 = jnp.bfloat16
H = 8
HD = 64
PAIR = 2 * HD
LOG2E = math.log2(math.e)
Q_SCALE = LOG2E / 8.0
K_BACK = 1.0 / LOG2E
MASKED = -1e30
VMEM_LIMIT = 58 * 1024 * 1024
PARAMS = pltpu.CompilerParams(vmem_limit_bytes=VMEM_LIMIT)


def nn(a, b):
    return lax.dot_general(a, b, (((1,), (0,)), ((), ())), preferred_element_type=F32)


def nt(a, b):
    return lax.dot_general(a, b, (((1,), (1,)), ((), ())), preferred_element_type=F32)


def tn(a, b):
    return lax.dot_general(a, b, (((0,), (0,)), ((), ())), preferred_element_type=F32)


def norm_parts(r):
    centre = r - jnp.mean(r, axis=-1, keepdims=True)
    rs = lax.rsqrt(jnp.mean(centre * centre, axis=-1, keepdims=True) + 1e-5)
    return centre * rs, rs


def norm(r, gain):
    return norm_parts(r)[0] * gain


def norm_back(r, gain, dy):
    z, rs = norm_parts(r)
    t = dy * gain
    dr = (t - jnp.mean(t, axis=-1, keepdims=True) - z * jnp.mean(t * z, axis=-1, keepdims=True)) * rs
    return dr, jnp.sum(dy * z, axis=0, keepdims=True)


def lanes(rows):
    return lax.broadcasted_iota(jnp.int32, (rows, PAIR), 1)


def key_extras(length, count):
    row = lax.broadcasted_iota(jnp.int32, (count, PAIR), 0)
    lane = lanes(count)
    bias = jnp.where(row < length, 0.0, MASKED)
    return jnp.where(lane == 3, bias, jnp.where(lane < 3, 1.0, 0.0)).astype(BF16)


def three_parts(v):
    hi = v.astype(BF16)
    rest = v - hi.astype(F32)
    mid = rest.astype(BF16)
    low = rest - mid.astype(F32)
    return hi.astype(F32), mid.astype(F32), low


def spread_parts(v, last):
    lane = lanes(v.shape[0])
    hi, mid, low = three_parts(v)
    tail = jnp.where(lane == 3, last, 0.0)
    return jnp.where(lane == 0, hi, jnp.where(lane == 1, mid, jnp.where(lane == 2, low, tail))).astype(BF16)


def whole(shape):
    return pl.BlockSpec(shape, lambda i: (0,) * len(shape))


def smem():
    return pl.BlockSpec(memory_space=pltpu.SMEM)


def vmem():
    return pl.BlockSpec(memory_space=pltpu.VMEM)


def cost(flops, nbytes, exps=0):
    return pl.CostEstimate(flops=int(flops), bytes_accessed=int(nbytes), transcendentals=int(exps))


INNER = 4
SEQ = 2


class Spot:
    def __init__(self, ref, outer, far):
        self.outer, self.far = outer, far
        self.o, self.i, self.s = ref[0], ref[1], ref[2]

    def owner(self, c, j, k):
        o = k if self.far else lax.rem(self.o - k + self.outer, self.outer)
        i = lax.rem(self.i - j + INNER, INNER)
        return (o * INNER + i) * SEQ + lax.rem(self.s - c + SEQ, SEQ)

    def ahead(self, o, i):
        return lax.rem(i - self.i + INNER, INNER), o if self.far else lax.rem(o - self.o + self.outer, self.outer)


def assemble(spot, refs, at, dst, block):
    stack, total, _ = dst.shape
    share = total // (spot.outer * INNER * SEQ)
    for c in range(SEQ):
        for j in range(INNER):
            for k in range(spot.outer):
                ref, x = (refs[c], k * INNER + j) if block else (refs[c * INNER + j], k)
                rows = pl.ds(pl.multiple_of(spot.owner(c, j, k) * share, share), share)
                for a in range(stack):
                    dst[a, rows, :] = ref[x, at + a * share:at + (a + 1) * share, :]


def deal(spot, src, at, keep, send):
    stack, total, _ = src.shape
    share = total // (spot.outer * INNER * SEQ)
    for core in range(SEQ):
        @pl.when(spot.s == core)
        def _():
            for o in range(spot.outer):
                for i in range(INNER):
                    j, k = spot.ahead(o, i)
                    for s in range(SEQ):
                        first = ((o * INNER + i) * SEQ + s) * share
                        dst = keep if s == core else send
                        for a in range(stack):
                            dst[j, k, at + a * share:at + (a + 1) * share, :] = src[a, first:first + share, :]


class Weights:
    def __init__(self, packed, arrays, shapes, at=0, spot=None, outer=0, far=(False, False), block=False, tail=0):
        self.packed, self.arrays, self.shapes, self.at, self.spot, self.outer = packed, arrays, shapes, at, spot, outer
        self.far, self.block, self.tail = far, block, tail

    def share(self, shape):
        return shape[0] * shape[1] // (self.outer * INNER * SEQ)

    def args(self):
        return [self.spot, *self.arrays] if self.packed else list(self.arrays)

    def specs(self, dims):
        zero = lambda n: (lambda *_: (0,) * n)
        if not self.packed:
            return [pl.BlockSpec(x.shape, zero(3), pipeline_mode=pl.Buffered(1)) if dims else vmem() for x in self.arrays]
        rows = sum(self.share(s) for s in self.shapes) + self.tail
        index = self.at // rows
        spec = lambda: pl.BlockSpec((self.arrays[0].shape[0], rows, self.shapes[0][2]), lambda *_: (0, index, 0),
                                    **(dict(pipeline_mode=pl.Buffered(1)) if dims else {}))
        return [smem()] + [spec() for _ in self.arrays]

    def scratch(self):
        return [pltpu.VMEM(s, BF16) for s in self.shapes] if self.packed else []

    def n_args(self):
        return len(self.arrays) + 1 if self.packed else len(self.arrays)

    def n_scratch(self):
        return len(self.shapes) if self.packed else 0

    def load(self, refs, scratch, first):
        if not self.packed:
            return list(refs)

        @pl.when(first)
        def _():
            spot = Spot(refs[0], self.outer, self.far[0])
            at = 0
            for shape, dst in zip(self.shapes, scratch):
                assemble(spot, refs[1:], at, dst, self.block)
                at += self.share(shape)
        return list(scratch)

    def grad_shapes(self, extra=0):
        if not self.packed:
            return [jax.ShapeDtypeStruct(s, BF16) for s in self.shapes]
        rows = sum(self.share(s) for s in self.shapes) + extra
        return [jax.ShapeDtypeStruct((INNER, self.outer, rows, self.shapes[0][2]), BF16)] * SEQ

    def grad_scratch(self):
        return [pltpu.VMEM(s, BF16) for s in self.shapes] if self.packed else []

    def store(self, refs, grads, outs, last):
        if not self.packed:
            return

        @pl.when(last)
        def _():
            spot = Spot(refs[0], self.outer, self.far[1])
            at = 0
            for shape, src in zip(self.shapes, grads):
                deal(spot, src, at, *outs)
                at += self.share(shape)


def cut(refs, *counts):
    out, at = [], 0
    for n in counts:
        out.append(refs[at:at + n])
        at += n
    assert at == len(refs)
    return out


def attn_fwd_kernel(cross, w, *refs):
    n_in, n_out = (5, 8) if cross else (3, 6)
    n_tail = 1 if w.tail else 0
    ins, w_refs, outs, tail, (kaug, vaug), w_scr = cut(refs, n_in, w.n_args(), n_out, n_tail, 2, w.n_scratch())
    count = kaug.shape[1]
    start = pl.program_id(0) == 0
    w_ref, = w.load(w_refs, w_scr, start)
    if cross:
        len_ref, rq_ref, rk_ref, gq_ref, gk_ref = ins
        xq_ref, xk_ref, q_ref, k_ref, v_ref, o_ref, qx_ref, r_ref = outs
    else:
        len_ref, xq_ref, xk_ref = ins
        q_ref, k_ref, v_ref, o_ref, qx_ref, r_ref = outs
    rows = r_ref.shape[0]

    @pl.when(start)
    def _():
        if w.tail:
            parts = [x[k, w.share(w.shapes[0]):, :].astype(F32) for x in w_refs[1:] for k in range(w.outer)]
            tail[0][...] = sum(parts[1:], parts[0])
        if cross:
            xk_ref[...] = norm(rk_ref[...], gk_ref[...]).astype(BF16)
        xk = xk_ref[...]
        k = nn(xk, w_ref[1]).astype(BF16)
        v = nn(xk, w_ref[2]).astype(BF16)
        k_ref[...] = k
        v_ref[...] = v
        extras = key_extras(len_ref[0], count)
        ones = jnp.ones((count, PAIR), BF16)
        for p in range(H // 2):
            kaug[p, :, :PAIR] = k[:, p * PAIR:(p + 1) * PAIR]
            kaug[p, :, PAIR:] = extras
            vaug[p, :, :PAIR] = v[:, p * PAIR:(p + 1) * PAIR]
            vaug[p, :, PAIR:] = ones

    if cross:
        resid = norm(rq_ref[...], gq_ref[...])
        xq = resid.astype(BF16)
        xq_ref[...] = xq
    else:
        xq = xq_ref[...]
        resid = xq.astype(F32)
    q = nn(xq, w_ref[0]) * Q_SCALE
    q_ref[...] = q.astype(BF16)
    lane = lanes(rows)
    first = lane < HD
    extra = jnp.where(lane == 3, 1.0, 0.0).astype(BF16)
    blended = []
    for p in range(H // 2):
        qp = q[:, p * PAIR:(p + 1) * PAIR]
        halves = []
        for h in range(2):
            qm = jnp.where(first if h == 0 else lane >= HD, qp, 0.0).astype(BF16)
            s = nt(jnp.concatenate([qm, extra], axis=1), kaug[p])
            m = jnp.max(s, axis=1, keepdims=True)
            e = jnp.exp2(s - m).astype(BF16)
            o = nn(e, vaug[p])
            total = o[:, PAIR:]
            halves.append(o[:, :PAIR] / total)
            qx_ref[2 * p + h] = spread_parts(-(m + jnp.log2(total)), 1.0)
        blended.append(jnp.where(first, halves[0], halves[1]).astype(BF16))
    o_all = jnp.concatenate(blended, axis=1)
    o_ref[...] = o_all
    r_ref[...] = resid + nn(o_all, w_ref[3])


def attn_forward(length, w, xq=None, xk=None, rq=None, rk=None, gq=None, gk=None):
    cross = rq is not None
    rows, width = (rq if cross else xq).shape
    count = (rk if cross else xk).shape[0]
    blk = math.gcd(rows, 256)
    sds = jax.ShapeDtypeStruct
    by_rows = pl.BlockSpec((blk, width), lambda i: (i, 0))
    outs = [
        sds((rows, width), BF16), sds((count, width), BF16), sds((count, width), BF16),
        sds((rows, width), BF16), sds((H, rows, PAIR), BF16), sds((rows, width), F32),
    ]
    out_specs = [
        by_rows, whole((count, width)), whole((count, width)),
        by_rows, pl.BlockSpec((H, blk, PAIR), lambda i: (0, i, 0)), by_rows,
    ]
    if cross:
        args = [length, rq, rk, gq, gk]
        in_specs = [smem(), by_rows, whole((count, width)), whole((1, width)), whole((1, width))]
        outs = [sds((rows, width), BF16), sds((count, width), BF16)] + outs
        out_specs = [by_rows, whole((count, width))] + out_specs
    else:
        args = [length, xq, xk]
        in_specs = [smem(), by_rows, whole((count, width))]
    if w.tail:
        outs.append(sds((w.tail, width), F32))
        out_specs.append(whole((w.tail, width)))
    return pl.pallas_call(
        functools.partial(attn_fwd_kernel, cross, w),
        grid=(rows // blk,),
        in_specs=in_specs + w.specs(1),
        out_specs=out_specs,
        out_shape=outs,
        scratch_shapes=[pltpu.VMEM((H // 2, count, 2 * PAIR), BF16)] * 2 + w.scratch(),
        compiler_params=PARAMS,
        cost_estimate=cost(rows * count * 5 * 512 * H, 14 << 20, rows * count * H),
        name="cross_fwd" if cross else "self_fwd",
    )(*args, *w.args())


def attn_bwd_kernel(norms, same, w, *refs):
    n_out = 1 if same else 2
    n_dg = 0 if same else norms
    n_grad = 2 if w.packed else 1
    (len_ref, dr_ref, q_ref, k_ref, v_ref, o_ref, qx_ref, xq_ref, xk_ref), n_refs, w_refs, outs, dg_refs, dw_outs, \
        (dab, kaug, vaug, qaug, oaug, kt, dqt, dq, dk, dv), w_scr, dw_scr = cut(
            refs, 9, 2 * norms, w.n_args(), n_out, n_dg, n_grad, 10, w.n_scratch(), w.n_scratch())
    dw_ref, = dw_scr if w.packed else dw_outs
    count = kaug.shape[0]
    rows = dab.shape[0]
    blk = math.gcd(count, 256)
    p = pl.program_id(0)
    w_ref, = w.load(w_refs, w_scr, p == 0)

    @pl.when(p == 0)
    def _():
        dab[...] = dr_ref[...].astype(BF16)
        kaug[:, PAIR:] = key_extras(len_ref[0], count)
        vaug[:, PAIR:] = jnp.where(lanes(count) < 3, 1.0, 0.0).astype(BF16)

    cols = pl.ds(pl.multiple_of(p * PAIR, PAIR), PAIR)
    out_rows = w_ref[3, cols, :]
    do = nt(dab[...], out_rows).astype(BF16).astype(F32)
    o = o_ref[...]
    dw_ref[3, cols, :] = tn(o, dab[...]).astype(BF16)
    inner = do * o.astype(F32)
    kaug[:, :PAIR] = k_ref[...]
    vaug[:, :PAIR] = v_ref[...]
    kt[...] = k_ref[...].T
    lane = lanes(rows)
    q = q_ref[...].astype(F32)
    for h in range(2):
        mine = lane < HD if h == 0 else lane >= HD
        qaug[h, :, :PAIR] = jnp.where(mine, q, 0.0).astype(BF16)
        qaug[h, :, PAIR:] = qx_ref[h]
        oaug[h, :, :PAIR] = jnp.where(mine, do, 0.0).astype(BF16)
        d = jnp.sum(jnp.where(mine, inner, 0.0), axis=1, keepdims=True)
        oaug[h, :, PAIR:] = spread_parts(jnp.broadcast_to(-d, (rows, PAIR)), 0.0)
    for j in range(count // blk):
        keys = slice(j * blk, (j + 1) * blk)
        dv_sum = dk_sum = None
        for h in range(2):
            st = nt(kaug[keys, :], qaug[h])
            pt = jnp.exp2(st)
            dpt = nt(vaug[keys, :], oaug[h])
            ptb = pt.astype(BF16)
            dst = (pt * dpt).astype(BF16)
            dv_h = nn(ptb, oaug[h, :, :PAIR])
            dk_h = nn(dst, qaug[h, :, :PAIR])
            dq_h = nn(kt[h * HD:(h + 1) * HD, keys], dst)
            dv_sum = dv_h if h == 0 else dv_sum + dv_h
            dk_sum = dk_h if h == 0 else dk_sum + dk_h
            if j == 0:
                dqt[h * HD:(h + 1) * HD, :] = dq_h
            else:
                dqt[h * HD:(h + 1) * HD, :] += dq_h
        dv[keys, cols] = dv_sum.astype(BF16)
        dk[keys, cols] = (dk_sum * K_BACK).astype(BF16)
    dq[:, cols] = (dqt[...].T * 0.125).astype(BF16)
    last = p == pl.num_programs(0) - 1

    @pl.when(last)
    def _():
        xqt = xq_ref[...].T
        xkt = xk_ref[...].T
        dw_ref[0] = nn(xqt, dq[...]).astype(BF16)
        dw_ref[1] = nn(xkt, dk[...]).astype(BF16)
        dw_ref[2] = nn(xkt, dv[...]).astype(BF16)
        dxq = dr_ref[...] + nt(dq[...], w_ref[0])
        dxk = nt(dk[...], w_ref[1]) + nt(dv[...], w_ref[2])
        if same:
            outs[0][...] = dxq + dxk
        else:
            for n, value in enumerate((dxq, dxk)):
                if n < norms:
                    value, dg_refs[n][...] = norm_back(n_refs[2 * n][...], n_refs[2 * n + 1][...], value)
                outs[n][...] = value

    w.store(w_refs, [dw_ref], dw_outs, last)


def attn_backward(same, length, dr, w, q, k, v, o, qx, xq, xk, norms=()):
    rows, width = dr.shape
    count = k.shape[0]
    sds = jax.ShapeDtypeStruct
    pair_of = lambda n: pl.BlockSpec((n, PAIR), lambda i: (0, i))
    once = lambda shape: pl.BlockSpec(shape, lambda i: (0,) * len(shape), pipeline_mode=pl.Buffered(1))
    in_specs = [
        smem(), once((rows, width)), pair_of(rows), pair_of(count), pair_of(count), pair_of(rows),
        pl.BlockSpec((2, rows, PAIR), lambda i: (i, 0, 0)), once((rows, width)), once((count, width)),
    ]
    norm_args = []
    for r, g in norms:
        norm_args += [r, g]
        in_specs += [once(r.shape), once(g.shape)]
    outs = [sds((rows, width), F32)]
    if not same:
        outs += [sds((count, width), F32)] + [sds((1, width), F32)] * len(norms)
    outs += w.grad_shapes()
    vm = pltpu.VMEM
    return pl.pallas_call(
        functools.partial(attn_bwd_kernel, len(norms), same, w),
        grid=(H // 2,),
        in_specs=in_specs + w.specs(1),
        out_specs=[whole(s.shape) for s in outs],
        out_shape=outs,
        scratch_shapes=[
            vm((rows, width), BF16), vm((count, 2 * PAIR), BF16), vm((count, 2 * PAIR), BF16),
            vm((2, rows, 2 * PAIR), BF16), vm((2, rows, 2 * PAIR), BF16), vm((PAIR, count), BF16),
            vm((PAIR, rows), F32), vm((rows, width), BF16), vm((count, width), BF16), vm((count, width), BF16),
        ] + w.scratch() + w.grad_scratch(),
        compiler_params=PARAMS,
        cost_estimate=cost(rows * count * 10 * 512 * H, 20 << 20, rows * count * H),
        name="self_bwd" if same else "cross_bwd",
    )(length, dr, q, k, v, o, qx, xq, xk, *norm_args, *w.args())


def gelu_parts(u):
    au = jnp.abs(u)
    t = 1.0 / (1.0 + (0.3275911 * math.sqrt(0.5)) * au)
    e = jnp.exp2(u * u * (-0.5 * LOG2E))
    c = [0.5 * x for x in (0.254829592, -0.284496736, 1.421413741, -1.453152027, 1.061405429)]
    tail = t * (c[0] + t * (c[1] + t * (c[2] + t * (c[3] + t * c[4])))) * e
    phi = jnp.where(u >= 0.0, 1.0 - tail, tail)
    return u * phi, phi + u * e * (1.0 / math.sqrt(2.0 * math.pi))


def ffn_fwd_kernel(w, *refs):
    (r_ref, g_ref), w_refs, (h_ref, a_ref, d_ref, out_ref), w_scr = cut(refs, 2, w.n_args(), 4, w.n_scratch())
    up_ref, down_ref = w.load(w_refs, w_scr, pl.program_id(0) == 0)
    hidden = norm(r_ref[...], g_ref[...])
    low = hidden.astype(BF16)
    h_ref[...] = low
    total = hidden
    span = up_ref.shape[2]
    for c in range(up_ref.shape[0]):
        cols = slice(c * span, (c + 1) * span)
        act, slope = gelu_parts(nn(low, up_ref[c]))
        act = act.astype(BF16)
        a_ref[:, cols] = act
        d_ref[:, cols] = slope.astype(BF16)
        total = total + nn(act, down_ref[0, cols, :])
    out_ref[...] = total


def ffn_forward(r, gain, w):
    rows, width = r.shape
    inner = w.shapes[1][1]
    blk = math.gcd(rows, 256)
    sds = jax.ShapeDtypeStruct
    by_rows = lambda n: pl.BlockSpec((blk, n), lambda i: (i, 0))
    return pl.pallas_call(
        functools.partial(ffn_fwd_kernel, w),
        grid=(rows // blk,),
        in_specs=[by_rows(width), whole((1, width))] + w.specs(1),
        out_specs=[by_rows(width), by_rows(inner), by_rows(inner), by_rows(width)],
        out_shape=[sds((rows, width), BF16), sds((rows, inner), BF16), sds((rows, inner), BF16), sds((rows, width), F32)],
        scratch_shapes=w.scratch(),
        compiler_params=PARAMS,
        cost_estimate=cost(16 * rows * width * inner, 17 << 20, rows * inner * 2),
        name="ffn_fwd",
    )(r, gain, *w.args())


def ffn_bwd_kernel(w, kind, *refs):
    n_more = {"none": 0, "slot": 2, "gains": 4}[kind]
    n_grad = 2
    (dr_ref, h_ref, a_ref, d_ref, r_ref, g_ref), more, w_refs, (dout_ref, dg_ref), dw_outs, (low, ht, acc), w_scr, dw_scr = cut(
        refs, 6, n_more, w.n_args(), 2, n_grad, 3, w.n_scratch(), w.n_scratch())
    n = pl.program_id(0)
    up_ref, down_ref = w.load(w_refs, w_scr, n == 0)
    dup_ref, ddown_ref = dw_scr if w.packed else dw_outs

    @pl.when(n == 0)
    def _():
        grad = dr_ref[...]
        acc[...] = grad
        low[...] = grad.astype(BF16)
        ht[...] = h_ref[...].T

    grad = low[...]
    span = up_ref.shape[2]
    rows = pl.ds(pl.multiple_of(n * span, span), span)
    ddown_ref[0, rows, :] = tn(a_ref[...], grad).astype(BF16)
    du = (nt(grad, down_ref[0, rows, :]) * d_ref[...].astype(F32)).astype(BF16)
    dup_ref[n] = nn(ht[...], du).astype(BF16)
    acc[...] += nt(du, up_ref[n])
    last = n == pl.num_programs(0) - 1

    @pl.when(last)
    def _():
        dout_ref[...], dg_ref[...] = norm_back(r_ref[...], g_ref[...], acc[...])

    w.store(w_refs, [dup_ref, ddown_ref], dw_outs, last)
    if not w.packed or kind == "none":
        return
    at = sum(w.share(s) for s in w.shapes)

    @pl.when(last)
    def _():
        if kind == "slot":
            for src, dst in zip(more, dw_outs):
                dst[:, :, at:, :] = src[...]
        else:
            gains = [dg_ref] + list(more)
            row = lax.broadcasted_iota(jnp.int32, (16, dg_ref.shape[1]), 0)
            block = jnp.zeros((16, dg_ref.shape[1]), F32)
            for x, ref in enumerate(gains):
                block = jnp.where(row == x, ref[...], block)
            block = block.astype(BF16)
            for dst in dw_outs:
                for j in range(INNER):
                    for k in range(w.outer):
                        dst[j, k, at:, :] = block


def ffn_backward(dr, hidden, act, slope, w, r, gain, kind="none", more=()):
    rows, width = dr.shape
    inner = w.shapes[1][1]
    span = inner // w.shapes[0][0]
    sds = jax.ShapeDtypeStruct
    once = lambda shape: pl.BlockSpec(shape, lambda i: (0,) * len(shape), pipeline_mode=pl.Buffered(1))
    by_cols = pl.BlockSpec((rows, span), lambda i: (0, i))
    extra = {"none": 0, "slot": more[0].shape[2] if kind == "slot" else 0, "gains": 16}[kind] if w.packed else 0
    if not w.packed:
        kind, more = "none", ()
    grads = w.grad_shapes(extra)
    return pl.pallas_call(
        functools.partial(ffn_bwd_kernel, w, kind),
        grid=(inner // span,),
        in_specs=[once((rows, width)), once((rows, width)), by_cols, by_cols, once((rows, width)), once((1, width))]
        + [once(x.shape) for x in more] + w.specs(1),
        out_specs=[whole((rows, width)), whole((1, width))] + [whole(s.shape) for s in grads],
        out_shape=[sds((rows, width), F32), sds((1, width), F32)] + grads,
        scratch_shapes=[pltpu.VMEM((rows, width), BF16), pltpu.VMEM((width, rows), BF16), pltpu.VMEM((rows, width), F32)]
        + w.scratch() + w.grad_scratch(),
        compiler_params=PARAMS,
        cost_estimate=cost(20 * rows * width * inner, 25 << 20),
        name="ffn_bwd",
    )(dr, hidden, act, slope, r, gain, *more, *w.args())


def slot_kernel(w, halo, *refs):
    n_grad = 2 if w.packed else 1
    (len_ref, r_ref, g_ref, cot_ref), halo_refs, w_refs, (out_ref, dr_ref, dg_ref), dw_outs, w_scr, dw_scr = cut(
        refs, 4, 3 if halo else 0, w.n_args(), 3, n_grad, w.n_scratch(), w.n_scratch())
    w_ref, = w.load(w_refs, w_scr, len_ref[0] >= 0)
    dw_ref, = dw_scr if w.packed else dw_outs
    rows, width = r_ref.shape
    gain = g_ref[...]
    low = norm(r_ref[...], gain).astype(BF16)
    row = lax.broadcasted_iota(jnp.int32, (rows, width), 0)
    above = below = 0.0
    place = row
    if halo:
        base_ref, next_ref, prev_ref = halo_refs
        place = row + base_ref[0]
        after = norm(next_ref[...], gain).astype(BF16)
        above = nn(after, w_ref[0, width:, :])[:1, :] * base_ref[1].astype(F32)
        below = jnp.where(base_ref[0] - 1 < len_ref[0] - 1, prev_ref[...].astype(F32)[:1, :], 0.0)
    live = place < len_ref[0] - 1
    second = nn(low, w_ref[0, width:, :])
    shifted = jnp.where(row == rows - 1, above, pltpu.roll(second, rows - 1, 0))
    out_ref[...] = jnp.where(live, nn(low, w_ref[0, :width, :]) + shifted, 0.0).astype(BF16)
    g = jnp.where(live, cot_ref[...].astype(F32), 0.0)
    before = jnp.where(row == 0, below, pltpu.roll(g, 1, 0)).astype(BF16)
    g = g.astype(BF16)
    low_t = low.T
    dw_ref[0, :width, :] = nn(low_t, g).astype(BF16)
    dw_ref[0, width:, :] = nn(low_t, before).astype(BF16)
    dy = nt(g, w_ref[0, :width, :]) + nt(before, w_ref[0, width:, :])
    dr_ref[...], dg_ref[...] = norm_back(r_ref[...], gain, dy)
    w.store(w_refs, [dw_ref], dw_outs, len_ref[0] >= 0)


def slot_step(length, r, gain, w, cot, halo):
    rows, width = r.shape
    sds = jax.ShapeDtypeStruct
    grads = w.grad_shapes()
    full = lambda x: pl.BlockSpec(x.shape, lambda i: (0,) * len(x.shape))
    outs = [sds((rows, width), BF16), sds((rows, width), F32), sds((1, width), F32)] + grads
    return pl.pallas_call(
        functools.partial(slot_kernel, w, len(halo) > 0),
        grid=(1,),
        in_specs=[smem()] + [full(x) for x in (r, gain, cot)] + [smem(), *map(full, halo[1:])][:len(halo)] + w.specs(1),
        out_specs=[full(x) for x in outs],
        out_shape=outs,
        scratch_shapes=w.scratch() + w.grad_scratch(),
        compiler_params=PARAMS,
        cost_estimate=cost(36 * rows * width * width, 9 << 20),
        name="slot",
    )(length, r, gain, cot, *halo, *w.args())


def pack_kernel(lane_ref, gains_ref, *refs):
    *ins, first_ref, second_ref = refs
    pieces = []
    for ref in ins:
        if len(ref.shape) == 3:
            pieces += [ref[a] for a in range(ref.shape[0])]
        elif ref.shape[1] > first_ref.shape[1]:
            width = first_ref.shape[1]
            pieces += [ref[:, a * width:(a + 1) * width] for a in range(ref.shape[1] // width)]
        else:
            pieces.append(ref[...])
        if ref is ins[0]:
            count, share = gains_ref.shape
            row = lax.broadcasted_iota(jnp.int32, (share, first_ref.shape[1]), 0)
            lane = lax.broadcasted_iota(jnp.int32, (share, first_ref.shape[1]), 1)
            spread = jnp.where(lane == row + lane_ref[0], 1.0, 0.0).astype(BF16)
            gains = nn(gains_ref[...], spread).astype(BF16)
            pieces.append(jnp.concatenate([gains, jnp.zeros((16 - count, gains.shape[1]), BF16)], axis=0))
    at = 0
    dst = first_ref
    for piece in pieces:
        if at == dst.shape[0]:
            at, dst = 0, second_ref
        dst[at:at + piece.shape[0], :] = piece
        at += piece.shape[0]


def pack(lane, gains, first, second):
    width = first[0].shape[-1]
    rows = [sum(x.size for x in xs) // width for xs in (first, second)]
    return pl.pallas_call(
        pack_kernel,
        in_specs=[smem()] + [vmem()] * (1 + len(first) + len(second)),
        out_specs=[vmem(), vmem()],
        out_shape=[jax.ShapeDtypeStruct((rows[0] + 16, width), BF16), jax.ShapeDtypeStruct((rows[1], width), BF16)],
        name="pack",
    )(lane, gains, *first, *second)


def to_examples(x, count):
    examples, rows, width = x.shape
    me = lax.axis_index("seq")
    if count == examples:
        buf = jnp.zeros((count, rows, width), x.dtype)
        for k in range(count):
            piece = lax.dynamic_index_in_dim(x, (me + k) % count, 0, keepdims=False)
            if k:
                piece = lax.ppermute(piece, "seq", [(s, (s + k) % count) for s in range(count)])
            buf = lax.dynamic_update_index_in_dim(buf, piece, (me - k) % count, 0)
        return buf.reshape(count * rows, width)
    group = count // examples
    all_rows = lax.all_gather(x, "seq", axis=1, tiled=True)
    one = lax.dynamic_index_in_dim(all_rows, me // group, 0, keepdims=False)
    return lax.dynamic_slice_in_dim(one, (me % group) * examples * rows, examples * rows, 0)


def to_positions(x, examples, count, *during):
    me = lax.axis_index("seq")
    width = x.shape[1]
    if count == examples:
        x = x.reshape(count, -1, width)
        buf = jnp.zeros_like(x)
        for k in range(count):
            piece = lax.dynamic_index_in_dim(x, (me + k) % count, 0, keepdims=False)
            if k:
                piece = hold(lax.ppermute(piece, "seq", [(s, (s + k) % count) for s in range(count)]), *during)
            buf = lax.dynamic_update_index_in_dim(buf, piece, (me - k) % count, 0)
        return buf
    rows = x.shape[0] // examples
    all_rows = lax.all_gather(x, "seq", axis=0, tiled=True).reshape(examples, count * rows, width)
    return lax.dynamic_slice_in_dim(all_rows, me * rows, rows, 1)


class Ring:
    def __init__(self):
        self.dp = lax.axis_size("dp")
        self.outer = self.dp // INNER
        self.columns = [[o * INNER + i for o in range(self.outer)] for i in range(INNER)]

    def inner_step(self, x, j):
        return lax.ppermute(x, "dp", [(d, d // INNER * INNER + (d + j) % INNER) for d in range(self.dp)])

    def outer_step(self, x, k):
        return lax.ppermute(x, "dp", [(d, (d + k * INNER) % self.dp) for d in range(self.dp)])

    def swap(self, x):
        return lax.ppermute(x, "seq", [(0, 1), (1, 0)])

    def column(self, shard, *during):
        return [shard] + [hold(self.outer_step(shard, k), *during) for k in range(1, self.outer)]

    def plane(self, column, *during):
        return [column] + [hold(self.inner_step(column, j), *during) for j in range(1, INNER)]

    def far_column(self, x):
        return lax.all_gather(x, "dp", axis=0, axis_index_groups=self.columns)

    def both(self, plane):
        return plane + [self.swap(x) for x in plane]

    def pairs(self, keep, send, *during):
        other = hold(self.swap(send), *during)
        return [low(keep[j].astype(F32) + other[j].astype(F32)) for j in range(INNER)]

    def across(self, pairs, *during):
        return low(summed([pairs[0]] + [hold(self.inner_step(pairs[j], j), *during) for j in range(1, INNER)]))

    def far_sum(self, total):
        return lax.psum_scatter(total, "dp", scatter_dimension=0, axis_index_groups=self.columns)

    def near_sum(self, total):
        return [total[0]] + [self.outer_step(total[k], k) for k in range(1, self.outer)]


def low(x):
    return x.astype(BF16)


def summed(parts):
    return sum(x.astype(F32) for x in parts)


def hold(x, *after):
    return lax.optimization_barrier((x, after))[0]


def per_device(source, canvas, source_len, canvas_len, cotangent, enc_attn, enc_up, enc_down, dec_attn, cross_attn,
               dec_up, dec_down, slot_proj, norm_gains):
    examples, _, width = source.shape
    seq = lax.axis_size("seq")
    devices = lax.axis_size("dp") * seq
    group = seq // examples
    me = lax.axis_index("seq")
    rank = lax.axis_index("dp") * seq + me
    groups = [[e * group + t for t in range(group)] for e in range(examples)]
    packed = seq == SEQ and lax.axis_size("dp") % INNER == 0 and enc_up.shape[0] % 16 == 0

    def whole_keys(x):
        return lax.all_gather(x, "seq", axis=0, tiled=True, axis_index_groups=groups) if group > 1 else x

    def own_keys(x):
        if group == 1:
            return x
        return lax.psum_scatter(x, "seq", scatter_dimension=0, tiled=True, axis_index_groups=groups)

    def neighbour(x, step):
        pairs = [(s, s + step) for s in range(seq) if 0 <= s % group + step < group]
        return lax.ppermute(x, "seq", pairs)

    def chunks(up):
        rows = up.shape[0]
        return up.reshape(rows, -1, width).transpose(1, 0, 2)

    def unchunk(up):
        return up.transpose(1, 0, 2).reshape(up.shape[1], -1)

    shards = {
        "enc": enc_attn, "dec": dec_attn, "cross": cross_attn, "eup": chunks(enc_up), "edown": enc_down[None],
        "dup": chunks(dec_up), "ddown": dec_down[None], "slot": slot_proj[None],
    }
    shapes = {name: (x.shape[0], x.shape[1] * devices, width) for name, x in shards.items()}
    flat = lambda name: shards[name].reshape(-1, width)
    if packed:
        ring = Ring()
        dp_index = lax.axis_index("dp")
        spot = jnp.stack([dp_index // INNER, dp_index % INNER, me]).astype(jnp.int32)
        share = norm_gains.shape[1]
        lane = jnp.reshape(rank * share, (1,)).astype(jnp.int32)
        late, flat5 = pack(lane, norm_gains, [dec_attn, enc_up, enc_down, cross_attn, slot_proj], [dec_up, dec_down])
        names = ["eup", "edown", "cross", "slot", "dup", "ddown"]
        sizes = [shapes[n][0] * shapes[n][1] // devices for n in names[:4]]
        late = ring.far_column(late)
        x5 = ring.plane(flat5)
        z1 = jnp.stack(hold(ring.column(flat("enc")), *x5[:-1]))
        g1 = ring.plane(z1)
        source, canvas, cotangent = hold((source, canvas, cotangent), z1)
        late = hold(late, *x5, *g1)
        x5 = ring.far_column(jnp.stack(hold(x5, *g1)))
        x5 = x5.reshape(-1, *x5.shape[2:])
        g1 = ring.both(g1)
        cuts = [shapes["dec"][0] * shapes["dec"][1] // devices + 16]
        cuts += [cuts[0] + sum(sizes[:2]), cuts[0] + sum(sizes)]
        late = [late[:, :cuts[0]], late[:, cuts[0]:cuts[1]], late[:, cuts[1]:]]

        def make(arrays, names, far=(True, True), **more):
            return Weights(True, arrays, [shapes[n] for n in names], spot=spot, outer=ring.outer, far=far, **more)

        w_enc = make(g1, ["enc"], (False, False))

        def fetch_dec(during):
            return make(ring.both(ring.plane(late[0], during)), ["dec"], (True, False), tail=16)

        def fetch_effn(before, during):
            return make(ring.both(ring.plane(hold(late[1], before), during)), ["eup", "edown"])

        def fetch_cross_slot(before, during):
            arrays = ring.both(ring.plane(hold(late[2], before), during))
            return make(arrays, ["cross"]), make(arrays, ["slot"], at=sizes[2])

        def fetch_dffn(before, during):
            return make([x5, hold(ring.swap(hold(x5, before)), during)], ["dup", "ddown"], block=True)
    else:
        def fetch(*names):
            return Weights(False, [lax.all_gather(shards[n], ("dp", "seq"), axis=1, tiled=True) for n in names],
                           [shapes[n] for n in names])
        w_enc = fetch("enc")
        fetch_dec = lambda *t: fetch("dec")
        fetch_effn = lambda *t: fetch("eup", "edown")
        fetch_cross_slot = lambda *t: (fetch("cross"), fetch("slot"))
        fetch_dffn = lambda *t: fetch("dup", "ddown")
        gains = lax.all_gather(norm_gains, ("dp", "seq"), axis=1, tiled=True).astype(F32)
    example = me // group
    s_len = lax.dynamic_slice_in_dim(source_len, example, 1)
    c_len = lax.dynamic_slice_in_dim(canvas_len, example, 1)
    src = to_examples(source, seq)
    can = to_examples(canvas, seq)
    cot = to_examples(cotangent, seq)
    src_all = whole_keys(src)
    can_all = whole_keys(can)
    q_a, k_a, v_a, o_a, x_a, r_a = attn_forward(s_len, w_enc, xq=src, xk=src_all)
    w_dec = fetch_dec(r_a)
    can = hold(can, r_a)
    q_b, k_b, v_b, o_b, x_b, r_c, *tail = attn_forward(c_len, w_dec, xq=can, xk=can if group == 1 else can_all)
    gains = tail[0] if packed else gains
    gain = [gains[i:i + 1] for i in range(5)]
    w_effn = fetch_effn(r_a, r_c)
    h_a, act_a, slope_a, r_b = ffn_forward(hold(r_a, r_c), gain[0], w_effn)
    w_cross, w_slot = fetch_cross_slot(r_c, r_b)
    low_one, low_enc, q_c, k_c, v_c, o_c, x_c, r_d = attn_forward(
        s_len, w_cross, rq=r_c, rk=whole_keys(r_b), gq=gain[2], gk=gain[1])
    w_dffn = fetch_dffn(r_b, r_d)
    h_b, act_b, slope_b, r_e = ffn_forward(r_d, gain[3], w_dffn)
    halo = []
    if group > 1:
        place = jnp.stack([me % group * src.shape[0], me % group < group - 1]).astype(jnp.int32)
        halo = [place, neighbour(r_e[:8], -1), neighbour(cot[-8:][::-1], 1)]
    slot_out, dr, dg4, *d_slot = slot_step(c_len, r_e, gain[4], w_slot, cot, halo)
    dr, dg3, *d_dffn = ffn_backward(dr, h_b, act_b, slope_b, w_dffn, r_d, gain[3], "slot", d_slot)
    slot_out = to_positions(slot_out, examples, seq)
    if packed:
        p1 = ring.pairs(*d_dffn)
        dr = hold(dr, *p1)
    alone = group == 1
    norms = [(r_c, gain[2])] + ([(r_b, gain[1])] if alone else [])
    dr_c, dr_b, dg2, *rest = attn_backward(False, s_len, dr, w_cross, q_c, k_c, v_c, o_c, x_c, low_one, low_enc, norms)
    if alone:
        dg1, *d_cross = rest
    else:
        d_cross = rest
        dr_b, dg1 = norm_back(r_b, gain[1], own_keys(dr_b))
    if packed:
        s1 = ring.across(p1, dr_b)
        d_cross = hold(tuple(d_cross), s1)
        dr_b = hold(dr_b, s1, slot_out)
    dr_a, dg0, *d_effn = ffn_backward(dr_b, h_a, act_a, slope_a, w_effn, r_a, gain[0], "gains", [dg1, dg2, dg3, dg4])
    if packed:
        p2 = ring.pairs(*d_cross, dr_a)
        p3 = ring.pairs(*hold(tuple(d_effn), *p2))
        dr_c = hold(dr_c, *p3)
    sides = 1 if alone else 2
    out = attn_backward(alone, c_len, dr_c, w_dec, q_b, k_b, v_b, o_b, x_b, can, can_all)
    d_can, d_dec = out[:sides], out[sides:]
    canvas_grad = d_can[0] if alone else d_can[0] + own_keys(d_can[1])
    if packed:
        def split(total, *names):
            out, at = [], 0
            for n in names:
                count = shards[n].shape[0] * shards[n].shape[1]
                out.append(total[at:at + count].astype(F32).reshape(shards[n].shape))
                at += count
            return out, total[at:].astype(F32)
        s2 = ring.across(p2, canvas_grad)
        s3 = ring.across(p3, canvas_grad)
        p4 = ring.pairs(*hold(tuple(d_dec), s2, s3))
        z1 = ring.far_sum(s1)
        dr_a = hold(dr_a, z1, *p4)
        z2, z3 = ring.far_sum(s2), ring.far_sum(s3)
    out = attn_backward(alone, s_len, dr_a, w_enc, q_a, k_a, v_a, o_a, x_a, src, src_all)
    d_src, d_enc = out[:sides], out[sides:]
    source_grad = d_src[0] if alone else d_src[0] + own_keys(d_src[1])

    if packed:
        s4 = ring.across(p4, source_grad)
        canvas_grad = to_positions(canvas_grad, examples, seq, source_grad)
        p5 = ring.pairs(*hold(tuple(d_enc), s4, z2, z3))
        z1, z2, z3 = hold((z1, z2, z3), *p5)
        (t_dup, t_ddown, t_slot), _ = split(z1, "dup", "ddown", "slot")
        (t_cross,), _ = split(z2, "cross")
        (t_eup, t_edown), t_gains = split(z3, "eup", "edown")
        t_eup, t_dup = unchunk(t_eup), unchunk(t_dup)
        source_grad = to_positions(hold(source_grad, *p5), examples, seq)
        s5 = ring.across(p5)
        z45 = hold(jnp.concatenate([s4, s5], axis=1), source_grad, canvas_grad)
        z45 = summed(ring.near_sum(z45))
        (t_dec, t_enc), _ = split(z45, "dec", "enc")
        t_gains = lax.dynamic_slice(t_gains, (0, rank * share), (5, share))
    else:
        def home(x):
            return lax.psum_scatter(x, ("dp", "seq"), scatter_dimension=1, tiled=True).astype(F32)
        t_enc, t_dec, t_cross = home(d_enc[0]), home(d_dec[0]), home(d_cross[0])
        t_eup, t_edown, t_dup, t_ddown, t_slot = (home(x) for x in (*d_effn, *d_dffn, *d_slot))
        t_eup, t_dup = unchunk(t_eup), unchunk(t_dup)
        t_gains = home(jnp.concatenate([dg0, dg1, dg2, dg3, dg4], axis=0))
        source_grad = to_positions(source_grad, examples, seq)
        canvas_grad = to_positions(canvas_grad, examples, seq)

    return (
        slot_out, source_grad, canvas_grad,
        t_enc, t_eup, t_edown[0], t_dec, t_cross, t_dup, t_ddown[0], t_slot[0], t_gains,
    )


def solution(mesh):
    by_seq = P("dp", "seq", None)
    stack = P(None, ("dp", "seq"), None)
    by_row = P(("dp", "seq"), None)
    gains = P(None, ("dp", "seq"))
    in_specs = (by_seq, by_seq, P("dp"), P("dp"), by_seq, stack, by_row, by_row, stack, stack, by_row, by_row, by_row,
                gains)
    out_specs = (by_seq, by_seq, by_seq, stack, by_row, by_row, stack, stack, by_row, by_row, by_row, gains)
    return jax.shard_map(per_device, mesh=mesh, in_specs=in_specs, out_specs=out_specs, check_vma=False)
```

```python
import functools
import math

import jax
import jax.numpy as jnp
from jax import lax
from jax.experimental import pallas as pl
from jax.experimental.pallas import tpu as pltpu
from jax.sharding import PartitionSpec as P

F32 = jnp.float32
BF16 = jnp.bfloat16
H = 8
HD = 64
PAIR = 2 * HD
LOG2E = math.log2(math.e)
Q_SCALE = LOG2E / 8.0
K_BACK = 1.0 / LOG2E
MASKED = -1e30
VMEM_LIMIT = 58 * 1024 * 1024
PARAMS = pltpu.CompilerParams(vmem_limit_bytes=VMEM_LIMIT)


def nn(a, b):
    return lax.dot_general(a, b, (((1,), (0,)), ((), ())), preferred_element_type=F32)


def nt(a, b):
    return lax.dot_general(a, b, (((1,), (1,)), ((), ())), preferred_element_type=F32)


def tn(a, b):
    return lax.dot_general(a, b, (((0,), (0,)), ((), ())), preferred_element_type=F32)


def norm_parts(r):
    centre = r - jnp.mean(r, axis=-1, keepdims=True)
    rs = lax.rsqrt(jnp.mean(centre * centre, axis=-1, keepdims=True) + 1e-5)
    return centre * rs, rs


def norm(r, gain):
    return norm_parts(r)[0] * gain


def norm_back(r, gain, dy):
    z, rs = norm_parts(r)
    t = dy * gain
    dr = (t - jnp.mean(t, axis=-1, keepdims=True) - z * jnp.mean(t * z, axis=-1, keepdims=True)) * rs
    return dr, jnp.sum(dy * z, axis=0, keepdims=True)


def lanes(rows):
    return lax.broadcasted_iota(jnp.int32, (rows, PAIR), 1)


def key_extras(length, count):
    row = lax.broadcasted_iota(jnp.int32, (count, PAIR), 0)
    lane = lanes(count)
    bias = jnp.where(row < length, 0.0, MASKED)
    return jnp.where(lane == 3, bias, jnp.where(lane < 3, 1.0, 0.0)).astype(BF16)


def three_parts(v):
    hi = v.astype(BF16)
    rest = v - hi.astype(F32)
    mid = rest.astype(BF16)
    low = rest - mid.astype(F32)
    return hi.astype(F32), mid.astype(F32), low


def spread_parts(v, last):
    lane = lanes(v.shape[0])
    hi, mid, low = three_parts(v)
    tail = jnp.where(lane == 3, last, 0.0)
    return jnp.where(lane == 0, hi, jnp.where(lane == 1, mid, jnp.where(lane == 2, low, tail))).astype(BF16)


def row_of(ref, row):
    return ref[row:row + 1, :]


def whole(shape):
    return pl.BlockSpec(shape, lambda i: (0,) * len(shape))


def smem():
    return pl.BlockSpec(memory_space=pltpu.SMEM)


def vmem():
    return pl.BlockSpec(memory_space=pltpu.VMEM)


def cost(flops, nbytes, exps=0):
    return pl.CostEstimate(flops=int(flops), bytes_accessed=int(nbytes), transcendentals=int(exps))


INNER = 4
SEQ = 2


class Spot:
    def __init__(self, ref, outer, far):
        self.outer, self.far = outer, far
        self.o, self.i, self.s = ref[0], ref[1], ref[2]

    def owner(self, c, j, k):
        o = k if self.far else lax.rem(self.o - k + self.outer, self.outer)
        i = j if self.far > 1 else lax.rem(self.i - j + INNER, INNER)
        return (o * INNER + i) * SEQ + lax.rem(self.s - c + SEQ, SEQ)

    def ahead(self, o, i):
        return (i if self.far > 1 else lax.rem(i - self.i + INNER, INNER),
                o if self.far else lax.rem(o - self.o + self.outer, self.outer))


def assemble(spot, refs, at, dst, block):
    stack, total, _ = dst.shape
    share = total // (spot.outer * INNER * SEQ)
    for c in range(SEQ):
        for j in range(INNER):
            for k in range(spot.outer):
                ref, x = (refs[c], (k, j)) if block else (refs[c * INNER + j], (k,))
                rows = pl.ds(pl.multiple_of(spot.owner(c, j, k) * share, share), share)
                for a in range(stack):
                    dst[a, rows, :] = ref[(*x, slice(at + a * share, at + (a + 1) * share))]


def deal(spot, src, at, keep, send):
    stack, total, _ = src.shape
    share = total // (spot.outer * INNER * SEQ)
    for core in range(SEQ):
        @pl.when(spot.s == core)
        def _():
            for o in range(spot.outer):
                for i in range(INNER):
                    j, k = spot.ahead(o, i)
                    for s in range(SEQ):
                        first = ((o * INNER + i) * SEQ + s) * share
                        dst = keep if s == core else send
                        for a in range(stack):
                            dst[j, k, at + a * share:at + (a + 1) * share, :] = src[a, first:first + share, :]


class Weights:
    def __init__(self, packed, arrays, shapes, at=0, spot=None, outer=0, far=(0, 0), block=False, tail=0):
        self.packed, self.arrays, self.shapes, self.at, self.spot, self.outer = packed, arrays, shapes, at, spot, outer
        self.far, self.block, self.tail = far, block, tail

    def share(self, shape):
        return shape[0] * shape[1] // (self.outer * INNER * SEQ)

    def args(self):
        return [self.spot, *self.arrays] if self.packed else list(self.arrays)

    def specs(self, dims):
        zero = lambda n: (lambda *_: (0,) * n)
        if not self.packed:
            return [pl.BlockSpec(x.shape, zero(3), pipeline_mode=pl.Buffered(1)) if dims else vmem() for x in self.arrays]
        rows = sum(self.share(s) for s in self.shapes) + self.tail
        index = self.at // rows
        lead = (self.outer, INNER) if self.block else (self.outer,)
        spec = lambda: pl.BlockSpec((*lead, rows, self.shapes[0][2]), lambda *_: (*(0 for _ in lead), index, 0),
                                    **(dict(pipeline_mode=pl.Buffered(1)) if dims else {}))
        return [smem()] + [spec() for _ in self.arrays]

    def scratch(self):
        return [pltpu.VMEM(s, BF16) for s in self.shapes] if self.packed else []

    def n_args(self):
        return len(self.arrays) + 1 if self.packed else len(self.arrays)

    def n_scratch(self):
        return len(self.shapes) if self.packed else 0

    def load(self, refs, scratch, first):
        if not self.packed:
            return list(refs)

        @pl.when(first)
        def _():
            spot = Spot(refs[0], self.outer, self.far[0])
            at = 0
            for shape, dst in zip(self.shapes, scratch):
                assemble(spot, refs[1:], at, dst, self.block)
                at += self.share(shape)
        return list(scratch)

    def plain_shapes(self):
        return [jax.ShapeDtypeStruct(s, BF16) for s in self.shapes] if self.packed else []

    def plain_blocks(self, steps):
        blocks = []
        for a, m, width in self.shapes if self.packed else []:
            if a % steps == 0:
                blocks.append(((a // steps, m, width), 0))
            else:
                assert m % steps == 0
                blocks.append(((a, m // steps, width), 1))
        return blocks

    def plain_specs(self, steps):
        first, second = (lambda i: (i, 0, 0)), (lambda i: (0, i, 0))
        return [pl.BlockSpec(b, second if dim else first) for b, dim in self.plain_blocks(steps)]

    def plain_store(self, outs, scratch, steps):
        i = pl.program_id(0)
        for out, src, (block, dim) in zip(outs, scratch, self.plain_blocks(steps)):
            n = block[dim]
            part = pl.ds(pl.multiple_of(i * n, n), n)
            out[...] = src[:, part, :] if dim else src[part]

    def grad_shapes(self, extra=0):
        if not self.packed:
            return [jax.ShapeDtypeStruct(s, BF16) for s in self.shapes]
        rows = sum(self.share(s) for s in self.shapes) + extra
        return [jax.ShapeDtypeStruct((INNER, self.outer, rows, self.shapes[0][2]), BF16)] * SEQ

    def grad_scratch(self):
        return [pltpu.VMEM(s, BF16) for s in self.shapes] if self.packed else []

    def place(self):
        return [self.spot] if self.packed else []

    def store(self, place, grads, outs, last):
        if not self.packed:
            return

        @pl.when(last)
        def _():
            spot = Spot(place[0], self.outer, self.far[1])
            at = 0
            for shape, src in zip(self.shapes, grads):
                deal(spot, src, at, *outs)
                at += self.share(shape)


def other_half(place_ref, ref):
    half = ref.shape[0] // 2
    return ref[pl.ds(pl.multiple_of((1 - place_ref[2]) * half, half), half), :]


def cut(refs, *counts):
    out, at = [], 0
    for n in counts:
        out.append(refs[at:at + n])
        at += n
    assert at == len(refs)
    return out


def attn_fwd_kernel(cross, gq, gk, steps, w, *refs):
    n_in, n_out = (5, 8) if cross else (4, 6)
    n_tail = 1 if w.tail else 0
    ins, w_refs, outs, tail, plain, (kaug, vaug), xk_s, w_scr = cut(
        refs, n_in, w.n_args(), n_out, n_tail, w.n_scratch(), 2, 1 if cross else 0, w.n_scratch())
    count = kaug.shape[1]
    i = pl.program_id(0)
    start = i == 0
    w_ref, = w.load(w_refs, w_scr, start)
    if cross:
        len_ref, place_ref, rq_ref, rk_ref, g_ref = ins
        xq_ref, xk_ref, q_ref, k_ref, v_ref, o_ref, qx_ref, r_ref = outs
    else:
        len_ref, place_ref, xq_ref, xk_ref = ins
        q_ref, k_ref, v_ref, o_ref, qx_ref, r_ref = outs
    rows = r_ref.shape[0]

    @pl.when(start)
    def _():
        if w.tail:
            parts = [x[k, w.share(w.shapes[0]):, :].astype(F32) for x in w_refs[1:] for k in range(w.outer)]
            tail[0][...] = sum(parts[1:], parts[0])
        if cross:
            xk = norm(rk_ref[...], row_of(g_ref, gk)).astype(BF16)
            xk_s[0][...] = xk
        else:
            xk = xk_ref[...]
        k = nn(xk, w_ref[1]).astype(BF16)
        v = nn(xk, w_ref[2]).astype(BF16)
        extras = key_extras(len_ref[place_ref[3]], count)
        ones = jnp.ones((count, PAIR), BF16)
        for p in range(H // 2):
            kaug[p, :, :PAIR] = k[:, p * PAIR:(p + 1) * PAIR]
            kaug[p, :, PAIR:] = extras
            vaug[p, :, :PAIR] = v[:, p * PAIR:(p + 1) * PAIR]
            vaug[p, :, PAIR:] = ones
        k_ref[...] = k
        v_ref[...] = v

    w.plain_store(plain, w_scr, steps)
    if cross:
        xk_ref[...] = xk_s[0][pl.ds(pl.multiple_of(i * (count // steps), count // steps), count // steps), :]
        resid = norm(rq_ref[...], row_of(g_ref, gq))
        xq = resid.astype(BF16)
        xq_ref[...] = xq
    else:
        xq = xq_ref[...]
        resid = xq.astype(F32)
    q = nn(xq, w_ref[0]) * Q_SCALE
    q_ref[...] = q.astype(BF16)
    lane = lanes(rows)
    first = lane < HD
    extra = jnp.where(lane == 3, 1.0, 0.0).astype(BF16)

    def score(h):
        p = h // 2
        mine = first if h % 2 == 0 else lane >= HD
        qm = jnp.where(mine, q[:, p * PAIR:(p + 1) * PAIR], 0.0).astype(BF16)
        return nt(jnp.concatenate([qm, extra], axis=1), kaug[p])

    halves = []
    ahead = score(0)
    for h in range(H):
        s = ahead
        if h + 1 < H:
            ahead = score(h + 1)
        m = jnp.max(s, axis=1, keepdims=True)
        o = nn(jnp.exp2(s - m).astype(BF16), vaug[h // 2])
        total = o[:, PAIR:]
        halves.append(o[:, :PAIR] / total)
        qx_ref[h] = spread_parts(-(m + jnp.log2(total)), 1.0)
    blended = [jnp.where(first, halves[2 * p], halves[2 * p + 1]).astype(BF16) for p in range(H // 2)]
    o_all = jnp.concatenate(blended, axis=1)
    o_ref[...] = o_all
    r_ref[...] = resid + nn(o_all, w_ref[3])


def attn_forward(length, w, xq=None, xk=None, rq=None, rk=None, gq=None, gk=None):
    cross = rq is not None
    rows, width = (rq if cross else xq).shape
    count = (rk if cross else xk).shape[0]
    blk = math.gcd(rows, 512)
    steps = rows // blk
    sds = jax.ShapeDtypeStruct
    by_rows = pl.BlockSpec((blk, width), lambda i: (i, 0))
    by_keys = pl.BlockSpec((count // steps, width), lambda i: (i, 0))
    outs = [
        sds((rows, width), BF16), sds((count, width), BF16), sds((count, width), BF16),
        sds((rows, width), BF16), sds((H, rows, PAIR), BF16), sds((rows, width), F32),
    ]
    out_specs = [by_rows, whole((count, width)), whole((count, width)), by_rows, pl.BlockSpec((H, blk, PAIR), lambda i: (0, i, 0)), by_rows]
    if cross:
        args = [*length, rq, rk, gq[0]]
        in_specs = [smem(), smem(), by_rows, whole((count, width)), whole(gq[0].shape)]
        outs = [sds((rows, width), BF16), sds((count, width), BF16)] + outs
        out_specs = [by_rows, by_keys] + out_specs
    else:
        args = [*length, xq, xk]
        in_specs = [smem(), smem(), by_rows, whole((count, width))]
    if w.tail:
        outs.append(sds((w.tail, width), F32))
        out_specs.append(whole((w.tail, width)))
    out = pl.pallas_call(
        functools.partial(attn_fwd_kernel, cross, *((gq[1], gk[1]) if cross else (0, 0)), steps, w),
        grid=(steps,),
        in_specs=in_specs + w.specs(1),
        out_specs=out_specs + w.plain_specs(steps),
        out_shape=outs + w.plain_shapes(),
        scratch_shapes=[pltpu.VMEM((H // 2, count, 2 * PAIR), BF16)] * 2
        + ([pltpu.VMEM((count, width), BF16)] if cross else []) + w.scratch(),
        compiler_params=PARAMS,
        cost_estimate=cost(rows * count * 5 * 512 * H, 14 << 20, rows * count * H),
        name="cross_fwd" if cross else "self_fwd",
    )(*args, *w.args())
    return out if w.packed else [*out, *w.arrays]


def pair_back(k_ref, v_ref, q_ref, qx_ref, o, do, kaug, vaug, qaug, oaug, kt, dqt):
    count, rows = kaug.shape[0], o.shape[0]
    blk = math.gcd(count, 512)
    kaug[:, :PAIR] = k_ref[...]
    vaug[:, :PAIR] = v_ref[...]
    kt[...] = k_ref[...].T
    lane = lanes(rows)
    inner = -(o.astype(F32) * do.astype(F32))
    high = inner.astype(BF16).astype(F32)
    rest = pltpu.roll(inner - high, HD, 1)
    q, do = q_ref[...].astype(F32), do.astype(F32)
    for h in range(2):
        mine = lane < HD if h == 0 else lane >= HD
        qaug[h, :, :PAIR] = jnp.where(mine, q, 0.0).astype(BF16)
        qaug[h, :, PAIR:] = qx_ref[h]
        oaug[h, :, :PAIR] = jnp.where(mine, do, 0.0).astype(BF16)
        oaug[h, :, PAIR:] = jnp.where(mine, high, rest).astype(BF16)
    for j in range(count // blk):
        keys = slice(j * blk, (j + 1) * blk)
        dv_sum = dk_sum = None
        for h in range(2):
            pt = jnp.exp2(nt(kaug[keys, :], qaug[h]))
            dpt = nt(vaug[keys, :], oaug[h])
            ptb = pt.astype(BF16)
            dst = (pt * dpt).astype(BF16)
            dv_h = nn(ptb, oaug[h, :, :PAIR])
            dk_h = nn(dst, qaug[h, :, :PAIR])
            dq_h = nn(kt[h * HD:(h + 1) * HD, keys], dst)
            dv_sum = dv_h if h == 0 else dv_sum + dv_h
            dk_sum = dk_h if h == 0 else dk_sum + dk_h
            if j == 0:
                dqt[h * HD:(h + 1) * HD, :] = dq_h
            else:
                dqt[h * HD:(h + 1) * HD, :] += dq_h
        yield keys, (dk_sum * K_BACK).astype(BF16), dv_sum.astype(BF16)


def attn_bwd_kernel(gains, same, w, *refs):
    norms = len(gains)
    n_out = 1 if same else 2
    n_dg = 0 if same else norms
    n_send = 1 if same and w.packed else 0
    n_grad = 2 if w.packed else 1
    (len_ref, place_ref, dr_ref, w3_ref, w_ref, q_ref, k_ref, v_ref, o_ref, qx_ref), x_refs, n_refs, place, outs, send, dg_refs, dw_outs, \
        (dab, do_s, kaug, vaug, qaug, oaug, kt, ot, dqt, grads_q, grads_k, w_all), xts, dw_scr = cut(
            refs, 10, n_out, 2 * norms, len(w.place()), n_out, n_send, n_dg, n_grad, 12, n_out, w.n_scratch())
    dw_ref, = dw_scr if w.packed else dw_outs
    count = kaug.shape[0]
    rows, width = dab.shape
    p = pl.program_id(0)

    @pl.when(p == 0)
    def _():
        dab[...] = dr_ref[...].astype(BF16)
        kaug[:, PAIR:] = key_extras(len_ref[place_ref[3]], count)
        vaug[:, PAIR:] = jnp.ones((count, PAIR), BF16)
        do = nt(dab[...], w3_ref[0]).astype(BF16)
        for n in range(H // 2):
            do_s[n] = do[:, n * PAIR:(n + 1) * PAIR]

    @pl.when(p < 3)
    def _():
        w_all[:, pl.ds(pl.multiple_of(p * width, PAIR), width)] = w_ref[0]

    own = pl.ds(pl.multiple_of(p * PAIR, PAIR), PAIR)
    behind = pl.ds(pl.multiple_of(width + p * PAIR, PAIR), PAIR)
    o, do = o_ref[...], do_s[p]
    ot[own, :] = o.T
    for x, xt in zip(x_refs, xts):
        xt[own, :] = x[...].T
    for keys, dk, dv in pair_back(k_ref, v_ref, q_ref, qx_ref, o, do, kaug, vaug, qaug, oaug, kt, dqt):
        grads_k[keys, own] = dk
        grads_k[keys, behind] = dv
    grads_q[:, own] = (dqt[...].T * 0.125).astype(BF16)
    last = p == pl.num_programs(0) - 1

    @pl.when(last)
    def _():
        dw_ref[0] = nn(xts[0][...], grads_q[...]).astype(BF16)
        both = nn(xts[-1][...], grads_k[...]).astype(BF16)
        dw_ref[1] = both[:, :width]
        dw_ref[2] = both[:, width:]
        dw_ref[3] = nn(ot[...], dab[...]).astype(BF16)
        dxq = dr_ref[...] + nt(grads_q[...], w_all[:, :width])
        dxk = nt(grads_k[...], w_all[:, width:])
        if same:
            outs[0][...] = dxq + dxk
            if n_send:
                send[0][...] = other_half(place_ref, outs[0])
        else:
            for n, value in enumerate((dxq, dxk)):
                if n < norms:
                    gain = row_of(n_refs[2 * n + 1], gains[n])
                    value, dg_refs[n][...] = norm_back(n_refs[2 * n][...], gain, value)
                outs[n][...] = value

    w.store(place, [dw_ref], dw_outs, last)


def attn_backward(same, length, dr, w, plain, q, k, v, o, qx, xs, norms=()):
    rows, width = dr.shape
    count = k.shape[0]
    sds = jax.ShapeDtypeStruct
    pair_of = lambda n: pl.BlockSpec((n, PAIR), lambda i: (0, i))
    once = lambda shape, index=None: pl.BlockSpec(
        shape, lambda i: index or (0,) * len(shape), pipeline_mode=pl.Buffered(1))
    in_specs = [
        smem(), smem(), once((rows, width)), once((1, width, width), (3, 0, 0)),
        pl.BlockSpec((1, width, width), lambda i: (jnp.minimum(i, 2), 0, 0)),
        pair_of(rows), pair_of(count), pair_of(count), pair_of(rows),
        pl.BlockSpec((2, rows, PAIR), lambda i: (i, 0, 0)),
    ] + [pair_of(x.shape[0]) for x in xs]
    norm_args = []
    for r, g in norms:
        norm_args += [r, g[0]]
        in_specs += [once(r.shape), once(g[0].shape)]
    outs = [sds((rows, width), F32)]
    if not same:
        outs += [sds((count, width), F32)] + [sds((1, width), F32)] * len(norms)
    elif w.packed:
        outs.append(sds((rows // 2, width), F32))
    outs += w.grad_shapes()
    vm = pltpu.VMEM
    return pl.pallas_call(
        functools.partial(attn_bwd_kernel, [g[1] for _, g in norms], same, w),
        grid=(H // 2,),
        in_specs=in_specs + [smem()] * len(w.place()),
        out_specs=[whole(s.shape) for s in outs],
        out_shape=outs,
        scratch_shapes=[
            vm((rows, width), BF16), vm((H // 2, rows, PAIR), BF16),
            vm((count, 2 * PAIR), BF16), vm((count, 2 * PAIR), BF16),
            vm((2, rows, 2 * PAIR), BF16), vm((2, rows, 2 * PAIR), BF16), vm((PAIR, count), BF16), vm((width, rows), BF16),
            vm((PAIR, rows), F32), vm((rows, width), BF16), vm((count, 2 * width), BF16), vm((width, 3 * width), BF16),
        ] + [vm((width, x.shape[0]), BF16) for x in xs] + w.grad_scratch(),
        compiler_params=PARAMS,
        cost_estimate=cost(rows * count * 9 * 512 * H, 20 << 20, rows * count * H),
        name="self_bwd" if same else "cross_bwd",
    )(*length, dr, plain, plain, q, k, v, o, qx, *xs, *norm_args, *w.place())


def attn_grads_kernel(w, len_ref, place_ref, dr_ref, w3_ref, q_ref, k_ref, v_ref, o_ref, qx_ref, x_ref, grads_ref, *refs):
    dw_outs, (dab, do_s, kaug, vaug, qaug, oaug, kt, ot, xt, dqt), (dw_ref,) = cut(refs, 2, 10, 1)
    count = kaug.shape[0]
    width = dab.shape[1]
    p = pl.program_id(0)

    @pl.when(p == 0)
    def _():
        dab[...] = dr_ref[...].astype(BF16)
        kaug[:, PAIR:] = key_extras(len_ref[place_ref[3]], count)
        vaug[:, PAIR:] = jnp.ones((count, PAIR), BF16)
        do = nt(dab[...], w3_ref[0]).astype(BF16)
        for n in range(H // 2):
            do_s[n] = do[:, n * PAIR:(n + 1) * PAIR]

    own = pl.ds(pl.multiple_of(p * PAIR, PAIR), PAIR)
    part = lambda n: pl.ds(pl.multiple_of(n * width + p * PAIR, PAIR), PAIR)
    o, do = o_ref[...], do_s[p]
    ot[own, :] = o.T
    xt[own, :] = x_ref[...].T
    for keys, dk, dv in pair_back(k_ref, v_ref, q_ref, qx_ref, o, do, kaug, vaug, qaug, oaug, kt, dqt):
        grads_ref[keys, part(1)] = dk
        grads_ref[keys, part(2)] = dv
    grads_ref[:, part(0)] = (dqt[...].T * 0.125).astype(BF16)
    last = p == pl.num_programs(0) - 1

    @pl.when(last)
    def _():
        dw = nn(xt[...], grads_ref[...]).astype(BF16)
        for n in range(3):
            dw_ref[n] = dw[:, n * width:(n + 1) * width]
        dw_ref[3] = nn(ot[...], dab[...]).astype(BF16)

    w.store([place_ref], [dw_ref], dw_outs, last)


def attn_grads(length, dr, w, plain, q, k, v, o, qx, x):
    rows, width = dr.shape
    sds = jax.ShapeDtypeStruct
    vm = pltpu.VMEM
    once = lambda shape, index=None: pl.BlockSpec(
        shape, lambda i: index or (0,) * len(shape), pipeline_mode=pl.Buffered(1))
    pair = pl.BlockSpec((rows, PAIR), lambda i: (0, i))
    outs = [sds((rows, 3 * width), BF16)] + w.grad_shapes()
    return pl.pallas_call(
        functools.partial(attn_grads_kernel, w),
        grid=(H // 2,),
        in_specs=[smem(), smem(), once((rows, width)), once((1, width, width), (3, 0, 0))] + [pair] * 4
        + [pl.BlockSpec((2, rows, PAIR), lambda i: (i, 0, 0)), pair],
        out_specs=[whole(x.shape) for x in outs],
        out_shape=outs,
        scratch_shapes=[
            vm((rows, width), BF16), vm((H // 2, rows, PAIR), BF16), vm((rows, 2 * PAIR), BF16), vm((rows, 2 * PAIR), BF16),
            vm((2, rows, 2 * PAIR), BF16), vm((2, rows, 2 * PAIR), BF16), vm((PAIR, rows), BF16), vm((width, rows), BF16),
            vm((width, rows), BF16), vm((PAIR, rows), F32),
        ] + w.grad_scratch(),
        compiler_params=PARAMS,
        cost_estimate=cost(rows * rows * 9 * 512 * H, 14 << 20, rows * rows * H),
        name="grads_bwd",
    )(*length, dr, plain, q, k, v, o, qx, x)


def input_grad_kernel(place_ref, dr_ref, grads_ref, *refs):
    *w_refs, out_ref, send_ref = refs
    out_ref[...] = dr_ref[...] + nt(grads_ref[...], jnp.concatenate([w[0] for w in w_refs], axis=1))

    @pl.when(pl.program_id(0) != place_ref[2])
    def _():
        send_ref[...] = out_ref[...]


def input_grad(place, dr, grads, plain):
    rows, width = dr.shape
    blk = rows // SEQ
    by_rows = lambda x: pl.BlockSpec((blk, x.shape[1]), lambda i: (i, 0))
    matrix = lambda n: pl.BlockSpec((1, width, width), lambda i: (n, 0, 0))
    return pl.pallas_call(
        input_grad_kernel,
        grid=(rows // blk,),
        in_specs=[smem(), by_rows(dr), by_rows(grads)] + [matrix(n) for n in range(3)],
        out_specs=[by_rows(dr), whole((blk, width))],
        out_shape=[jax.ShapeDtypeStruct(dr.shape, F32), jax.ShapeDtypeStruct((blk, width), F32)],
        compiler_params=PARAMS,
        cost_estimate=cost(6 * rows * width * width, 9 << 20),
        name="input_grad",
    )(place, dr, grads, plain, plain, plain)


def gelu_parts(u):
    phi = 0.5 + 0.5 * lax.erf(u * math.sqrt(0.5))
    return u * phi, phi + u * jnp.exp2(u * u * (-0.5 * LOG2E)) * (1.0 / math.sqrt(2.0 * math.pi))


def ffn_fwd_kernel(gain, steps, w, *refs):
    (r_ref, g_ref), w_refs, (h_ref, a_ref, d_ref, out_ref), plain, w_scr = cut(
        refs, 2, w.n_args(), 4, w.n_scratch(), w.n_scratch())
    up_ref, down_ref = w.load(w_refs, w_scr, pl.program_id(0) == 0)
    w.plain_store(plain, w_scr, steps)
    hidden = norm(r_ref[...], row_of(g_ref, gain))
    low = hidden.astype(BF16)
    h_ref[...] = low
    total = hidden
    span = up_ref.shape[2]
    for c in range(up_ref.shape[0]):
        cols = slice(c * span, (c + 1) * span)
        act, slope = gelu_parts(nn(low, up_ref[c]))
        act = act.astype(BF16)
        a_ref[:, cols] = act
        d_ref[:, cols] = slope.astype(BF16)
        total = total + nn(act, down_ref[0, cols, :])
    out_ref[...] = total


def ffn_forward(r, gain, w):
    rows, width = r.shape
    inner = w.shapes[1][1]
    blk = math.gcd(rows, 512)
    steps = rows // blk
    sds = jax.ShapeDtypeStruct
    by_rows = lambda n: pl.BlockSpec((blk, n), lambda i: (i, 0))
    out = pl.pallas_call(
        functools.partial(ffn_fwd_kernel, gain[1], steps, w),
        grid=(steps,),
        in_specs=[by_rows(width), whole(gain[0].shape)] + w.specs(1),
        out_specs=[by_rows(width), by_rows(inner), by_rows(inner), by_rows(width)] + w.plain_specs(steps),
        out_shape=[sds((rows, width), BF16), sds((rows, inner), BF16), sds((rows, inner), BF16), sds((rows, width), F32)]
        + w.plain_shapes(),
        scratch_shapes=w.scratch(),
        compiler_params=PARAMS,
        cost_estimate=cost(12 * rows * width * inner, 17 << 20, rows * inner * 2),
        name="ffn_fwd",
    )(r, gain[0], *w.args())
    return out if w.packed else [*out, *w.arrays]


def ffn_bwd_kernel(gain, w, kind, *refs):
    n_more = {"none": 0, "slot": 2, "gains": 4}[kind]
    (dr_ref, h_ref, a_ref, d_ref, r_ref, g_ref, up_ref, down_ref), more, place, (dout_ref, dg_ref), dw_outs, \
        (low, ht, acc, r_s), dw_scr = cut(refs, 8, n_more, len(w.place()), 2, 2, 4, w.n_scratch())
    n = pl.program_id(0)
    dup_ref, ddown_ref = dw_scr if w.packed else dw_outs

    @pl.when(n == 0)
    def _():
        grad = dr_ref[...]
        acc[...] = grad
        low[...] = grad.astype(BF16)
        ht[...] = h_ref[...].T

    grad = low[...]
    some = r_ref.shape[0]
    r_s[pl.ds(pl.multiple_of(n * some, some), some), :] = r_ref[...]
    span = up_ref.shape[2]
    rows = pl.ds(pl.multiple_of(n * span, span), span)
    ddown_ref[0, rows, :] = tn(a_ref[...], grad).astype(BF16)
    du = (nt(grad, down_ref[0]) * d_ref[...].astype(F32)).astype(BF16)
    dup_ref[n] = nn(ht[...], du).astype(BF16)
    acc[...] += nt(du, up_ref[0])
    last = n == pl.num_programs(0) - 1

    @pl.when(last)
    def _():
        dout_ref[...], dg_ref[...] = norm_back(r_s[...], row_of(g_ref, gain), acc[...])

    w.store(place, [dup_ref, ddown_ref], dw_outs, last)
    if not w.packed or kind == "none":
        return
    at = sum(w.share(s) for s in w.shapes)

    @pl.when(last)
    def _():
        if kind == "slot":
            for src, dst in zip(more, dw_outs):
                dst[:, :, at:, :] = src[...]
        else:
            gains = [dg_ref] + list(more)
            row = lax.broadcasted_iota(jnp.int32, (16, dg_ref.shape[1]), 0)
            block = jnp.zeros((16, dg_ref.shape[1]), F32)
            for x, ref in enumerate(gains):
                block = jnp.where(row == x, ref[...], block)
            block = block.astype(BF16)
            for dst in dw_outs:
                for j in range(INNER):
                    for k in range(w.outer):
                        dst[j, k, at:, :] = block


def ffn_backward(dr, hidden, act, slope, w, plain, r, gain, kind="none", more=()):
    rows, width = dr.shape
    inner = w.shapes[1][1]
    span = inner // w.shapes[0][0]
    steps = inner // span
    sds = jax.ShapeDtypeStruct
    once = lambda shape: pl.BlockSpec(shape, lambda i: (0,) * len(shape), pipeline_mode=pl.Buffered(1))
    by_cols = pl.BlockSpec((rows, span), lambda i: (0, i))
    extra = {"none": 0, "slot": more[0].shape[2] if kind == "slot" else 0, "gains": 16}[kind] if w.packed else 0
    if not w.packed:
        kind, more = "none", ()
    grads = w.grad_shapes(extra)
    return pl.pallas_call(
        functools.partial(ffn_bwd_kernel, gain[1], w, kind),
        grid=(steps,),
        in_specs=[once((rows, width)), once((rows, width)), by_cols, by_cols,
                  pl.BlockSpec((rows // steps, width), lambda i: (i, 0)), once(gain[0].shape),
                  pl.BlockSpec((1, width, span), lambda i: (i, 0, 0)), pl.BlockSpec((1, span, width), lambda i: (0, i, 0))]
        + [once(x.shape) for x in more] + [smem()] * len(w.place()),
        out_specs=[whole((rows, width)), whole((1, width))] + [whole(s.shape) for s in grads],
        out_shape=[sds((rows, width), F32), sds((1, width), F32)] + grads,
        scratch_shapes=[pltpu.VMEM((rows, width), BF16), pltpu.VMEM((width, rows), BF16), pltpu.VMEM((rows, width), F32),
                        pltpu.VMEM((rows, width), F32)] + w.grad_scratch(),
        compiler_params=PARAMS,
        cost_estimate=cost(16 * rows * width * inner, 25 << 20),
        name="ffn_bwd",
    )(dr, hidden, act, slope, r, gain[0], *plain, *more, *w.place())


def slot_kernel(gain, w, halo, *refs):
    n_grad = 2 if w.packed else 1
    (len_ref, place_ref, r_ref, g_ref, cot_ref), halo_refs, w_refs, (out_ref, dr_ref, dg_ref), send, dw_outs, w_scr, dw_scr = cut(
        refs, 5, 3 if halo else 0, w.n_args(), 3, n_grad - 1, n_grad, w.n_scratch(), w.n_scratch())
    length = len_ref[place_ref[3]]
    w_ref, = w.load(w_refs, w_scr, length >= 0)
    dw_ref, = dw_scr if w.packed else dw_outs
    rows, width = r_ref.shape
    gain = row_of(g_ref, gain)
    low = norm(r_ref[...], gain).astype(BF16)
    row = lax.broadcasted_iota(jnp.int32, (rows, width), 0)
    above = below = 0.0
    place = row
    if halo:
        base_ref, next_ref, prev_ref = halo_refs
        place = row + base_ref[0]
        after = norm(next_ref[...], gain).astype(BF16)
        above = nn(after, w_ref[0, width:, :])[:1, :] * base_ref[1].astype(F32)
        below = jnp.where(base_ref[0] - 1 < length - 1, prev_ref[...].astype(F32)[:1, :], 0.0)
    live = place < length - 1
    second = nn(low, w_ref[0, width:, :])
    shifted = jnp.where(row == rows - 1, above, pltpu.roll(second, rows - 1, 0))
    out_ref[...] = jnp.where(live, nn(low, w_ref[0, :width, :]) + shifted, 0.0).astype(BF16)
    if send:
        send[0][...] = other_half(place_ref, out_ref)
    g = jnp.where(live, cot_ref[...].astype(F32), 0.0)
    before = jnp.where(row == 0, below, pltpu.roll(g, 1, 0)).astype(BF16)
    g = g.astype(BF16)
    low_t = low.T
    dw_ref[0, :width, :] = nn(low_t, g).astype(BF16)
    dw_ref[0, width:, :] = nn(low_t, before).astype(BF16)
    dy = nt(g, w_ref[0, :width, :]) + nt(before, w_ref[0, width:, :])
    dr_ref[...], dg_ref[...] = norm_back(r_ref[...], gain, dy)
    w.store(w_refs[:1], [dw_ref], dw_outs, length >= 0)


def slot_step(length, r, gain, w, cot, halo):
    rows, width = r.shape
    sds = jax.ShapeDtypeStruct
    grads = w.grad_shapes()
    full = lambda x: pl.BlockSpec(x.shape, lambda i: (0,) * len(x.shape))
    outs = [sds((rows, width), BF16), sds((rows, width), F32), sds((1, width), F32)]
    outs += ([sds((rows // 2, width), BF16)] if w.packed else []) + grads
    return pl.pallas_call(
        functools.partial(slot_kernel, gain[1], w, len(halo) > 0),
        grid=(1,),
        in_specs=[smem(), smem()] + [full(x) for x in (r, gain[0], cot)] + [smem(), *map(full, halo[1:])][:len(halo)] + w.specs(1),
        out_specs=[full(x) for x in outs],
        out_shape=outs,
        scratch_shapes=w.scratch() + w.grad_scratch(),
        compiler_params=PARAMS,
        cost_estimate=cost(36 * rows * width * width, 9 << 20),
        name="slot",
    )(*length, r, gain[0], cot, *halo, *w.args())


def pack_kernel(lane_ref, gains_ref, *refs):
    *ins, first_ref, second_ref = refs
    pieces = []
    for ref in ins:
        if len(ref.shape) == 3:
            pieces += [ref[a] for a in range(ref.shape[0])]
        elif ref.shape[1] > first_ref.shape[1]:
            width = first_ref.shape[1]
            pieces += [ref[:, a * width:(a + 1) * width] for a in range(ref.shape[1] // width)]
        else:
            pieces.append(ref[...])
        if ref is ins[0]:
            count, share = gains_ref.shape
            row = lax.broadcasted_iota(jnp.int32, (share, first_ref.shape[1]), 0)
            lane = lax.broadcasted_iota(jnp.int32, (share, first_ref.shape[1]), 1)
            spread = jnp.where(lane == row + lane_ref[0], 1.0, 0.0).astype(BF16)
            gains = nn(gains_ref[...], spread).astype(BF16)
            pieces.append(jnp.concatenate([gains, jnp.zeros((16 - count, gains.shape[1]), BF16)], axis=0))
    at = 0
    dsts = [first_ref, second_ref]
    for piece in pieces:
        if at == dsts[0].shape[0]:
            at = 0
            dsts.pop(0)
        dst = dsts[0]
        dst[at:at + piece.shape[0], :] = piece
        at += piece.shape[0]


def pack(lane, gains, *groups):
    width = groups[0][0].shape[-1]
    rows = [sum(x.size for x in xs) // width for xs in groups]
    rows[0] += 16
    arrays = [x for xs in groups for x in xs]
    return pl.pallas_call(
        pack_kernel,
        in_specs=[smem()] + [vmem()] * (1 + len(arrays)),
        out_specs=[vmem() for _ in rows],
        out_shape=[jax.ShapeDtypeStruct((n, width), BF16) for n in rows],
        name="pack",
    )(lane, gains, *arrays)


def finish_kernel(shapes, terms, lane_ref, *refs):
    *ins, outs = cut(refs, *terms, len(refs) - sum(terms))
    at_out = 0
    for group, parts in zip(shapes, ins):
        total = summed([x[...] for x in parts])
        at = 0
        for stack, share in group:
            out = outs[at_out]
            width = total.shape[1]
            for a in range(stack):
                rows = total[at:at + share, :]
                at += share
                if len(out.shape) == 3:
                    out[a] = rows
                else:
                    out[:, a * width:(a + 1) * width] = rows
            at_out += 1
        if at < total.shape[0]:
            out = outs[at_out]
            count, share = out.shape
            row = lax.broadcasted_iota(jnp.int32, (width, share), 0)
            lane = lax.broadcasted_iota(jnp.int32, (width, share), 1)
            pick = jnp.where(row == lane + lane_ref[0], 1.0, 0.0).astype(BF16)
            out[...] = nn(total[at:, :].astype(BF16), pick)[:count, :]
            at_out += 1


def finish(lane, shapes, sums, more, outs):
    groups = [[x] for x in sums] + more
    arrays = [x for g in groups for x in g]
    return pl.pallas_call(
        functools.partial(finish_kernel, shapes, [len(g) for g in groups]),
        in_specs=[smem()] + [vmem()] * len(arrays),
        out_specs=[vmem() for _ in outs],
        out_shape=[jax.ShapeDtypeStruct(s, F32) for s in outs],
        name="finish",
    )(lane, *arrays)


def exchange(x, send, *during):
    count = x.shape[0]
    me = lax.axis_index("seq")
    out = x
    for k in range(1, count):
        piece = lax.dynamic_index_in_dim(x, (me + k) % count, 0, keepdims=False) if send is None else send
        piece = hold(lax.ppermute(piece, "seq", [(s, (s + k) % count) for s in range(count)]), *during)
        out = lax.dynamic_update_index_in_dim(out, piece, (me - k) % count, 0)
    return out


def to_examples(x, count):
    examples, rows, width = x.shape
    if count == examples:
        return exchange(x, None).reshape(count * rows, width)
    me = lax.axis_index("seq")
    group = count // examples
    all_rows = lax.all_gather(x, "seq", axis=1, tiled=True)
    one = lax.dynamic_index_in_dim(all_rows, me // group, 0, keepdims=False)
    return lax.dynamic_slice_in_dim(one, (me % group) * examples * rows, examples * rows, 0)


def to_positions(x, examples, count, *during, send=None):
    width = x.shape[1]
    if count == examples:
        return exchange(x.reshape(count, -1, width), send, *during)
    me = lax.axis_index("seq")
    rows = x.shape[0] // examples
    all_rows = lax.all_gather(x, "seq", axis=0, tiled=True).reshape(examples, count * rows, width)
    return lax.dynamic_slice_in_dim(all_rows, me * rows, rows, 1)


class Ring:
    def __init__(self):
        self.dp = lax.axis_size("dp")
        self.outer = self.dp // INNER
        self.columns = [[o * INNER + i for o in range(self.outer)] for i in range(INNER)]
        self.planes = [[o * INNER + i for i in range(INNER)] for o in range(self.outer)]

    def inner_step(self, x, j):
        return lax.ppermute(x, "dp", [(d, d // INNER * INNER + (d + j) % INNER) for d in range(self.dp)])

    def outer_step(self, x, k):
        return lax.ppermute(x, "dp", [(d, (d + k * INNER) % self.dp) for d in range(self.dp)])

    def swap(self, x):
        return lax.ppermute(x, "seq", [(0, 1), (1, 0)])

    def column(self, shard, *during):
        return [shard] + [hold(self.outer_step(shard, k), *during) for k in range(1, self.outer)]

    def plane(self, column, *during):
        return [column] + [hold(self.inner_step(column, j), *during) for j in range(1, INNER)]

    def far_column(self, x):
        return lax.all_gather(x, "dp", axis=0, axis_index_groups=self.columns)

    def both(self, plane):
        return plane + [self.swap(x) for x in plane]

    def pairs(self, keep, send, *during):
        other = hold(self.swap(send), *during)
        return [low(keep[j].astype(F32) + other[j].astype(F32)) for j in range(INNER)]

    def across(self, pairs, *during):
        return low(summed([pairs[0]] + [hold(self.inner_step(pairs[j], j), *during) for j in range(1, INNER)]))

    def pair(self, keep, send):
        return low(keep.astype(F32) + self.swap(send).astype(F32))

    def plane_sum(self, pair):
        return lax.psum_scatter(pair, "dp", scatter_dimension=0, axis_index_groups=self.planes)

    def far_sum(self, total):
        return lax.psum_scatter(total, "dp", scatter_dimension=0, axis_index_groups=self.columns)

    def near_sum(self, total):
        return [total[0]] + [self.outer_step(total[k], k) for k in range(1, self.outer)]


def low(x):
    return x.astype(BF16)


def summed(parts):
    return sum(x.astype(F32) for x in parts)


def hold(x, *after):
    return lax.optimization_barrier((x, after))[0]


def per_device(source, canvas, source_len, canvas_len, cotangent, enc_attn, enc_up, enc_down, dec_attn, cross_attn,
               dec_up, dec_down, slot_proj, norm_gains):
    examples, _, width = source.shape
    seq = lax.axis_size("seq")
    devices = lax.axis_size("dp") * seq
    group = seq // examples
    me = lax.axis_index("seq")
    rank = lax.axis_index("dp") * seq + me
    groups = [[e * group + t for t in range(group)] for e in range(examples)]
    packed = seq == SEQ and lax.axis_size("dp") % INNER == 0 and enc_up.shape[0] % 16 == 0

    def whole_keys(x):
        return lax.all_gather(x, "seq", axis=0, tiled=True, axis_index_groups=groups) if group > 1 else x

    def own_keys(x):
        if group == 1:
            return x
        return lax.psum_scatter(x, "seq", scatter_dimension=0, tiled=True, axis_index_groups=groups)

    def neighbour(x, step):
        pairs = [(s, s + step) for s in range(seq) if 0 <= s % group + step < group]
        return lax.ppermute(x, "seq", pairs)

    def chunks(up):
        rows = up.shape[0]
        return up.reshape(rows, -1, width).transpose(1, 0, 2)

    def unchunk(up):
        return up.transpose(1, 0, 2).reshape(up.shape[1], -1)

    shards = {
        "enc": enc_attn, "dec": dec_attn, "cross": cross_attn, "eup": chunks(enc_up), "edown": enc_down[None],
        "dup": chunks(dec_up), "ddown": dec_down[None], "slot": slot_proj[None],
    }
    shapes = {name: (x.shape[0], x.shape[1] * devices, width) for name, x in shards.items()}
    flat = lambda name: shards[name].reshape(-1, width)
    dp_index = lax.axis_index("dp")
    spot = jnp.stack([dp_index // INNER, dp_index % INNER, me, me // group]).astype(jnp.int32)
    if packed:
        ring = Ring()
        share = norm_gains.shape[1]
        lane = jnp.reshape(rank * share, (1,)).astype(jnp.int32)
        late, flat5 = pack(
            lane, norm_gains, [dec_attn, enc_up, enc_down, cross_attn, slot_proj], [dec_up, dec_down])
        names = ["eup", "edown", "cross", "slot", "dup", "ddown"]
        sizes = [shapes[n][0] * shapes[n][1] // devices for n in names[:4]]
        late = ring.far_column(late)
        x5 = ring.plane(flat5)
        z1 = jnp.stack(hold(ring.column(flat("enc")), *x5))
        g1 = ring.plane(z1)
        source, canvas, cotangent = hold((source, canvas, cotangent), z1)
        late = hold(late, *g1)
        x5 = ring.far_column(jnp.stack(hold(x5, *g1)))
        g1 = ring.both(g1)
        cuts = [shapes["dec"][0] * shapes["dec"][1] // devices + 16]
        cuts.append(cuts[0] + sum(sizes[:2]))
        late = [late[:, :cuts[0]], late[:, cuts[0]:cuts[1]], late[:, cuts[1]:]]

        def make(arrays, names, far=(1, 1), **more):
            return Weights(True, arrays, [shapes[n] for n in names], spot=spot, outer=ring.outer, far=far, **more)

        w_enc = make(g1, ["enc"], (0, 0))

        def fetch_dec(during):
            return make(ring.both(ring.plane(late[0], during)), ["dec"], (1, 0), tail=16)

        def fetch_effn(before, during):
            return make(ring.both(ring.plane(hold(late[1], before), during)), ["eup", "edown"])

        def fetch_cross_slot(before, during):
            arrays = ring.both(ring.plane(hold(late[2], before), during))
            return make(arrays, ["cross"]), make(arrays, ["slot"], (1, 2), at=sizes[2])

        def fetch_dffn(before, during):
            return make([x5, hold(ring.swap(hold(x5, before)), during)], ["dup", "ddown"], (1, 2), block=True)
    else:
        def fetch(*names):
            return Weights(False, [lax.all_gather(shards[n], ("dp", "seq"), axis=1, tiled=True) for n in names],
                           [shapes[n] for n in names])
        w_enc = fetch("enc")
        fetch_dec = lambda *t: fetch("dec")
        fetch_effn = lambda *t: fetch("eup", "edown")
        fetch_cross_slot = lambda *t: (fetch("cross"), fetch("slot"))
        fetch_dffn = lambda *t: fetch("dup", "ddown")
        gains = lax.all_gather(norm_gains, ("dp", "seq"), axis=1, tiled=True).astype(F32)
    s_len, c_len = (source_len, spot), (canvas_len, spot)
    src = to_examples(source, seq)
    can = to_examples(canvas, seq)
    cot = to_examples(cotangent, seq)
    src_all = whole_keys(src)
    can_all = whole_keys(can)
    q_a, k_a, v_a, o_a, x_a, r_a, p_enc = attn_forward(s_len, w_enc, xq=src, xk=src_all)
    w_dec = fetch_dec(r_a)
    can = hold(can, r_a)
    q_b, k_b, v_b, o_b, x_b, r_c, *tail, p_dec = attn_forward(c_len, w_dec, xq=can, xk=can if group == 1 else can_all)
    gains = tail[0] if packed else gains
    gain = [(gains, i) for i in range(5)]
    w_effn = fetch_effn(r_a, r_c)
    h_a, act_a, slope_a, r_b, *p_effn = ffn_forward(hold(r_a, r_c), gain[0], w_effn)
    w_cross, w_slot = fetch_cross_slot(r_c, r_b)
    low_one, low_enc, q_c, k_c, v_c, o_c, x_c, r_d, p_cross = attn_forward(
        s_len, w_cross, rq=r_c, rk=whole_keys(r_b), gq=gain[2], gk=gain[1])
    w_dffn = fetch_dffn(r_b, r_d)
    h_b, act_b, slope_b, r_e, *p_dffn = ffn_forward(r_d, gain[3], w_dffn)
    halo = []
    if group > 1:
        place = jnp.stack([me % group * src.shape[0], me % group < group - 1]).astype(jnp.int32)
        halo = [place, neighbour(r_e[:8], -1), neighbour(cot[-8:][::-1], 1)]
    slot_out, dr, dg4, *d_slot = slot_step(c_len, r_e, gain[4], w_slot, cot, halo)
    slot_send = d_slot.pop(0) if packed else None
    dr, dg3, *d_dffn = ffn_backward(dr, h_b, act_b, slope_b, w_dffn, p_dffn, r_d, gain[3], "slot", d_slot)
    slot_out = to_positions(slot_out, examples, seq, send=slot_send)
    if packed:
        p1 = ring.pair(*d_dffn)
        dr = hold(dr, p1)
    alone = group == 1
    norms = [(r_c, gain[2])] + ([(r_b, gain[1])] if alone else [])
    dr_c, dr_b, dg2, *rest = attn_backward(
        False, s_len, dr, w_cross, p_cross, q_c, k_c, v_c, o_c, x_c, (low_one, low_enc), norms)
    if alone:
        dg1, *d_cross = rest
    else:
        d_cross = rest
        dr_b, dg1 = norm_back(r_b, gains[1:2], own_keys(dr_b))
    if packed:
        s1 = ring.plane_sum(p1)
        dr_b = hold(dr_b, slot_out)
    dr_a, dg0, *d_effn = ffn_backward(
        dr_b, h_a, act_a, slope_a, w_effn, p_effn, r_a, gain[0], "gains", [dg1, dg2, dg3, dg4])
    if packed:
        p2 = ring.pairs(*d_cross, dr_a)
        p3 = ring.pairs(*hold(tuple(d_effn), *p2))
        dr_c = hold(dr_c, *p3)
        z1 = ring.far_sum(s1)
    sides = 1 if alone else 2
    out = attn_backward(alone, c_len, dr_c, w_dec, p_dec, q_b, k_b, v_b, o_b, x_b, [can, can_all][:sides])
    d_can, d_dec = out[:sides], list(out[sides:])
    can_send = d_dec.pop(0) if packed else None
    canvas_grad = d_can[0] if alone else d_can[0] + own_keys(d_can[1])
    if packed:
        s2 = ring.across(p2, canvas_grad)
        s3 = ring.across(p3, canvas_grad)
        p4 = ring.pairs(*hold(tuple(d_dec), s2, s3, z1))
        dr_a = hold(dr_a, *p4)
        z23 = ring.far_sum(jnp.concatenate([s2, s3], axis=1))
        grads, *d_enc = attn_grads(s_len, dr_a, w_enc, p_enc, q_a, k_a, v_a, o_a, x_a, src)
        canvas_grad = to_positions(canvas_grad, examples, seq, grads, send=can_send)
        s4 = ring.across(p4, grads)
        d_enc = hold(tuple(d_enc), s4, z23)
        source_grad, source_send = input_grad(spot, dr_a, grads, p_enc)
        z4 = ring.near_sum(s4)
        p5 = ring.pairs(*d_enc, source_grad, *z4[1:])
        source_grad = to_positions(source_grad, examples, seq, send=hold(source_send, *p5))
        s5 = ring.across(p5, source_grad, canvas_grad)
        z5 = ring.near_sum(s5)
        groups = [("dup", "ddown", "slot"), ("cross", "eup", "edown"), ("dec",), ("enc",)]
        rows_of = [[(shards[n].shape[0], shards[n].shape[1]) for n in names] for names in groups]
        like = {"enc": enc_attn, "eup": enc_up, "edown": enc_down, "dec": dec_attn, "cross": cross_attn, "dup": dec_up,
                "ddown": dec_down, "slot": slot_proj}
        outs = [like[n].shape for n in groups[0] + groups[1]] + [norm_gains.shape, dec_attn.shape, enc_attn.shape]
        t_dup, t_ddown, t_slot, t_cross, t_eup, t_edown, t_gains, t_dec, t_enc = finish(
            lane, rows_of, [z1, z23], [z4, z5], outs)
    else:
        def home(x):
            return lax.psum_scatter(x, ("dp", "seq"), scatter_dimension=1, tiled=True).astype(F32)
        t_dec, t_cross = home(d_dec[0]), home(d_cross[0])
        t_eup, t_edown, t_dup, t_ddown, t_slot = (home(x) for x in (*d_effn, *d_dffn, *d_slot))
        t_eup, t_edown, t_dup, t_ddown, t_slot = unchunk(t_eup), t_edown[0], unchunk(t_dup), t_ddown[0], t_slot[0]
        out = attn_backward(alone, s_len, dr_a, w_enc, p_enc, q_a, k_a, v_a, o_a, x_a, [src, src_all][:sides])
        d_src, d_enc = out[:sides], out[sides:]
        source_grad = d_src[0] if alone else d_src[0] + own_keys(d_src[1])
        t_enc = home(d_enc[0])
        t_gains = home(jnp.concatenate([dg0, dg1, dg2, dg3, dg4], axis=0))
        source_grad = to_positions(source_grad, examples, seq)
        canvas_grad = to_positions(canvas_grad, examples, seq)

    return (
        slot_out, source_grad, canvas_grad,
        t_enc, t_eup, t_edown, t_dec, t_cross, t_dup, t_ddown, t_slot, t_gains,
    )


def solution(mesh):
    by_seq = P("dp", "seq", None)
    stack = P(None, ("dp", "seq"), None)
    by_row = P(("dp", "seq"), None)
    gains = P(None, ("dp", "seq"))
    in_specs = (by_seq, by_seq, P("dp"), P("dp"), by_seq, stack, by_row, by_row, stack, stack, by_row, by_row, by_row,
                gains)
    out_specs = (by_seq, by_seq, by_seq, stack, by_row, by_row, stack, stack, by_row, by_row, by_row, gains)
    return jax.shard_map(per_device, mesh=mesh, in_specs=in_specs, out_specs=out_specs, check_vma=False)
```

```python
import functools
import math

import jax
import jax.numpy as jnp
from jax import lax
from jax.experimental import pallas as pl
from jax.experimental.pallas import tpu as pltpu
from jax.sharding import PartitionSpec as P

F32 = jnp.float32
BF16 = jnp.bfloat16
H = 8
HD = 64
PAIR = 2 * HD
LOG2E = math.log2(math.e)
Q_SCALE = LOG2E / 8.0
K_BACK = 1.0 / LOG2E
MASKED = -1e30
VMEM_LIMIT = 58 * 1024 * 1024
PARAMS = pltpu.CompilerParams(vmem_limit_bytes=VMEM_LIMIT)


def nn(a, b):
    return lax.dot_general(a, b, (((1,), (0,)), ((), ())), preferred_element_type=F32)


def nt(a, b):
    return lax.dot_general(a, b, (((1,), (1,)), ((), ())), preferred_element_type=F32)


def tn(a, b):
    return lax.dot_general(a, b, (((0,), (0,)), ((), ())), preferred_element_type=F32)


def norm_parts(r):
    centre = r - jnp.mean(r, axis=-1, keepdims=True)
    rs = lax.rsqrt(jnp.mean(centre * centre, axis=-1, keepdims=True) + 1e-5)
    return centre * rs, rs


def norm(r, gain):
    return norm_parts(r)[0] * gain


def norm_back(r, gain, dy):
    z, rs = norm_parts(r)
    t = dy * gain
    dr = (t - jnp.mean(t, axis=-1, keepdims=True) - z * jnp.mean(t * z, axis=-1, keepdims=True)) * rs
    return dr, jnp.sum(dy * z, axis=0, keepdims=True)


def lanes(rows):
    return lax.broadcasted_iota(jnp.int32, (rows, PAIR), 1)


def key_extras(length, count):
    row = lax.broadcasted_iota(jnp.int32, (count, PAIR), 0)
    lane = lanes(count)
    bias = jnp.where(row < length, 0.0, MASKED)
    return jnp.where(lane == 3, bias, jnp.where(lane < 3, 1.0, 0.0)).astype(BF16)


def three_parts(v):
    hi = v.astype(BF16)
    rest = v - hi.astype(F32)
    mid = rest.astype(BF16)
    low = rest - mid.astype(F32)
    return hi.astype(F32), mid.astype(F32), low


def spread_parts(v, last):
    lane = lanes(v.shape[0])
    hi, mid, low = three_parts(v)
    tail = jnp.where(lane == 3, last, 0.0)
    return jnp.where(lane == 0, hi, jnp.where(lane == 1, mid, jnp.where(lane == 2, low, tail))).astype(BF16)


def row_of(ref, row):
    return ref[row:row + 1, :]


def whole(shape):
    return pl.BlockSpec(shape, lambda i: (0,) * len(shape))


def smem():
    return pl.BlockSpec(memory_space=pltpu.SMEM)


def vmem():
    return pl.BlockSpec(memory_space=pltpu.VMEM)


def cost(flops, nbytes, exps=0):
    return pl.CostEstimate(flops=int(flops), bytes_accessed=int(nbytes), transcendentals=int(exps))


INNER = 4
SEQ = 2


class Spot:
    def __init__(self, ref, outer, far):
        self.outer, self.far = outer, far
        self.o, self.i, self.s = ref[0], ref[1], ref[2]

    def owner(self, c, j, k):
        o = k if self.far else lax.rem(self.o - k + self.outer, self.outer)
        i = j if self.far > 1 else lax.rem(self.i - j + INNER, INNER)
        return (o * INNER + i) * SEQ + lax.rem(self.s - c + SEQ, SEQ)

    def ahead(self, o, i):
        return (i if self.far > 1 else lax.rem(i - self.i + INNER, INNER),
                o if self.far else lax.rem(o - self.o + self.outer, self.outer))


def assemble(spot, refs, at, dst, block):
    stack, total, _ = dst.shape
    share = total // (spot.outer * INNER * SEQ)
    for c in range(SEQ):
        for j in range(INNER):
            for k in range(spot.outer):
                ref, x = (refs[c], (k, j)) if block else (refs[c * INNER + j], (k,))
                rows = pl.ds(pl.multiple_of(spot.owner(c, j, k) * share, share), share)
                for a in range(stack):
                    dst[a, rows, :] = ref[(*x, slice(at + a * share, at + (a + 1) * share))]


def deal(spot, src, at, keep, send):
    stack, total, _ = src.shape
    share = total // (spot.outer * INNER * SEQ)
    for core in range(SEQ):
        @pl.when(spot.s == core)
        def _():
            for o in range(spot.outer):
                for i in range(INNER):
                    j, k = spot.ahead(o, i)
                    for s in range(SEQ):
                        first = ((o * INNER + i) * SEQ + s) * share
                        dst = keep if s == core else send
                        for a in range(stack):
                            dst[j, k, at + a * share:at + (a + 1) * share, :] = src[a, first:first + share, :]


class Weights:
    def __init__(self, packed, arrays, shapes, at=0, spot=None, outer=0, far=(0, 0), block=False, tail=0):
        self.packed, self.arrays, self.shapes, self.at, self.spot, self.outer = packed, arrays, shapes, at, spot, outer
        self.far, self.block, self.tail = far, block, tail

    def share(self, shape):
        return shape[0] * shape[1] // (self.outer * INNER * SEQ)

    def args(self):
        return [self.spot, *self.arrays] if self.packed else list(self.arrays)

    def specs(self, dims):
        zero = lambda n: (lambda *_: (0,) * n)
        if not self.packed:
            return [pl.BlockSpec(x.shape, zero(3), pipeline_mode=pl.Buffered(1)) if dims else vmem() for x in self.arrays]
        if not dims:
            return [smem()] + [vmem() for _ in self.arrays]
        rows = sum(self.share(s) for s in self.shapes) + self.tail
        index = self.at // rows
        lead = (self.outer, INNER) if self.block else (self.outer,)
        spec = lambda: pl.BlockSpec((*lead, rows, self.shapes[0][2]), lambda *_: (*(0 for _ in lead), index, 0),
                                    **(dict(pipeline_mode=pl.Buffered(1)) if dims else {}))
        return [smem()] + [spec() for _ in self.arrays]

    def scratch(self):
        return [pltpu.VMEM(s, BF16) for s in self.shapes] if self.packed else []

    def n_args(self):
        return len(self.arrays) + 1 if self.packed else len(self.arrays)

    def n_scratch(self):
        return len(self.shapes) if self.packed else 0

    def load(self, refs, scratch, first, entire=False):
        if not self.packed:
            return list(refs)

        @pl.when(first)
        def _():
            spot = Spot(refs[0], self.outer, self.far[0])
            at = self.at if entire else 0
            for shape, dst in zip(self.shapes, scratch):
                assemble(spot, refs[1:], at, dst, self.block)
                at += self.share(shape)
        return list(scratch)

    def plain_shapes(self):
        return [jax.ShapeDtypeStruct(s, BF16) for s in self.shapes] if self.packed else []

    def plain_blocks(self, steps):
        blocks = []
        for a, m, width in self.shapes if self.packed else []:
            if a % steps == 0:
                blocks.append(((a // steps, m, width), 0))
            else:
                assert m % steps == 0
                blocks.append(((a, m // steps, width), 1))
        return blocks

    def plain_specs(self, steps):
        first, second = (lambda i: (i, 0, 0)), (lambda i: (0, i, 0))
        return [pl.BlockSpec(b, second if dim else first) for b, dim in self.plain_blocks(steps)]

    def plain_store(self, outs, scratch, steps):
        i = pl.program_id(0)
        for out, src, (block, dim) in zip(outs, scratch, self.plain_blocks(steps)):
            n = block[dim]
            part = pl.ds(pl.multiple_of(i * n, n), n)
            out[...] = src[:, part, :] if dim else src[part]

    def grad_shapes(self, extra=0):
        if not self.packed:
            return [jax.ShapeDtypeStruct(s, BF16) for s in self.shapes]
        rows = sum(self.share(s) for s in self.shapes) + extra
        return [jax.ShapeDtypeStruct((INNER, self.outer, rows, self.shapes[0][2]), BF16)] * SEQ

    def grad_scratch(self):
        return [pltpu.VMEM(s, BF16) for s in self.shapes] if self.packed else []

    def place(self):
        return [self.spot] if self.packed else []

    def store(self, place, grads, outs, last):
        if not self.packed:
            return

        @pl.when(last)
        def _():
            spot = Spot(place[0], self.outer, self.far[1])
            at = 0
            for shape, src in zip(self.shapes, grads):
                deal(spot, src, at, *outs)
                at += self.share(shape)


def other_half(place_ref, ref):
    half = ref.shape[0] // 2
    return ref[pl.ds(pl.multiple_of((1 - place_ref[2]) * half, half), half), :]


def join(place_ref, own_ref, other_ref, dst):
    half = other_ref.shape[0]
    me = place_ref[2]
    dst[pl.ds(pl.multiple_of(me * half, half), half), :] = own_ref[me]
    dst[pl.ds(pl.multiple_of((1 - me) * half, half), half), :] = other_ref[...]


def cut(refs, *counts):
    out, at = [], 0
    for n in counts:
        out.append(refs[at:at + n])
        at += n
    assert at == len(refs)
    return out


def attn_fwd_kernel(cross, joined, gq, gk, steps, w, *refs):
    n_in, n_out = (5, 8) if cross else (4, 7 if joined else 6)
    n_tail = 1 if w.tail else 0
    ins, w_refs, outs, tail, plain, (kaug, vaug), xk_s, w_scr = cut(
        refs, n_in, w.n_args(), n_out, n_tail, w.n_scratch(), 2, 1 if cross else 0, w.n_scratch())
    count = kaug.shape[1]
    i = pl.program_id(0)
    start = i == 0
    w_ref, = w.load(w_refs, w_scr, start)
    if cross:
        len_ref, place_ref, rq_ref, rk_ref, g_ref = ins
        xq_ref, xk_ref, q_ref, k_ref, v_ref, o_ref, qx_ref, r_ref = outs
    else:
        len_ref, place_ref, xq_ref, xk_ref = ins
        if joined:
            own_ref, other_ref = xq_ref, xk_ref
            xk_ref, *outs = outs
        q_ref, k_ref, v_ref, o_ref, qx_ref, r_ref = outs
    rows = r_ref.shape[0]

    @pl.when(start)
    def _():
        if w.tail:
            parts = [x[k, w.share(w.shapes[0]):, :].astype(F32) for x in w_refs[1:] for k in range(w.outer)]
            tail[0][...] = sum(parts[1:], parts[0])
        if cross:
            xk = norm(rk_ref[...], row_of(g_ref, gk)).astype(BF16)
            xk_s[0][...] = xk
        else:
            if joined:
                join(place_ref, own_ref, other_ref, xk_ref)
            xk = xk_ref[...]
        k = nn(xk, w_ref[1]).astype(BF16)
        v = nn(xk, w_ref[2]).astype(BF16)
        extras = key_extras(len_ref[place_ref[3]], count)
        ones = jnp.ones((count, PAIR), BF16)
        for p in range(H // 2):
            kaug[p, :, :PAIR] = k[:, p * PAIR:(p + 1) * PAIR]
            kaug[p, :, PAIR:] = extras
            vaug[p, :, :PAIR] = v[:, p * PAIR:(p + 1) * PAIR]
            vaug[p, :, PAIR:] = ones
        k_ref[...] = k
        v_ref[...] = v

    w.plain_store(plain, w_scr, steps)
    if cross:
        xk_ref[...] = xk_s[0][pl.ds(pl.multiple_of(i * (count // steps), count // steps), count // steps), :]
        resid = norm(rq_ref[...], row_of(g_ref, gq))
        xq = resid.astype(BF16)
        xq_ref[...] = xq
    else:
        xq = xk_ref[pl.ds(pl.multiple_of(i * rows, rows), rows), :] if joined else xq_ref[...]
        resid = xq.astype(F32)
    q = nn(xq, w_ref[0]) * Q_SCALE
    q_ref[...] = q.astype(BF16)
    lane = lanes(rows)
    first = lane < HD
    extra = jnp.where(lane == 3, 1.0, 0.0).astype(BF16)

    def score(h):
        p = h // 2
        mine = first if h % 2 == 0 else lane >= HD
        qm = jnp.where(mine, q[:, p * PAIR:(p + 1) * PAIR], 0.0).astype(BF16)
        return nt(jnp.concatenate([qm, extra], axis=1), kaug[p])

    halves = []
    ahead = score(0)
    for h in range(H):
        s = ahead
        if h + 1 < H:
            ahead = score(h + 1)
        m = jnp.max(s, axis=1, keepdims=True)
        o = nn(jnp.exp2(s - m).astype(BF16), vaug[h // 2])
        total = o[:, PAIR:]
        halves.append(o[:, :PAIR] / total)
        qx_ref[h] = spread_parts(-(m + jnp.log2(total)), 1.0)
    blended = [jnp.where(first, halves[2 * p], halves[2 * p + 1]).astype(BF16) for p in range(H // 2)]
    o_all = jnp.concatenate(blended, axis=1)
    o_ref[...] = o_all
    r_ref[...] = resid + nn(o_all, w_ref[3])


def attn_forward(length, w, xq=None, xk=None, rq=None, rk=None, gq=None, gk=None, halves=None):
    cross, joined = rq is not None, halves is not None
    if joined:
        rows, width = 2 * halves[1].shape[0], halves[1].shape[1]
        count = rows
    else:
        rows, width = (rq if cross else xq).shape
        count = (rk if cross else xk).shape[0]
    blk = math.gcd(rows, 512)
    steps = rows // blk
    sds = jax.ShapeDtypeStruct
    by_rows = pl.BlockSpec((blk, width), lambda i: (i, 0))
    by_keys = pl.BlockSpec((count // steps, width), lambda i: (i, 0))
    outs = [
        sds((rows, width), BF16), sds((count, width), BF16), sds((count, width), BF16),
        sds((rows, width), BF16), sds((H, rows, PAIR), BF16), sds((rows, width), F32),
    ]
    out_specs = [by_rows, whole((count, width)), whole((count, width)), by_rows, pl.BlockSpec((H, blk, PAIR), lambda i: (0, i, 0)), by_rows]
    if cross:
        args = [*length, rq, rk, gq[0]]
        in_specs = [smem(), smem(), by_rows, whole((count, width)), whole(gq[0].shape)]
        outs = [sds((rows, width), BF16), sds((count, width), BF16)] + outs
        out_specs = [by_rows, by_keys] + out_specs
    elif joined:
        args = [*length, *halves]
        in_specs = [smem(), smem(), *(whole(x.shape) for x in halves)]
        outs = [sds((rows, width), BF16)] + outs
        out_specs = [whole((rows, width))] + out_specs
    else:
        args = [*length, xq, xk]
        in_specs = [smem(), smem(), by_rows, whole((count, width))]
    if w.tail:
        outs.append(sds((w.tail, width), F32))
        out_specs.append(whole((w.tail, width)))
    out = pl.pallas_call(
        functools.partial(attn_fwd_kernel, cross, joined, *((gq[1], gk[1]) if cross else (0, 0)), steps, w),
        grid=(steps,),
        in_specs=in_specs + w.specs(1),
        out_specs=out_specs + w.plain_specs(steps),
        out_shape=outs + w.plain_shapes(),
        scratch_shapes=[pltpu.VMEM((H // 2, count, 2 * PAIR), BF16)] * 2
        + ([pltpu.VMEM((count, width), BF16)] if cross else []) + w.scratch(),
        compiler_params=PARAMS,
        cost_estimate=cost(rows * count * 5 * 512 * H, 14 << 20, rows * count * H),
        name="cross_fwd" if cross else "self_fwd",
    )(*args, *w.args())
    return out if w.packed else [*out, *w.arrays]


def pair_back(k_ref, v_ref, q_ref, qx_ref, o, do, kaug, vaug, qaug, oaug, kt, dqt):
    count, rows = kaug.shape[0], o.shape[0]
    blk = math.gcd(count, 512)
    kaug[:, :PAIR] = k_ref[...]
    vaug[:, :PAIR] = v_ref[...]
    kt[...] = k_ref[...].T
    lane = lanes(rows)
    inner = -(o.astype(F32) * do.astype(F32))
    high = inner.astype(BF16).astype(F32)
    rest = pltpu.roll(inner - high, HD, 1)
    q, do = q_ref[...].astype(F32), do.astype(F32)
    for h in range(2):
        mine = lane < HD if h == 0 else lane >= HD
        qaug[h, :, :PAIR] = jnp.where(mine, q, 0.0).astype(BF16)
        qaug[h, :, PAIR:] = qx_ref[h]
        oaug[h, :, :PAIR] = jnp.where(mine, do, 0.0).astype(BF16)
        oaug[h, :, PAIR:] = jnp.where(mine, high, rest).astype(BF16)
    for j in range(count // blk):
        keys = slice(j * blk, (j + 1) * blk)
        dv_sum = dk_sum = None
        for h in range(2):
            pt = jnp.exp2(nt(kaug[keys, :], qaug[h]))
            dpt = nt(vaug[keys, :], oaug[h])
            ptb = pt.astype(BF16)
            dst = (pt * dpt).astype(BF16)
            dv_h = nn(ptb, oaug[h, :, :PAIR])
            dk_h = nn(dst, qaug[h, :, :PAIR])
            dq_h = nn(kt[h * HD:(h + 1) * HD, keys], dst)
            dv_sum = dv_h if h == 0 else dv_sum + dv_h
            dk_sum = dk_h if h == 0 else dk_sum + dk_h
            if j == 0:
                dqt[h * HD:(h + 1) * HD, :] = dq_h
            else:
                dqt[h * HD:(h + 1) * HD, :] += dq_h
        yield keys, (dk_sum * K_BACK).astype(BF16), dv_sum.astype(BF16)


def attn_bwd_kernel(gains, same, w, *refs):
    norms = len(gains)
    n_out = 1 if same else 2
    n_dg = 0 if same else norms
    n_send = 1 if same and w.packed else 0
    n_grad = 2 if w.packed else 1
    (len_ref, place_ref, dr_ref, w3_ref, w_ref, q_ref, k_ref, v_ref, o_ref, qx_ref), x_refs, n_refs, place, outs, send, dg_refs, dw_outs, \
        (dab, do_s, kaug, vaug, qaug, oaug, kt, ot, dqt, grads_q, grads_k, w_all), xts, dw_scr = cut(
            refs, 10, n_out, 2 * norms, len(w.place()), n_out, n_send, n_dg, n_grad, 12, n_out, w.n_scratch())
    dw_ref, = dw_scr if w.packed else dw_outs
    count = kaug.shape[0]
    rows, width = dab.shape
    p = pl.program_id(0)

    @pl.when(p == 0)
    def _():
        dab[...] = dr_ref[...].astype(BF16)
        kaug[:, PAIR:] = key_extras(len_ref[place_ref[3]], count)
        vaug[:, PAIR:] = jnp.ones((count, PAIR), BF16)
        do = nt(dab[...], w3_ref[0]).astype(BF16)
        for n in range(H // 2):
            do_s[n] = do[:, n * PAIR:(n + 1) * PAIR]

    @pl.when(p < 3)
    def _():
        w_all[:, pl.ds(pl.multiple_of(p * width, PAIR), width)] = w_ref[0]

    own = pl.ds(pl.multiple_of(p * PAIR, PAIR), PAIR)
    behind = pl.ds(pl.multiple_of(width + p * PAIR, PAIR), PAIR)
    o, do = o_ref[...], do_s[p]
    ot[own, :] = o.T
    for x, xt in zip(x_refs, xts):
        xt[own, :] = x[...].T
    for keys, dk, dv in pair_back(k_ref, v_ref, q_ref, qx_ref, o, do, kaug, vaug, qaug, oaug, kt, dqt):
        grads_k[keys, own] = dk
        grads_k[keys, behind] = dv
    grads_q[:, own] = (dqt[...].T * 0.125).astype(BF16)
    last = p == pl.num_programs(0) - 1

    @pl.when(last)
    def _():
        dw_ref[0] = nn(xts[0][...], grads_q[...]).astype(BF16)
        both = nn(xts[-1][...], grads_k[...]).astype(BF16)
        dw_ref[1] = both[:, :width]
        dw_ref[2] = both[:, width:]
        dw_ref[3] = nn(ot[...], dab[...]).astype(BF16)
        dxq = dr_ref[...] + nt(grads_q[...], w_all[:, :width])
        dxk = nt(grads_k[...], w_all[:, width:])
        if same:
            outs[0][...] = dxq + dxk
            if n_send:
                send[0][...] = other_half(place_ref, outs[0])
        else:
            for n, value in enumerate((dxq, dxk)):
                if n < norms:
                    gain = row_of(n_refs[2 * n + 1], gains[n])
                    value, dg_refs[n][...] = norm_back(n_refs[2 * n][...], gain, value)
                outs[n][...] = value

    w.store(place, [dw_ref], dw_outs, last)


def attn_backward(same, length, dr, w, plain, q, k, v, o, qx, xs, norms=()):
    rows, width = dr.shape
    count = k.shape[0]
    sds = jax.ShapeDtypeStruct
    pair_of = lambda n: pl.BlockSpec((n, PAIR), lambda i: (0, i))
    once = lambda shape, index=None: pl.BlockSpec(
        shape, lambda i: index or (0,) * len(shape), pipeline_mode=pl.Buffered(1))
    in_specs = [
        smem(), smem(), once((rows, width)), once((1, width, width), (3, 0, 0)),
        pl.BlockSpec((1, width, width), lambda i: (jnp.minimum(i, 2), 0, 0)),
        pair_of(rows), pair_of(count), pair_of(count), pair_of(rows),
        pl.BlockSpec((2, rows, PAIR), lambda i: (i, 0, 0)),
    ] + [pair_of(x.shape[0]) for x in xs]
    norm_args = []
    for r, g in norms:
        norm_args += [r, g[0]]
        in_specs += [once(r.shape), once(g[0].shape)]
    outs = [sds((rows, width), F32)]
    if not same:
        outs += [sds((count, width), F32)] + [sds((1, width), F32)] * len(norms)
    elif w.packed:
        outs.append(sds((rows // 2, width), F32))
    outs += w.grad_shapes()
    vm = pltpu.VMEM
    return pl.pallas_call(
        functools.partial(attn_bwd_kernel, [g[1] for _, g in norms], same, w),
        grid=(H // 2,),
        in_specs=in_specs + [smem()] * len(w.place()),
        out_specs=[whole(s.shape) for s in outs],
        out_shape=outs,
        scratch_shapes=[
            vm((rows, width), BF16), vm((H // 2, rows, PAIR), BF16),
            vm((count, 2 * PAIR), BF16), vm((count, 2 * PAIR), BF16),
            vm((2, rows, 2 * PAIR), BF16), vm((2, rows, 2 * PAIR), BF16), vm((PAIR, count), BF16), vm((width, rows), BF16),
            vm((PAIR, rows), F32), vm((rows, width), BF16), vm((count, 2 * width), BF16), vm((width, 3 * width), BF16),
        ] + [vm((width, x.shape[0]), BF16) for x in xs] + w.grad_scratch(),
        compiler_params=PARAMS,
        cost_estimate=cost(rows * count * 9 * 512 * H, 20 << 20, rows * count * H),
        name="self_bwd" if same else "cross_bwd",
    )(*length, dr, plain, plain, q, k, v, o, qx, *xs, *norm_args, *w.place())


def attn_grads_kernel(w, len_ref, place_ref, dr_ref, w3_ref, q_ref, k_ref, v_ref, o_ref, qx_ref, x_ref, grads_ref, *refs):
    dw_outs, (dab, do_s, kaug, vaug, qaug, oaug, kt, ot, xt, dqt), (dw_ref,) = cut(refs, 2, 10, 1)
    count = kaug.shape[0]
    width = dab.shape[1]
    p = pl.program_id(0)

    @pl.when(p == 0)
    def _():
        dab[...] = dr_ref[...].astype(BF16)
        kaug[:, PAIR:] = key_extras(len_ref[place_ref[3]], count)
        vaug[:, PAIR:] = jnp.ones((count, PAIR), BF16)
        do = nt(dab[...], w3_ref[0]).astype(BF16)
        for n in range(H // 2):
            do_s[n] = do[:, n * PAIR:(n + 1) * PAIR]

    own = pl.ds(pl.multiple_of(p * PAIR, PAIR), PAIR)
    part = lambda n: pl.ds(pl.multiple_of(n * width + p * PAIR, PAIR), PAIR)
    o, do = o_ref[...], do_s[p]
    ot[own, :] = o.T
    xt[own, :] = x_ref[...].T
    for keys, dk, dv in pair_back(k_ref, v_ref, q_ref, qx_ref, o, do, kaug, vaug, qaug, oaug, kt, dqt):
        grads_ref[keys, part(1)] = dk
        grads_ref[keys, part(2)] = dv
    grads_ref[:, part(0)] = (dqt[...].T * 0.125).astype(BF16)
    last = p == pl.num_programs(0) - 1

    @pl.when(last)
    def _():
        dw = nn(xt[...], grads_ref[...]).astype(BF16)
        for n in range(3):
            dw_ref[n] = dw[:, n * width:(n + 1) * width]
        dw_ref[3] = nn(ot[...], dab[...]).astype(BF16)

    w.store([place_ref], [dw_ref], dw_outs, last)


def attn_grads(length, dr, w, plain, q, k, v, o, qx, x):
    rows, width = dr.shape
    sds = jax.ShapeDtypeStruct
    vm = pltpu.VMEM
    once = lambda shape, index=None: pl.BlockSpec(
        shape, lambda i: index or (0,) * len(shape), pipeline_mode=pl.Buffered(1))
    pair = pl.BlockSpec((rows, PAIR), lambda i: (0, i))
    outs = [sds((rows, 3 * width), BF16)] + w.grad_shapes()
    return pl.pallas_call(
        functools.partial(attn_grads_kernel, w),
        grid=(H // 2,),
        in_specs=[smem(), smem(), once((rows, width)), once((1, width, width), (3, 0, 0))] + [pair] * 4
        + [pl.BlockSpec((2, rows, PAIR), lambda i: (i, 0, 0)), pair],
        out_specs=[whole(x.shape) for x in outs],
        out_shape=outs,
        scratch_shapes=[
            vm((rows, width), BF16), vm((H // 2, rows, PAIR), BF16), vm((rows, 2 * PAIR), BF16), vm((rows, 2 * PAIR), BF16),
            vm((2, rows, 2 * PAIR), BF16), vm((2, rows, 2 * PAIR), BF16), vm((PAIR, rows), BF16), vm((width, rows), BF16),
            vm((width, rows), BF16), vm((PAIR, rows), F32),
        ] + w.grad_scratch(),
        compiler_params=PARAMS,
        cost_estimate=cost(rows * rows * 9 * 512 * H, 14 << 20, rows * rows * H),
        name="grads_bwd",
    )(*length, dr, plain, q, k, v, o, qx, x)


def input_grad_kernel(place_ref, dr_ref, grads_ref, *refs):
    *w_refs, out_ref, send_ref = refs
    out_ref[...] = dr_ref[...] + nt(grads_ref[...], jnp.concatenate([w[0] for w in w_refs], axis=1))

    @pl.when(pl.program_id(0) != place_ref[2])
    def _():
        send_ref[...] = out_ref[...]


def input_grad(place, dr, grads, plain):
    rows, width = dr.shape
    blk = rows // SEQ
    by_rows = lambda x: pl.BlockSpec((blk, x.shape[1]), lambda i: (i, 0))
    matrix = lambda n: pl.BlockSpec((1, width, width), lambda i: (n, 0, 0))
    return pl.pallas_call(
        input_grad_kernel,
        grid=(rows // blk,),
        in_specs=[smem(), by_rows(dr), by_rows(grads)] + [matrix(n) for n in range(3)],
        out_specs=[by_rows(dr), whole((blk, width))],
        out_shape=[jax.ShapeDtypeStruct(dr.shape, F32), jax.ShapeDtypeStruct((blk, width), F32)],
        compiler_params=PARAMS,
        cost_estimate=cost(6 * rows * width * width, 9 << 20),
        name="input_grad",
    )(place, dr, grads, plain, plain, plain)


def gelu_parts(u):
    phi = 0.5 + 0.5 * lax.erf(u * math.sqrt(0.5))
    return u * phi, phi + u * jnp.exp2(u * u * (-0.5 * LOG2E)) * (1.0 / math.sqrt(2.0 * math.pi))


def ffn_fwd_kernel(gain, steps, w, *refs):
    (r_ref, g_ref), w_refs, (h_ref, a_ref, d_ref, out_ref), plain, w_scr = cut(
        refs, 2, w.n_args(), 4, w.n_scratch(), w.n_scratch())
    up_ref, down_ref = w.load(w_refs, w_scr, pl.program_id(0) == 0)
    w.plain_store(plain, w_scr, steps)
    hidden = norm(r_ref[...], row_of(g_ref, gain))
    low = hidden.astype(BF16)
    h_ref[...] = low
    total = hidden
    span = up_ref.shape[2]
    for c in range(up_ref.shape[0]):
        cols = slice(c * span, (c + 1) * span)
        act, slope = gelu_parts(nn(low, up_ref[c]))
        act = act.astype(BF16)
        a_ref[:, cols] = act
        d_ref[:, cols] = slope.astype(BF16)
        total = total + nn(act, down_ref[0, cols, :])
    out_ref[...] = total


def ffn_forward(r, gain, w):
    rows, width = r.shape
    inner = w.shapes[1][1]
    blk = math.gcd(rows, 512)
    steps = rows // blk
    sds = jax.ShapeDtypeStruct
    by_rows = lambda n: pl.BlockSpec((blk, n), lambda i: (i, 0))
    out = pl.pallas_call(
        functools.partial(ffn_fwd_kernel, gain[1], steps, w),
        grid=(steps,),
        in_specs=[by_rows(width), whole(gain[0].shape)] + w.specs(1),
        out_specs=[by_rows(width), by_rows(inner), by_rows(inner), by_rows(width)] + w.plain_specs(steps),
        out_shape=[sds((rows, width), BF16), sds((rows, inner), BF16), sds((rows, inner), BF16), sds((rows, width), F32)]
        + w.plain_shapes(),
        scratch_shapes=w.scratch(),
        compiler_params=PARAMS,
        cost_estimate=cost(12 * rows * width * inner, 17 << 20, rows * inner * 2),
        name="ffn_fwd",
    )(r, gain[0], *w.args())
    return out if w.packed else [*out, *w.arrays]


def ffn_bwd_kernel(gain, w, kind, *refs):
    n_more = {"none": 0, "slot": 2, "gains": 4}[kind]
    (dr_ref, h_ref, a_ref, d_ref, r_ref, g_ref, up_ref, down_ref), more, place, (dout_ref, dg_ref), dw_outs, \
        (low, ht, acc, r_s), dw_scr = cut(refs, 8, n_more, len(w.place()), 2, 2, 4, w.n_scratch())
    n = pl.program_id(0)
    dup_ref, ddown_ref = dw_scr if w.packed else dw_outs

    @pl.when(n == 0)
    def _():
        grad = dr_ref[...]
        acc[...] = grad
        low[...] = grad.astype(BF16)
        ht[...] = h_ref[...].T

    grad = low[...]
    some = r_ref.shape[0]
    r_s[pl.ds(pl.multiple_of(n * some, some), some), :] = r_ref[...]
    span = up_ref.shape[2]
    rows = pl.ds(pl.multiple_of(n * span, span), span)
    ddown_ref[0, rows, :] = tn(a_ref[...], grad).astype(BF16)
    du = (nt(grad, down_ref[0]) * d_ref[...].astype(F32)).astype(BF16)
    dup_ref[n] = nn(ht[...], du).astype(BF16)
    acc[...] += nt(du, up_ref[0])
    last = n == pl.num_programs(0) - 1

    @pl.when(last)
    def _():
        dout_ref[...], dg_ref[...] = norm_back(r_s[...], row_of(g_ref, gain), acc[...])

    w.store(place, [dup_ref, ddown_ref], dw_outs, last)
    if not w.packed or kind == "none":
        return
    at = sum(w.share(s) for s in w.shapes)

    @pl.when(last)
    def _():
        if kind == "slot":
            for src, dst in zip(more, dw_outs):
                dst[:, :, at:, :] = src[...]
        else:
            gains = [dg_ref] + list(more)
            row = lax.broadcasted_iota(jnp.int32, (16, dg_ref.shape[1]), 0)
            block = jnp.zeros((16, dg_ref.shape[1]), F32)
            for x, ref in enumerate(gains):
                block = jnp.where(row == x, ref[...], block)
            block = block.astype(BF16)
            for dst in dw_outs:
                for j in range(INNER):
                    for k in range(w.outer):
                        dst[j, k, at:, :] = block


def ffn_backward(dr, hidden, act, slope, w, plain, r, gain, kind="none", more=()):
    rows, width = dr.shape
    inner = w.shapes[1][1]
    span = inner // w.shapes[0][0]
    steps = inner // span
    sds = jax.ShapeDtypeStruct
    once = lambda shape: pl.BlockSpec(shape, lambda i: (0,) * len(shape), pipeline_mode=pl.Buffered(1))
    by_cols = pl.BlockSpec((rows, span), lambda i: (0, i))
    extra = {"none": 0, "slot": more[0].shape[2] if kind == "slot" else 0, "gains": 16}[kind] if w.packed else 0
    if not w.packed:
        kind, more = "none", ()
    grads = w.grad_shapes(extra)
    return pl.pallas_call(
        functools.partial(ffn_bwd_kernel, gain[1], w, kind),
        grid=(steps,),
        in_specs=[once((rows, width)), once((rows, width)), by_cols, by_cols,
                  pl.BlockSpec((rows // steps, width), lambda i: (i, 0)), once(gain[0].shape),
                  pl.BlockSpec((1, width, span), lambda i: (i, 0, 0)), pl.BlockSpec((1, span, width), lambda i: (0, i, 0))]
        + [once(x.shape) for x in more] + [smem()] * len(w.place()),
        out_specs=[whole((rows, width)), whole((1, width))] + [whole(s.shape) for s in grads],
        out_shape=[sds((rows, width), F32), sds((1, width), F32)] + grads,
        scratch_shapes=[pltpu.VMEM((rows, width), BF16), pltpu.VMEM((width, rows), BF16), pltpu.VMEM((rows, width), F32),
                        pltpu.VMEM((rows, width), F32)] + w.grad_scratch(),
        compiler_params=PARAMS,
        cost_estimate=cost(16 * rows * width * inner, 25 << 20),
        name="ffn_bwd",
    )(dr, hidden, act, slope, r, gain[0], *plain, *more, *w.place())


def slot_kernel(gain, w, halo, *refs):
    n_grad = 2 if w.packed else 1
    n_join = n_grad - 1
    (len_ref, place_ref, r_ref, g_ref, cot_ref), other, halo_refs, w_refs, (out_ref, dr_ref, dg_ref), send, dw_outs, \
        w_scr, dw_scr, joined = cut(
            refs, 5, n_join, 3 if halo else 0, w.n_args(), 3, n_join, n_grad, w.n_scratch(), w.n_scratch(), n_join)
    if other:
        join(place_ref, cot_ref, other[0], joined[0])
        cot_ref = joined[0]
    length = len_ref[place_ref[3]]
    w_ref, = w.load(w_refs, w_scr, length >= 0)
    dw_ref, = dw_scr if w.packed else dw_outs
    rows, width = r_ref.shape
    gain = row_of(g_ref, gain)
    low = norm(r_ref[...], gain).astype(BF16)
    row = lax.broadcasted_iota(jnp.int32, (rows, width), 0)
    above = below = 0.0
    place = row
    if halo:
        base_ref, next_ref, prev_ref = halo_refs
        place = row + base_ref[0]
        after = norm(next_ref[...], gain).astype(BF16)
        above = nn(after, w_ref[0, width:, :])[:1, :] * base_ref[1].astype(F32)
        below = jnp.where(base_ref[0] - 1 < length - 1, prev_ref[...].astype(F32)[:1, :], 0.0)
    live = place < length - 1
    second = nn(low, w_ref[0, width:, :])
    shifted = jnp.where(row == rows - 1, above, pltpu.roll(second, rows - 1, 0))
    out_ref[...] = jnp.where(live, nn(low, w_ref[0, :width, :]) + shifted, 0.0).astype(BF16)
    if send:
        send[0][...] = other_half(place_ref, out_ref)
    g = jnp.where(live, cot_ref[...].astype(F32), 0.0)
    before = jnp.where(row == 0, below, pltpu.roll(g, 1, 0)).astype(BF16)
    g = g.astype(BF16)
    low_t = low.T
    dw_ref[0, :width, :] = nn(low_t, g).astype(BF16)
    dw_ref[0, width:, :] = nn(low_t, before).astype(BF16)
    dy = nt(g, w_ref[0, :width, :]) + nt(before, w_ref[0, width:, :])
    dr_ref[...], dg_ref[...] = norm_back(r_ref[...], gain, dy)
    w.store(w_refs[:1], [dw_ref], dw_outs, length >= 0)


def slot_step(length, r, gain, w, cot, halo):
    rows, width = r.shape
    sds = jax.ShapeDtypeStruct
    grads = w.grad_shapes()
    full = lambda x: pl.BlockSpec(x.shape, lambda i: (0,) * len(x.shape))
    outs = [sds((rows, width), BF16), sds((rows, width), F32), sds((1, width), F32)]
    outs += ([sds((rows // 2, width), BF16)] if w.packed else []) + grads
    return pl.pallas_call(
        functools.partial(slot_kernel, gain[1], w, len(halo) > 0),
        grid=(1,),
        in_specs=[smem(), smem()] + [full(x) for x in (r, gain[0], *cot)] + [smem(), *map(full, halo[1:])][:len(halo)] + w.specs(1),
        out_specs=[full(x) for x in outs],
        out_shape=outs,
        scratch_shapes=w.scratch() + w.grad_scratch() + ([pltpu.VMEM((rows, width), BF16)] if w.packed else []),
        compiler_params=PARAMS,
        cost_estimate=cost(36 * rows * width * width, 9 << 20),
        name="slot",
    )(*length, r, gain[0], *cot, *halo, *w.args())


def turn_kernel(g_in, g_out, wf, ws, *refs):
    (len_ref, place_ref, r_ref, g_ref, cot_ref, other_ref), f_refs, s_refs, \
        (out_ref, send_ref, dr_ref, dg_in_ref, dg_out_ref), dw_outs, (h_s, a_s, d_s, r_s, acc, cot_s), \
        f_scr, s_scr, f_dw, s_dw = cut(
            refs, 6, wf.n_args(), ws.n_args(), 5, 2, 6, wf.n_scratch(), ws.n_scratch(), wf.n_scratch(), ws.n_scratch())
    length = len_ref[place_ref[3]]
    always = length >= 0
    up_ref, down_ref = wf.load(f_refs, f_scr, always, True)
    slot_ref, = ws.load(s_refs, s_scr, always, True)
    join(place_ref, cot_ref, other_ref, cot_s)
    rows, width = r_ref.shape
    span = up_ref.shape[2]
    blk = math.gcd(rows, 512)
    for b in range(rows // blk):
        part = slice(b * blk, (b + 1) * blk)
        total = norm(r_ref[part, :], row_of(g_ref, g_in))
        low_in = total.astype(BF16)
        h_s[part, :] = low_in
        for c in range(up_ref.shape[0]):
            cols = slice(c * span, (c + 1) * span)
            act, slope = gelu_parts(nn(low_in, up_ref[c]))
            act = act.astype(BF16)
            a_s[part, cols] = act
            d_s[part, cols] = slope.astype(BF16)
            total = total + nn(act, down_ref[0, cols, :])
        r_s[part, :] = total

    gain = row_of(g_ref, g_out)
    row = lax.broadcasted_iota(jnp.int32, (rows, width), 0)
    live = row < length - 1
    rounded = norm(r_s[...], gain).astype(BF16)
    second = nn(rounded, slot_ref[0, width:, :])
    second = jnp.where(row == rows - 1, 0.0, pltpu.roll(second, rows - 1, 0))
    out_ref[...] = jnp.where(live, nn(rounded, slot_ref[0, :width, :]) + second, 0.0).astype(BF16)
    send_ref[...] = other_half(place_ref, out_ref)
    g = jnp.where(live, cot_s[...].astype(F32), 0.0)
    before = jnp.where(row == 0, 0.0, pltpu.roll(g, 1, 0)).astype(BF16)
    g = g.astype(BF16)
    turned = rounded.T
    s_dw[0][0, :width, :] = nn(turned, g).astype(BF16)
    s_dw[0][0, width:, :] = nn(turned, before).astype(BF16)
    dy = nt(g, slot_ref[0, :width, :]) + nt(before, slot_ref[0, width:, :])
    grad, dg_out_ref[...] = norm_back(r_s[...], gain, dy)

    acc[...] = grad
    grad = grad.astype(BF16)
    turned = h_s[...].T
    for c in range(up_ref.shape[0]):
        cols = slice(c * span, (c + 1) * span)
        f_dw[1][0, cols, :] = tn(a_s[:, cols], grad).astype(BF16)
        du = (nt(grad, down_ref[0, cols, :]) * d_s[:, cols].astype(F32)).astype(BF16)
        f_dw[0][c] = nn(turned, du).astype(BF16)
        acc[...] += nt(du, up_ref[c])
    dr_ref[...], dg_in_ref[...] = norm_back(r_ref[...], row_of(g_ref, g_in), acc[...])
    wf.store([place_ref], f_dw, dw_outs, always)

    @pl.when(always)
    def _():
        deal(Spot(place_ref, wf.outer, ws.far[1]), s_dw[0], sum(wf.share(x) for x in wf.shapes), *dw_outs)


def turn(length, r, gain_in, gain_out, wf, ws, halves):
    rows, width = r.shape
    inner = wf.shapes[1][1]
    sds = jax.ShapeDtypeStruct
    vm = pltpu.VMEM
    outs = [sds((rows, width), BF16), sds((rows // 2, width), BF16), sds((rows, width), F32), sds((1, width), F32),
            sds((1, width), F32)] + wf.grad_shapes(sum(ws.share(x) for x in ws.shapes))
    return pl.pallas_call(
        functools.partial(turn_kernel, gain_in[1], gain_out[1], wf, ws),
        in_specs=[smem(), smem()] + [vmem()] * 4 + wf.specs(0) + ws.specs(0),
        out_specs=[vmem() for _ in outs],
        out_shape=outs,
        scratch_shapes=[vm((rows, width), BF16), vm((rows, inner), BF16), vm((rows, inner), BF16), vm((rows, width), F32),
                        vm((rows, width), F32), vm((rows, width), BF16)]
        + wf.scratch() + ws.scratch() + wf.grad_scratch() + ws.grad_scratch(),
        compiler_params=PARAMS,
        cost_estimate=cost(36 * rows * width * inner, 17 << 20, rows * inner * 2),
        name="turn",
    )(*length, r, gain_in[0], *halves, *wf.args(), *ws.args())


def pack_kernel(lane_ref, gains_ref, *refs):
    *ins, first_ref, second_ref = refs
    pieces = []
    for ref in ins:
        if len(ref.shape) == 3:
            pieces += [ref[a] for a in range(ref.shape[0])]
        elif ref.shape[1] > first_ref.shape[1]:
            width = first_ref.shape[1]
            pieces += [ref[:, a * width:(a + 1) * width] for a in range(ref.shape[1] // width)]
        else:
            pieces.append(ref[...])
        if ref is ins[0]:
            count, share = gains_ref.shape
            row = lax.broadcasted_iota(jnp.int32, (share, first_ref.shape[1]), 0)
            lane = lax.broadcasted_iota(jnp.int32, (share, first_ref.shape[1]), 1)
            spread = jnp.where(lane == row + lane_ref[0], 1.0, 0.0).astype(BF16)
            gains = nn(gains_ref[...], spread).astype(BF16)
            pieces.append(jnp.concatenate([gains, jnp.zeros((16 - count, gains.shape[1]), BF16)], axis=0))
    at = 0
    dsts = [first_ref, second_ref]
    for piece in pieces:
        if at == dsts[0].shape[0]:
            at = 0
            dsts.pop(0)
        dst = dsts[0]
        dst[at:at + piece.shape[0], :] = piece
        at += piece.shape[0]


def pack(lane, gains, *groups):
    width = groups[0][0].shape[-1]
    rows = [sum(x.size for x in xs) // width for xs in groups]
    rows[0] += 16
    arrays = [x for xs in groups for x in xs]
    return pl.pallas_call(
        pack_kernel,
        in_specs=[smem()] + [vmem()] * (1 + len(arrays)),
        out_specs=[vmem() for _ in rows],
        out_shape=[jax.ShapeDtypeStruct((n, width), BF16) for n in rows],
        name="pack",
    )(lane, gains, *arrays)


def finish_kernel(shapes, terms, lane_ref, *refs):
    *ins, outs = cut(refs, *terms, len(refs) - sum(terms))
    at_out = 0
    for group, parts in zip(shapes, ins):
        total = summed([x[...] for x in parts])
        at = 0
        for stack, share in group:
            out = outs[at_out]
            width = total.shape[1]
            for a in range(stack):
                rows = total[at:at + share, :]
                at += share
                if len(out.shape) == 3:
                    out[a] = rows
                else:
                    out[:, a * width:(a + 1) * width] = rows
            at_out += 1
        if at < total.shape[0]:
            out = outs[at_out]
            count, share = out.shape
            row = lax.broadcasted_iota(jnp.int32, (width, share), 0)
            lane = lax.broadcasted_iota(jnp.int32, (width, share), 1)
            pick = jnp.where(row == lane + lane_ref[0], 1.0, 0.0).astype(BF16)
            out[...] = nn(total[at:, :].astype(BF16), pick)[:count, :]
            at_out += 1


def finish(lane, shapes, sums, more, outs):
    groups = [[x] for x in sums] + more
    arrays = [x for g in groups for x in g]
    return pl.pallas_call(
        functools.partial(finish_kernel, shapes, [len(g) for g in groups]),
        in_specs=[smem()] + [vmem()] * len(arrays),
        out_specs=[vmem() for _ in outs],
        out_shape=[jax.ShapeDtypeStruct(s, F32) for s in outs],
        name="finish",
    )(lane, *arrays)


def exchange(x, send, *during):
    count = x.shape[0]
    me = lax.axis_index("seq")
    out = x
    for k in range(1, count):
        piece = lax.dynamic_index_in_dim(x, (me + k) % count, 0, keepdims=False) if send is None else send
        piece = hold(lax.ppermute(piece, "seq", [(s, (s + k) % count) for s in range(count)]), *during)
        out = lax.dynamic_update_index_in_dim(out, piece, (me - k) % count, 0)
    return out


def to_examples(x, count):
    examples, rows, width = x.shape
    if count == examples:
        return exchange(x, None).reshape(count * rows, width)
    me = lax.axis_index("seq")
    group = count // examples
    all_rows = lax.all_gather(x, "seq", axis=1, tiled=True)
    one = lax.dynamic_index_in_dim(all_rows, me // group, 0, keepdims=False)
    return lax.dynamic_slice_in_dim(one, (me % group) * examples * rows, examples * rows, 0)


def to_positions(x, examples, count, *during, send=None):
    width = x.shape[1]
    if count == examples:
        return exchange(x.reshape(count, -1, width), send, *during)
    me = lax.axis_index("seq")
    rows = x.shape[0] // examples
    all_rows = lax.all_gather(x, "seq", axis=0, tiled=True).reshape(examples, count * rows, width)
    return lax.dynamic_slice_in_dim(all_rows, me * rows, rows, 1)


class Ring:
    def __init__(self):
        self.dp = lax.axis_size("dp")
        self.outer = self.dp // INNER
        self.columns = [[o * INNER + i for o in range(self.outer)] for i in range(INNER)]
        self.planes = [[o * INNER + i for i in range(INNER)] for o in range(self.outer)]

    def inner_step(self, x, j):
        return lax.ppermute(x, "dp", [(d, d // INNER * INNER + (d + j) % INNER) for d in range(self.dp)])

    def outer_step(self, x, k):
        return lax.ppermute(x, "dp", [(d, (d + k * INNER) % self.dp) for d in range(self.dp)])

    def swap(self, x):
        return lax.ppermute(x, "seq", [(0, 1), (1, 0)])

    def column(self, shard, *during):
        return [shard] + [hold(self.outer_step(shard, k), *during) for k in range(1, self.outer)]

    def plane(self, column, *during):
        return [column] + [hold(self.inner_step(column, j), *during) for j in range(1, INNER)]

    def far_column(self, x):
        return lax.all_gather(x, "dp", axis=0, axis_index_groups=self.columns)

    def both(self, plane):
        return plane + [self.swap(x) for x in plane]

    def pairs(self, keep, send, *during):
        other = hold(self.swap(send), *during)
        return [low(keep[j].astype(F32) + other[j].astype(F32)) for j in range(INNER)]

    def across(self, pairs, *during):
        return low(summed([pairs[0]] + [hold(self.inner_step(pairs[j], j), *during) for j in range(1, INNER)]))

    def pair(self, keep, send):
        return low(keep.astype(F32) + self.swap(send).astype(F32))

    def plane_sum(self, pair):
        return lax.psum_scatter(pair, "dp", scatter_dimension=0, axis_index_groups=self.planes)

    def far_sum(self, total):
        return lax.psum_scatter(total, "dp", scatter_dimension=0, axis_index_groups=self.columns)

    def near_sum(self, total):
        return [total[0]] + [self.outer_step(total[k], k) for k in range(1, self.outer)]


def low(x):
    return x.astype(BF16)


def summed(parts):
    return sum(x.astype(F32) for x in parts)


def hold(x, *after):
    return lax.optimization_barrier((x, after))[0]


def per_device(source, canvas, source_len, canvas_len, cotangent, enc_attn, enc_up, enc_down, dec_attn, cross_attn,
               dec_up, dec_down, slot_proj, norm_gains):
    examples, _, width = source.shape
    seq = lax.axis_size("seq")
    devices = lax.axis_size("dp") * seq
    group = seq // examples
    me = lax.axis_index("seq")
    rank = lax.axis_index("dp") * seq + me
    groups = [[e * group + t for t in range(group)] for e in range(examples)]
    packed = seq == SEQ and lax.axis_size("dp") % INNER == 0 and enc_up.shape[0] % 16 == 0

    def whole_keys(x):
        return lax.all_gather(x, "seq", axis=0, tiled=True, axis_index_groups=groups) if group > 1 else x

    def own_keys(x):
        if group == 1:
            return x
        return lax.psum_scatter(x, "seq", scatter_dimension=0, tiled=True, axis_index_groups=groups)

    def neighbour(x, step):
        pairs = [(s, s + step) for s in range(seq) if 0 <= s % group + step < group]
        return lax.ppermute(x, "seq", pairs)

    def chunks(up):
        rows = up.shape[0]
        return up.reshape(rows, -1, width).transpose(1, 0, 2)

    def unchunk(up):
        return up.transpose(1, 0, 2).reshape(up.shape[1], -1)

    shards = {
        "enc": enc_attn, "dec": dec_attn, "cross": cross_attn, "eup": chunks(enc_up), "edown": enc_down[None],
        "dup": chunks(dec_up), "ddown": dec_down[None], "slot": slot_proj[None],
    }
    shapes = {name: (x.shape[0], x.shape[1] * devices, width) for name, x in shards.items()}
    flat = lambda name: shards[name].reshape(-1, width)
    dp_index = lax.axis_index("dp")
    spot = jnp.stack([dp_index // INNER, dp_index % INNER, me, me // group]).astype(jnp.int32)
    if packed:
        ring = Ring()
        share = norm_gains.shape[1]
        lane = jnp.reshape(rank * share, (1,)).astype(jnp.int32)
        late, flat5 = pack(
            lane, norm_gains, [dec_attn, enc_up, enc_down, cross_attn, slot_proj], [dec_up, dec_down])
        names = ["eup", "edown", "cross", "slot", "dup", "ddown"]
        sizes = [shapes[n][0] * shapes[n][1] // devices for n in names[:4]]
        late = ring.far_column(late)
        x5 = ring.plane(flat5)
        z1 = jnp.stack(hold(ring.column(flat("enc")), *x5))
        g1 = ring.plane(z1)
        source, canvas, cotangent = hold((source, canvas, cotangent), z1)
        late = hold(late, *g1)
        x5 = ring.far_column(jnp.stack(hold(x5, *g1)))
        g1 = ring.both(g1)
        cuts = [shapes["dec"][0] * shapes["dec"][1] // devices + 16]
        cuts.append(cuts[0] + sum(sizes[:2]))
        late = [late[:, :cuts[0]], late[:, cuts[0]:cuts[1]], late[:, cuts[1]:]]

        def make(arrays, names, far=(1, 1), **more):
            return Weights(True, arrays, [shapes[n] for n in names], spot=spot, outer=ring.outer, far=far, **more)

        w_enc = make(g1, ["enc"], (0, 0))

        def fetch_dec(during):
            return make(ring.both(ring.plane(late[0], during)), ["dec"], (1, 0), tail=16)

        def fetch_effn(before, during):
            return make(ring.both(ring.plane(hold(late[1], before), during)), ["eup", "edown"])

        def fetch_cross_slot(before, during):
            arrays = ring.both(ring.plane(hold(late[2], before), during))
            return make(arrays, ["cross"]), make(arrays, ["slot"], (1, 2), at=sizes[2])

        def fetch_dffn(before, during):
            return make([x5, hold(ring.swap(hold(x5, before)), during)], ["dup", "ddown"], (1, 2), block=True)
    else:
        def fetch(*names):
            return Weights(False, [lax.all_gather(shards[n], ("dp", "seq"), axis=1, tiled=True) for n in names],
                           [shapes[n] for n in names])
        w_enc = fetch("enc")
        fetch_dec = lambda *t: fetch("dec")
        fetch_effn = lambda *t: fetch("eup", "edown")
        fetch_cross_slot = lambda *t: (fetch("cross"), fetch("slot"))
        fetch_dffn = lambda *t: fetch("dup", "ddown")
        gains = lax.all_gather(norm_gains, ("dp", "seq"), axis=1, tiled=True).astype(F32)
    s_len, c_len = (source_len, spot), (canvas_len, spot)
    if packed:
        def halves(x):
            return x, ring.swap(lax.dynamic_index_in_dim(x, 1 - me, 0, keepdims=False))
        src, can, cot = halves(source), halves(canvas), halves(cotangent)
        src = attn_forward(s_len, w_enc, halves=src)
    else:
        src, can, cot = (to_examples(x, seq) for x in (source, canvas, cotangent))
        src_all, can_all = whole_keys(src), whole_keys(can)
        src = [src, *attn_forward(s_len, w_enc, xq=src, xk=src_all)]
    src, q_a, k_a, v_a, o_a, x_a, r_a, p_enc = src
    w_dec = fetch_dec(r_a)
    can = hold(can, r_a)
    if packed:
        can = attn_forward(c_len, w_dec, halves=can)
    else:
        can = [can, *attn_forward(c_len, w_dec, xq=can, xk=can_all)]
    can, q_b, k_b, v_b, o_b, x_b, r_c, *tail, p_dec = can
    gains = tail[0] if packed else gains
    gain = [(gains, i) for i in range(5)]
    w_effn = fetch_effn(r_a, r_c)
    h_a, act_a, slope_a, r_b, *p_effn = ffn_forward(hold(r_a, r_c), gain[0], w_effn)
    w_cross, w_slot = fetch_cross_slot(r_c, r_b)
    low_one, low_enc, q_c, k_c, v_c, o_c, x_c, r_d, p_cross = attn_forward(
        s_len, w_cross, rq=r_c, rk=whole_keys(r_b), gq=gain[2], gk=gain[1])
    w_dffn = fetch_dffn(r_b, r_d)
    if packed:
        slot_out, slot_send, dr, dg3, dg4, *d_dffn = turn(c_len, r_d, gain[3], gain[4], w_dffn, w_slot, cot)
    else:
        h_b, act_b, slope_b, r_e, *p_dffn = ffn_forward(r_d, gain[3], w_dffn)
        halo = []
        if group > 1:
            place = jnp.stack([me % group * r_e.shape[0], me % group < group - 1]).astype(jnp.int32)
            halo = [place, neighbour(r_e[:8], -1), neighbour(cot[-8:][::-1], 1)]
        slot_out, dr, dg4, *d_slot = slot_step(c_len, r_e, gain[4], w_slot, [cot], halo)
        slot_send = None
        dr, dg3, *d_dffn = ffn_backward(dr, h_b, act_b, slope_b, w_dffn, p_dffn, r_d, gain[3], "slot", d_slot)
    slot_out = to_positions(slot_out, examples, seq, send=slot_send)
    if packed:
        p1 = ring.pair(*d_dffn)
        dr = hold(dr, p1)
    alone = group == 1
    norms = [(r_c, gain[2])] + ([(r_b, gain[1])] if alone else [])
    dr_c, dr_b, dg2, *rest = attn_backward(
        False, s_len, dr, w_cross, p_cross, q_c, k_c, v_c, o_c, x_c, (low_one, low_enc), norms)
    if alone:
        dg1, *d_cross = rest
    else:
        d_cross = rest
        dr_b, dg1 = norm_back(r_b, gains[1:2], own_keys(dr_b))
    if packed:
        s1 = ring.plane_sum(p1)
        dr_b = hold(dr_b, slot_out)
    dr_a, dg0, *d_effn = ffn_backward(
        dr_b, h_a, act_a, slope_a, w_effn, p_effn, r_a, gain[0], "gains", [dg1, dg2, dg3, dg4])
    if packed:
        p2 = ring.pairs(*d_cross, dr_a)
        p3 = ring.pairs(*hold(tuple(d_effn), *p2))
        dr_c = hold(dr_c, *p3)
        z1 = ring.far_sum(s1)
    sides = 1 if alone else 2
    out = attn_backward(alone, c_len, dr_c, w_dec, p_dec, q_b, k_b, v_b, o_b, x_b, [can, can if alone else can_all][:sides])
    d_can, d_dec = out[:sides], list(out[sides:])
    can_send = d_dec.pop(0) if packed else None
    canvas_grad = d_can[0] if alone else d_can[0] + own_keys(d_can[1])
    if packed:
        s2 = ring.across(p2, canvas_grad)
        s3 = ring.across(p3, canvas_grad)
        p4 = ring.pairs(*hold(tuple(d_dec), s2, s3, z1))
        dr_a = hold(dr_a, *p4)
        z23 = ring.far_sum(jnp.concatenate([s2, s3], axis=1))
        grads, *d_enc = attn_grads(s_len, dr_a, w_enc, p_enc, q_a, k_a, v_a, o_a, x_a, src)
        canvas_grad = to_positions(canvas_grad, examples, seq, grads, send=can_send)
        s4 = ring.across(p4, grads)
        d_enc = hold(tuple(d_enc), s4, z23)
        source_grad, source_send = input_grad(spot, dr_a, grads, p_enc)
        z4 = ring.near_sum(s4)
        p5 = ring.pairs(*d_enc, source_grad, *z4[1:])
        source_grad = to_positions(source_grad, examples, seq, send=hold(source_send, *p5))
        s5 = ring.across(p5, source_grad, canvas_grad)
        z5 = ring.near_sum(s5)
        groups = [("dup", "ddown", "slot"), ("cross", "eup", "edown"), ("dec",), ("enc",)]
        rows_of = [[(shards[n].shape[0], shards[n].shape[1]) for n in names] for names in groups]
        like = {"enc": enc_attn, "eup": enc_up, "edown": enc_down, "dec": dec_attn, "cross": cross_attn, "dup": dec_up,
                "ddown": dec_down, "slot": slot_proj}
        outs = [like[n].shape for n in groups[0] + groups[1]] + [norm_gains.shape, dec_attn.shape, enc_attn.shape]
        t_dup, t_ddown, t_slot, t_cross, t_eup, t_edown, t_gains, t_dec, t_enc = finish(
            lane, rows_of, [z1, z23], [z4, z5], outs)
    else:
        def home(x):
            return lax.psum_scatter(x, ("dp", "seq"), scatter_dimension=1, tiled=True).astype(F32)
        t_dec, t_cross = home(d_dec[0]), home(d_cross[0])
        t_eup, t_edown, t_dup, t_ddown, t_slot = (home(x) for x in (*d_effn, *d_dffn, *d_slot))
        t_eup, t_edown, t_dup, t_ddown, t_slot = unchunk(t_eup), t_edown[0], unchunk(t_dup), t_ddown[0], t_slot[0]
        out = attn_backward(alone, s_len, dr_a, w_enc, p_enc, q_a, k_a, v_a, o_a, x_a, [src, src if alone else src_all][:sides])
        d_src, d_enc = out[:sides], out[sides:]
        source_grad = d_src[0] if alone else d_src[0] + own_keys(d_src[1])
        t_enc = home(d_enc[0])
        t_gains = home(jnp.concatenate([dg0, dg1, dg2, dg3, dg4], axis=0))
        source_grad = to_positions(source_grad, examples, seq)
        canvas_grad = to_positions(canvas_grad, examples, seq)

    return (
        slot_out, source_grad, canvas_grad,
        t_enc, t_eup, t_edown, t_dec, t_cross, t_dup, t_ddown, t_slot, t_gains,
    )


def solution(mesh):
    by_seq = P("dp", "seq", None)
    stack = P(None, ("dp", "seq"), None)
    by_row = P(("dp", "seq"), None)
    gains = P(None, ("dp", "seq"))
    in_specs = (by_seq, by_seq, P("dp"), P("dp"), by_seq, stack, by_row, by_row, stack, stack, by_row, by_row, by_row,
                gains)
    out_specs = (by_seq, by_seq, by_seq, stack, by_row, by_row, stack, stack, by_row, by_row, by_row, gains)
    return jax.shard_map(per_device, mesh=mesh, in_specs=in_specs, out_specs=out_specs, check_vma=False)
```

```python
import functools
import math

import jax
import jax.numpy as jnp
from jax import lax
from jax.experimental import pallas as pl
from jax.experimental.pallas import tpu as pltpu
from jax.sharding import PartitionSpec as P

F32 = jnp.float32
BF16 = jnp.bfloat16
H = 8
HD = 64
PAIR = 2 * HD
LOG2E = math.log2(math.e)
Q_SCALE = LOG2E / 8.0
K_BACK = 1.0 / LOG2E
MASKED = -1e30
VMEM_LIMIT = 58 * 1024 * 1024
PARAMS = pltpu.CompilerParams(vmem_limit_bytes=VMEM_LIMIT)


def nn(a, b):
    return lax.dot_general(a, b, (((1,), (0,)), ((), ())), preferred_element_type=F32)


def nt(a, b):
    return lax.dot_general(a, b, (((1,), (1,)), ((), ())), preferred_element_type=F32)


def tn(a, b):
    return lax.dot_general(a, b, (((0,), (0,)), ((), ())), preferred_element_type=F32)


def norm_parts(r):
    centre = r - jnp.mean(r, axis=-1, keepdims=True)
    rs = lax.rsqrt(jnp.mean(centre * centre, axis=-1, keepdims=True) + 1e-5)
    return centre * rs, rs


def norm(r, gain):
    return norm_parts(r)[0] * gain


def norm_back(r, gain, dy):
    z, rs = norm_parts(r)
    t = dy * gain
    dr = (t - jnp.mean(t, axis=-1, keepdims=True) - z * jnp.mean(t * z, axis=-1, keepdims=True)) * rs
    return dr, jnp.sum(dy * z, axis=0, keepdims=True)


def lanes(rows):
    return lax.broadcasted_iota(jnp.int32, (rows, PAIR), 1)


def key_extras(length, count):
    row = lax.broadcasted_iota(jnp.int32, (count, PAIR), 0)
    lane = lanes(count)
    bias = jnp.where(row < length, 0.0, MASKED)
    return jnp.where(lane == 3 * H, bias, jnp.where(lane < 3 * H, 1.0, 0.0)).astype(BF16)


def spread_parts(v):
    high = v.astype(BF16).astype(F32)
    rest = v - high
    middle = rest.astype(BF16).astype(F32)
    parts = high + pltpu.roll(middle, H, 1) + pltpu.roll(rest - middle, 2 * H, 1)
    return jnp.where(lanes(v.shape[0]) == 3 * H, 1.0, parts).astype(BF16)


def parts_of(parts, head):
    lane = lanes(parts.shape[0])
    mine = (lane == 3 * H) | ((lane < 3 * H) & ((lane & (H - 1)) == head))
    return jnp.where(mine, parts, 0.0)


def row_of(ref, row):
    return ref[row:row + 1, :]


def whole(shape):
    return pl.BlockSpec(shape, lambda i: (0,) * len(shape))


def smem():
    return pl.BlockSpec(memory_space=pltpu.SMEM)


def vmem():
    return pl.BlockSpec(memory_space=pltpu.VMEM)


def cost(flops, nbytes, exps=0):
    return pl.CostEstimate(flops=int(flops), bytes_accessed=int(nbytes), transcendentals=int(exps))


INNER = 4
SEQ = 2


class Spot:
    def __init__(self, ref, outer, far):
        self.outer, self.far = outer, far
        self.o, self.i, self.s = ref[0], ref[1], ref[2]

    def owner(self, c, j, k):
        o = k if self.far else lax.rem(self.o - k + self.outer, self.outer)
        i = j if self.far > 1 else lax.rem(self.i - j + INNER, INNER)
        return (o * INNER + i) * SEQ + lax.rem(self.s - c + SEQ, SEQ)

    def ahead(self, o, i):
        return (i if self.far > 1 else lax.rem(i - self.i + INNER, INNER),
                o if self.far else lax.rem(o - self.o + self.outer, self.outer))


def assemble(spot, refs, at, dst, block):
    stack, total, _ = dst.shape
    share = total // (spot.outer * INNER * SEQ)
    for c in range(SEQ):
        for j in range(INNER):
            for k in range(spot.outer):
                ref, x = (refs[c], (k, j)) if block else (refs[c * INNER + j], (k,))
                rows = pl.ds(pl.multiple_of(spot.owner(c, j, k) * share, share), share)
                for a in range(stack):
                    dst[a, rows, :] = ref[(*x, slice(at + a * share, at + (a + 1) * share))]


def deal(spot, src, at, keep, send):
    stack, total, _ = src.shape
    share = total // (spot.outer * INNER * SEQ)
    for core in range(SEQ):
        @pl.when(spot.s == core)
        def _():
            for o in range(spot.outer):
                for i in range(INNER):
                    j, k = spot.ahead(o, i)
                    for s in range(SEQ):
                        first = ((o * INNER + i) * SEQ + s) * share
                        dst = keep if s == core else send
                        for a in range(stack):
                            dst[j, k, at + a * share:at + (a + 1) * share, :] = src[a, first:first + share, :]


class Weights:
    def __init__(self, packed, arrays, shapes, at=0, spot=None, outer=0, far=(0, 0), block=False, tail=0):
        self.packed, self.arrays, self.shapes, self.at, self.spot, self.outer = packed, arrays, shapes, at, spot, outer
        self.far, self.block, self.tail = far, block, tail

    def share(self, shape):
        return shape[0] * shape[1] // (self.outer * INNER * SEQ)

    def args(self):
        return [self.spot, *self.arrays] if self.packed else list(self.arrays)

    def specs(self, dims):
        zero = lambda n: (lambda *_: (0,) * n)
        if not self.packed:
            return [pl.BlockSpec(x.shape, zero(3), pipeline_mode=pl.Buffered(1)) if dims else vmem() for x in self.arrays]
        if not dims:
            return [smem()] + [vmem() for _ in self.arrays]
        rows = sum(self.share(s) for s in self.shapes) + self.tail
        index = self.at // rows
        lead = (self.outer, INNER) if self.block else (self.outer,)
        spec = lambda: pl.BlockSpec((*lead, rows, self.shapes[0][2]), lambda *_: (*(0 for _ in lead), index, 0),
                                    **(dict(pipeline_mode=pl.Buffered(1)) if dims else {}))
        return [smem()] + [spec() for _ in self.arrays]

    def scratch(self):
        return [pltpu.VMEM(s, BF16) for s in self.shapes] if self.packed else []

    def n_args(self):
        return len(self.arrays) + 1 if self.packed else len(self.arrays)

    def n_scratch(self):
        return len(self.shapes) if self.packed else 0

    def load(self, refs, scratch, first, entire=False):
        if not self.packed:
            return list(refs)

        @pl.when(first)
        def _():
            spot = Spot(refs[0], self.outer, self.far[0])
            at = self.at if entire else 0
            for shape, dst in zip(self.shapes, scratch):
                assemble(spot, refs[1:], at, dst, self.block)
                at += self.share(shape)
        return list(scratch)

    def plain_shapes(self):
        return [jax.ShapeDtypeStruct(s, BF16) for s in self.shapes] if self.packed else []

    def plain_blocks(self, steps):
        blocks = []
        for a, m, width in self.shapes if self.packed else []:
            if a % steps == 0:
                blocks.append(((a // steps, m, width), 0))
            else:
                assert m % steps == 0
                blocks.append(((a, m // steps, width), 1))
        return blocks

    def plain_specs(self, steps):
        first, second = (lambda i: (i, 0, 0)), (lambda i: (0, i, 0))
        return [pl.BlockSpec(b, second if dim else first) for b, dim in self.plain_blocks(steps)]

    def plain_store(self, outs, scratch, steps):
        i = pl.program_id(0)
        for out, src, (block, dim) in zip(outs, scratch, self.plain_blocks(steps)):
            n = block[dim]
            part = pl.ds(pl.multiple_of(i * n, n), n)
            out[...] = src[:, part, :] if dim else src[part]

    def grad_shapes(self, extra=0):
        if not self.packed:
            return [jax.ShapeDtypeStruct(s, BF16) for s in self.shapes]
        rows = sum(self.share(s) for s in self.shapes) + extra
        return [jax.ShapeDtypeStruct((INNER, self.outer, rows, self.shapes[0][2]), BF16)] * SEQ

    def grad_scratch(self):
        return [pltpu.VMEM(s, BF16) for s in self.shapes] if self.packed else []

    def place(self):
        return [self.spot] if self.packed else []

    def store(self, place, grads, outs, last):
        if not self.packed:
            return

        @pl.when(last)
        def _():
            spot = Spot(place[0], self.outer, self.far[1])
            at = 0
            for shape, src in zip(self.shapes, grads):
                deal(spot, src, at, *outs)
                at += self.share(shape)


def other_half(place_ref, ref):
    half = ref.shape[0] // 2
    return ref[pl.ds(pl.multiple_of((1 - place_ref[2]) * half, half), half), :]


def join(place_ref, own_ref, other_ref, dst):
    half = other_ref.shape[0]
    me = place_ref[2]
    dst[pl.ds(pl.multiple_of(me * half, half), half), :] = own_ref[me]
    dst[pl.ds(pl.multiple_of((1 - me) * half, half), half), :] = other_ref[...]


def cut(refs, *counts):
    out, at = [], 0
    for n in counts:
        out.append(refs[at:at + n])
        at += n
    assert at == len(refs)
    return out


def attn_fwd_kernel(cross, joined, gq, gk, steps, w, *refs):
    n_in, n_out = (5, 8) if cross else (4, 7 if joined else 6)
    n_tail = 1 if w.tail else 0
    ins, w_refs, outs, tail, plain, (kaug, vaug), xk_s, w_scr = cut(
        refs, n_in, w.n_args(), n_out, n_tail, w.n_scratch(), 2, 1 if cross else 0, w.n_scratch())
    count = kaug.shape[1]
    i = pl.program_id(0)
    start = i == 0
    w_ref, = w.load(w_refs, w_scr, start)
    if cross:
        len_ref, place_ref, rq_ref, rk_ref, g_ref = ins
        xq_ref, xk_ref, q_ref, k_ref, v_ref, o_ref, qx_ref, r_ref = outs
    else:
        len_ref, place_ref, xq_ref, xk_ref = ins
        if joined:
            own_ref, other_ref = xq_ref, xk_ref
            xk_ref, *outs = outs
        q_ref, k_ref, v_ref, o_ref, qx_ref, r_ref = outs
    rows = r_ref.shape[0]

    @pl.when(start)
    def _():
        if w.tail:
            parts = [x[k, w.share(w.shapes[0]):, :].astype(F32) for x in w_refs[1:] for k in range(w.outer)]
            tail[0][...] = sum(parts[1:], parts[0])
        if cross:
            xk = norm(rk_ref[...], row_of(g_ref, gk)).astype(BF16)
            xk_s[0][...] = xk
        else:
            if joined:
                join(place_ref, own_ref, other_ref, xk_ref)
            xk = xk_ref[...]
        k = nn(xk, w_ref[1]).astype(BF16)
        v = nn(xk, w_ref[2]).astype(BF16)
        extras = key_extras(len_ref[place_ref[3]], count)
        ones = jnp.ones((count, PAIR), BF16)
        for p in range(H // 2):
            kaug[p, :, :PAIR] = k[:, p * PAIR:(p + 1) * PAIR]
            kaug[p, :, PAIR:] = extras
            vaug[p, :, :PAIR] = v[:, p * PAIR:(p + 1) * PAIR]
            vaug[p, :, PAIR:] = ones
        k_ref[...] = k
        v_ref[...] = v

    w.plain_store(plain, w_scr, steps)
    if cross:
        xk_ref[...] = xk_s[0][pl.ds(pl.multiple_of(i * (count // steps), count // steps), count // steps), :]
        resid = norm(rq_ref[...], row_of(g_ref, gq))
        xq = resid.astype(BF16)
        xq_ref[...] = xq
    else:
        xq = xk_ref[pl.ds(pl.multiple_of(i * rows, rows), rows), :] if joined else xq_ref[...]
        resid = xq.astype(F32)
    q = nn(xq, w_ref[0]) * Q_SCALE
    q_ref[...] = q.astype(BF16)
    lane = lanes(rows)
    first = lane < HD
    extra = jnp.where(lane == 3 * H, 1.0, 0.0).astype(BF16)

    def score(h):
        p = h // 2
        mine = first if h % 2 == 0 else lane >= HD
        qm = jnp.where(mine, q[:, p * PAIR:(p + 1) * PAIR], 0.0).astype(BF16)
        return nt(jnp.concatenate([qm, extra], axis=1), kaug[p])

    halves = []
    sums = jnp.zeros((rows, PAIR), F32)
    ahead = score(0)
    for h in range(H):
        s = ahead
        if h + 1 < H:
            ahead = score(h + 1)
        m = jnp.max(s, axis=1, keepdims=True)
        o = nn(jnp.exp2(s - m).astype(BF16), vaug[h // 2])
        total = o[:, PAIR:]
        halves.append(o[:, :PAIR] / total)
        sums = jnp.where(lane == h, -(m + jnp.log2(total)), sums)
    qx_ref[...] = spread_parts(sums)
    blended = [jnp.where(first, halves[2 * p], halves[2 * p + 1]).astype(BF16) for p in range(H // 2)]
    o_all = jnp.concatenate(blended, axis=1)
    o_ref[...] = o_all
    r_ref[...] = resid + nn(o_all, w_ref[3])


def attn_forward(length, w, xq=None, xk=None, rq=None, rk=None, gq=None, gk=None, halves=None):
    cross, joined = rq is not None, halves is not None
    if joined:
        rows, width = 2 * halves[1].shape[0], halves[1].shape[1]
        count = rows
    else:
        rows, width = (rq if cross else xq).shape
        count = (rk if cross else xk).shape[0]
    blk = math.gcd(rows, 512)
    steps = rows // blk
    sds = jax.ShapeDtypeStruct
    by_rows = pl.BlockSpec((blk, width), lambda i: (i, 0))
    by_keys = pl.BlockSpec((count // steps, width), lambda i: (i, 0))
    outs = [
        sds((rows, width), BF16), sds((count, width), BF16), sds((count, width), BF16),
        sds((rows, width), BF16), sds((rows, PAIR), BF16), sds((rows, width), F32),
    ]
    out_specs = [by_rows, whole((count, width)), whole((count, width)), by_rows, pl.BlockSpec((blk, PAIR), lambda i: (i, 0)), by_rows]
    if cross:
        args = [*length, rq, rk, gq[0]]
        in_specs = [smem(), smem(), by_rows, whole((count, width)), whole(gq[0].shape)]
        outs = [sds((rows, width), BF16), sds((count, width), BF16)] + outs
        out_specs = [by_rows, by_keys] + out_specs
    elif joined:
        args = [*length, *halves]
        in_specs = [smem(), smem(), *(whole(x.shape) for x in halves)]
        outs = [sds((rows, width), BF16)] + outs
        out_specs = [whole((rows, width))] + out_specs
    else:
        args = [*length, xq, xk]
        in_specs = [smem(), smem(), by_rows, whole((count, width))]
    if w.tail:
        outs.append(sds((w.tail, width), F32))
        out_specs.append(whole((w.tail, width)))
    out = pl.pallas_call(
        functools.partial(attn_fwd_kernel, cross, joined, *((gq[1], gk[1]) if cross else (0, 0)), steps, w),
        grid=(steps,),
        in_specs=in_specs + w.specs(1),
        out_specs=out_specs + w.plain_specs(steps),
        out_shape=outs + w.plain_shapes(),
        scratch_shapes=[pltpu.VMEM((H // 2, count, 2 * PAIR), BF16)] * 2
        + ([pltpu.VMEM((count, width), BF16)] if cross else []) + w.scratch(),
        compiler_params=PARAMS,
        cost_estimate=cost(rows * count * 5 * 512 * H, 14 << 20, rows * count * H),
        name="cross_fwd" if cross else "self_fwd",
    )(*args, *w.args())
    return out if w.packed else [*out, *w.arrays]


def pair_back(p, k_ref, v_ref, q_ref, qx_ref, o, do, kaug, vaug, qaug, oaug, kt, dqt):
    count, rows = kaug.shape[0], o.shape[0]
    blk = math.gcd(count, 512)
    kaug[:, :PAIR] = k_ref[...]
    vaug[:, :PAIR] = v_ref[...]
    kt[...] = k_ref[...].T
    lane = lanes(rows)
    inner = -(o.astype(F32) * do.astype(F32))
    high = inner.astype(BF16).astype(F32)
    rest = pltpu.roll(inner - high, HD, 1)
    q, do, parts = q_ref[...].astype(F32), do.astype(F32), qx_ref[...].astype(F32)
    for h in range(2):
        mine = lane < HD if h == 0 else lane >= HD
        qaug[h, :, :PAIR] = jnp.where(mine, q, 0.0).astype(BF16)
        qaug[h, :, PAIR:] = parts_of(parts, 2 * p + h).astype(BF16)
        oaug[h, :, :PAIR] = jnp.where(mine, do, 0.0).astype(BF16)
        oaug[h, :, PAIR:] = jnp.where(mine, high, rest).astype(BF16)
    for j in range(count // blk):
        keys = slice(j * blk, (j + 1) * blk)
        dv_sum = dk_sum = None
        for h in range(2):
            pt = jnp.exp2(nt(kaug[keys, :], qaug[h]))
            dpt = nt(vaug[keys, :], oaug[h])
            ptb = pt.astype(BF16)
            dst = (pt * dpt).astype(BF16)
            dv_h = nn(ptb, oaug[h, :, :PAIR])
            dk_h = nn(dst, qaug[h, :, :PAIR])
            dq_h = nn(kt[h * HD:(h + 1) * HD, keys], dst)
            dv_sum = dv_h if h == 0 else dv_sum + dv_h
            dk_sum = dk_h if h == 0 else dk_sum + dk_h
            if j == 0:
                dqt[h * HD:(h + 1) * HD, :] = dq_h
            else:
                dqt[h * HD:(h + 1) * HD, :] += dq_h
        yield keys, (dk_sum * K_BACK).astype(BF16), dv_sum.astype(BF16)


def attn_bwd_kernel(gains, same, w, *refs):
    norms = len(gains)
    n_out = 1 if same else 2
    n_dg = 0 if same else norms
    n_send = 1 if same and w.packed else 0
    n_grad = 2 if w.packed else 1
    (len_ref, place_ref, dr_ref, w3_ref, w_ref, q_ref, k_ref, v_ref, o_ref, qx_ref), x_refs, n_refs, place, outs, send, dg_refs, dw_outs, \
        (dab, do_s, kaug, vaug, qaug, oaug, kt, ot, dqt, grads_q, grads_k, w_all), xts, dw_scr = cut(
            refs, 10, n_out, 2 * norms, len(w.place()), n_out, n_send, n_dg, n_grad, 12, n_out, w.n_scratch())
    dw_ref, = dw_scr if w.packed else dw_outs
    count = kaug.shape[0]
    rows, width = dab.shape
    p = pl.program_id(0)

    @pl.when(p == 0)
    def _():
        dab[...] = dr_ref[...].astype(BF16)
        kaug[:, PAIR:] = key_extras(len_ref[place_ref[3]], count)
        vaug[:, PAIR:] = jnp.ones((count, PAIR), BF16)
        do = nt(dab[...], w3_ref[0]).astype(BF16)
        for n in range(H // 2):
            do_s[n] = do[:, n * PAIR:(n + 1) * PAIR]

    @pl.when(p < 3)
    def _():
        w_all[:, pl.ds(pl.multiple_of(p * width, PAIR), width)] = w_ref[0]

    own = pl.ds(pl.multiple_of(p * PAIR, PAIR), PAIR)
    behind = pl.ds(pl.multiple_of(width + p * PAIR, PAIR), PAIR)
    o, do = o_ref[...], do_s[p]
    ot[own, :] = o.T
    for x, xt in zip(x_refs, xts):
        xt[own, :] = x[...].T
    for keys, dk, dv in pair_back(p, k_ref, v_ref, q_ref, qx_ref, o, do, kaug, vaug, qaug, oaug, kt, dqt):
        grads_k[keys, own] = dk
        grads_k[keys, behind] = dv
    grads_q[:, own] = (dqt[...].T * 0.125).astype(BF16)
    last = p == pl.num_programs(0) - 1

    @pl.when(last)
    def _():
        dw_ref[0] = nn(xts[0][...], grads_q[...]).astype(BF16)
        both = nn(xts[-1][...], grads_k[...]).astype(BF16)
        dw_ref[1] = both[:, :width]
        dw_ref[2] = both[:, width:]
        dw_ref[3] = nn(ot[...], dab[...]).astype(BF16)
        dxq = dr_ref[...] + nt(grads_q[...], w_all[:, :width])
        dxk = nt(grads_k[...], w_all[:, width:])
        if same:
            outs[0][...] = dxq + dxk
            if n_send:
                send[0][...] = other_half(place_ref, outs[0])
        else:
            for n, value in enumerate((dxq, dxk)):
                if n < norms:
                    gain = row_of(n_refs[2 * n + 1], gains[n])
                    value, dg_refs[n][...] = norm_back(n_refs[2 * n][...], gain, value)
                outs[n][...] = value

    w.store(place, [dw_ref], dw_outs, last)


def attn_backward(same, length, dr, w, plain, q, k, v, o, qx, xs, norms=()):
    rows, width = dr.shape
    count = k.shape[0]
    sds = jax.ShapeDtypeStruct
    pair_of = lambda n: pl.BlockSpec((n, PAIR), lambda i: (0, i))
    once = lambda shape, index=None: pl.BlockSpec(
        shape, lambda i: index or (0,) * len(shape), pipeline_mode=pl.Buffered(1))
    in_specs = [
        smem(), smem(), once((rows, width)), once((1, width, width), (3, 0, 0)),
        pl.BlockSpec((1, width, width), lambda i: (jnp.minimum(i, 2), 0, 0)),
        pair_of(rows), pair_of(count), pair_of(count), pair_of(rows),
        once((rows, PAIR)),
    ] + [pair_of(x.shape[0]) for x in xs]
    norm_args = []
    for r, g in norms:
        norm_args += [r, g[0]]
        in_specs += [once(r.shape), once(g[0].shape)]
    outs = [sds((rows, width), F32)]
    if not same:
        outs += [sds((count, width), F32)] + [sds((1, width), F32)] * len(norms)
    elif w.packed:
        outs.append(sds((rows // 2, width), F32))
    outs += w.grad_shapes()
    vm = pltpu.VMEM
    return pl.pallas_call(
        functools.partial(attn_bwd_kernel, [g[1] for _, g in norms], same, w),
        grid=(H // 2,),
        in_specs=in_specs + [smem()] * len(w.place()),
        out_specs=[whole(s.shape) for s in outs],
        out_shape=outs,
        scratch_shapes=[
            vm((rows, width), BF16), vm((H // 2, rows, PAIR), BF16),
            vm((count, 2 * PAIR), BF16), vm((count, 2 * PAIR), BF16),
            vm((2, rows, 2 * PAIR), BF16), vm((2, rows, 2 * PAIR), BF16), vm((PAIR, count), BF16), vm((width, rows), BF16),
            vm((PAIR, rows), F32), vm((rows, width), BF16), vm((count, 2 * width), BF16), vm((width, 3 * width), BF16),
        ] + [vm((width, x.shape[0]), BF16) for x in xs] + w.grad_scratch(),
        compiler_params=PARAMS,
        cost_estimate=cost(rows * count * 9 * 512 * H, 20 << 20, rows * count * H),
        name="self_bwd" if same else "cross_bwd",
    )(*length, dr, plain, plain, q, k, v, o, qx, *xs, *norm_args, *w.place())


def attn_grads_kernel(w, len_ref, place_ref, dr_ref, w3_ref, q_ref, k_ref, v_ref, o_ref, qx_ref, x_ref, grads_ref, *refs):
    dw_outs, (dab, do_s, kaug, vaug, qaug, oaug, kt, ot, xt, dqt), (dw_ref,) = cut(refs, 2, 10, 1)
    count = kaug.shape[0]
    width = dab.shape[1]
    p = pl.program_id(0)

    @pl.when(p == 0)
    def _():
        dab[...] = dr_ref[...].astype(BF16)
        kaug[:, PAIR:] = key_extras(len_ref[place_ref[3]], count)
        vaug[:, PAIR:] = jnp.ones((count, PAIR), BF16)
        do = nt(dab[...], w3_ref[0]).astype(BF16)
        for n in range(H // 2):
            do_s[n] = do[:, n * PAIR:(n + 1) * PAIR]

    own = pl.ds(pl.multiple_of(p * PAIR, PAIR), PAIR)
    part = lambda n: pl.ds(pl.multiple_of(n * width + p * PAIR, PAIR), PAIR)
    o, do = o_ref[...], do_s[p]
    ot[own, :] = o.T
    xt[own, :] = x_ref[...].T
    for keys, dk, dv in pair_back(p, k_ref, v_ref, q_ref, qx_ref, o, do, kaug, vaug, qaug, oaug, kt, dqt):
        grads_ref[keys, part(1)] = dk
        grads_ref[keys, part(2)] = dv
    grads_ref[:, part(0)] = (dqt[...].T * 0.125).astype(BF16)
    last = p == pl.num_programs(0) - 1

    @pl.when(last)
    def _():
        dw = nn(xt[...], grads_ref[...]).astype(BF16)
        for n in range(3):
            dw_ref[n] = dw[:, n * width:(n + 1) * width]
        dw_ref[3] = nn(ot[...], dab[...]).astype(BF16)

    w.store([place_ref], [dw_ref], dw_outs, last)


def attn_grads(length, dr, w, plain, q, k, v, o, qx, x):
    rows, width = dr.shape
    sds = jax.ShapeDtypeStruct
    vm = pltpu.VMEM
    once = lambda shape, index=None: pl.BlockSpec(
        shape, lambda i: index or (0,) * len(shape), pipeline_mode=pl.Buffered(1))
    pair = pl.BlockSpec((rows, PAIR), lambda i: (0, i))
    outs = [sds((rows, 3 * width), BF16)] + w.grad_shapes()
    return pl.pallas_call(
        functools.partial(attn_grads_kernel, w),
        grid=(H // 2,),
        in_specs=[smem(), smem(), once((rows, width)), once((1, width, width), (3, 0, 0))] + [pair] * 4
        + [once((rows, PAIR)), pair],
        out_specs=[whole(x.shape) for x in outs],
        out_shape=outs,
        scratch_shapes=[
            vm((rows, width), BF16), vm((H // 2, rows, PAIR), BF16), vm((rows, 2 * PAIR), BF16), vm((rows, 2 * PAIR), BF16),
            vm((2, rows, 2 * PAIR), BF16), vm((2, rows, 2 * PAIR), BF16), vm((PAIR, rows), BF16), vm((width, rows), BF16),
            vm((width, rows), BF16), vm((PAIR, rows), F32),
        ] + w.grad_scratch(),
        compiler_params=PARAMS,
        cost_estimate=cost(rows * rows * 9 * 512 * H, 14 << 20, rows * rows * H),
        name="grads_bwd",
    )(*length, dr, plain, q, k, v, o, qx, x)


def input_grad_kernel(place_ref, dr_ref, grads_ref, *refs):
    *w_refs, out_ref, send_ref = refs
    out_ref[...] = dr_ref[...] + nt(grads_ref[...], jnp.concatenate([w[0] for w in w_refs], axis=1))

    @pl.when(pl.program_id(0) != place_ref[2])
    def _():
        send_ref[...] = out_ref[...]


def input_grad(place, dr, grads, plain):
    rows, width = dr.shape
    blk = rows // SEQ
    by_rows = lambda x: pl.BlockSpec((blk, x.shape[1]), lambda i: (i, 0))
    matrix = lambda n: pl.BlockSpec((1, width, width), lambda i: (n, 0, 0))
    return pl.pallas_call(
        input_grad_kernel,
        grid=(rows // blk,),
        in_specs=[smem(), by_rows(dr), by_rows(grads)] + [matrix(n) for n in range(3)],
        out_specs=[by_rows(dr), whole((blk, width))],
        out_shape=[jax.ShapeDtypeStruct(dr.shape, F32), jax.ShapeDtypeStruct((blk, width), F32)],
        compiler_params=PARAMS,
        cost_estimate=cost(6 * rows * width * width, 9 << 20),
        name="input_grad",
    )(place, dr, grads, plain, plain, plain)


def gelu_parts(u):
    phi = 0.5 + 0.5 * lax.erf(u * math.sqrt(0.5))
    return u * phi, phi + u * jnp.exp2(u * u * (-0.5 * LOG2E)) * (1.0 / math.sqrt(2.0 * math.pi))


def ffn_fwd_kernel(gain, steps, w, *refs):
    (r_ref, g_ref), w_refs, (h_ref, a_ref, d_ref, out_ref), plain, w_scr = cut(
        refs, 2, w.n_args(), 4, w.n_scratch(), w.n_scratch())
    up_ref, down_ref = w.load(w_refs, w_scr, pl.program_id(0) == 0)
    w.plain_store(plain, w_scr, steps)
    hidden = norm(r_ref[...], row_of(g_ref, gain))
    low = hidden.astype(BF16)
    h_ref[...] = low
    total = hidden
    span = up_ref.shape[2]
    for c in range(up_ref.shape[0]):
        cols = slice(c * span, (c + 1) * span)
        act, slope = gelu_parts(nn(low, up_ref[c]))
        act = act.astype(BF16)
        a_ref[:, cols] = act
        d_ref[:, cols] = slope.astype(BF16)
        total = total + nn(act, down_ref[0, cols, :])
    out_ref[...] = total


def ffn_forward(r, gain, w):
    rows, width = r.shape
    inner = w.shapes[1][1]
    blk = math.gcd(rows, 512)
    steps = rows // blk
    sds = jax.ShapeDtypeStruct
    by_rows = lambda n: pl.BlockSpec((blk, n), lambda i: (i, 0))
    out = pl.pallas_call(
        functools.partial(ffn_fwd_kernel, gain[1], steps, w),
        grid=(steps,),
        in_specs=[by_rows(width), whole(gain[0].shape)] + w.specs(1),
        out_specs=[by_rows(width), by_rows(inner), by_rows(inner), by_rows(width)] + w.plain_specs(steps),
        out_shape=[sds((rows, width), BF16), sds((rows, inner), BF16), sds((rows, inner), BF16), sds((rows, width), F32)]
        + w.plain_shapes(),
        scratch_shapes=w.scratch(),
        compiler_params=PARAMS,
        cost_estimate=cost(12 * rows * width * inner, 17 << 20, rows * inner * 2),
        name="ffn_fwd",
    )(r, gain[0], *w.args())
    return out if w.packed else [*out, *w.arrays]


def ffn_bwd_kernel(gain, w, kind, *refs):
    n_more = {"none": 0, "slot": 2, "gains": 4}[kind]
    (dr_ref, h_ref, a_ref, d_ref, r_ref, g_ref, up_ref, down_ref), more, place, (dout_ref, dg_ref), dw_outs, \
        (low, ht, acc, r_s), dw_scr = cut(refs, 8, n_more, len(w.place()), 2, 2, 4, w.n_scratch())
    n = pl.program_id(0)
    dup_ref, ddown_ref = dw_scr if w.packed else dw_outs

    @pl.when(n == 0)
    def _():
        grad = dr_ref[...]
        acc[...] = grad
        low[...] = grad.astype(BF16)
        ht[...] = h_ref[...].T

    grad = low[...]
    some = r_ref.shape[0]
    r_s[pl.ds(pl.multiple_of(n * some, some), some), :] = r_ref[...]
    span = up_ref.shape[2]
    rows = pl.ds(pl.multiple_of(n * span, span), span)
    ddown_ref[0, rows, :] = tn(a_ref[...], grad).astype(BF16)
    du = (nt(grad, down_ref[0]) * d_ref[...].astype(F32)).astype(BF16)
    dup_ref[n] = nn(ht[...], du).astype(BF16)
    acc[...] += nt(du, up_ref[0])
    last = n == pl.num_programs(0) - 1

    @pl.when(last)
    def _():
        dout_ref[...], dg_ref[...] = norm_back(r_s[...], row_of(g_ref, gain), acc[...])

    w.store(place, [dup_ref, ddown_ref], dw_outs, last)
    if not w.packed or kind == "none":
        return
    at = sum(w.share(s) for s in w.shapes)

    @pl.when(last)
    def _():
        if kind == "slot":
            for src, dst in zip(more, dw_outs):
                dst[:, :, at:, :] = src[...]
        else:
            gains = [dg_ref] + list(more)
            row = lax.broadcasted_iota(jnp.int32, (16, dg_ref.shape[1]), 0)
            block = jnp.zeros((16, dg_ref.shape[1]), F32)
            for x, ref in enumerate(gains):
                block = jnp.where(row == x, ref[...], block)
            block = block.astype(BF16)
            for dst in dw_outs:
                for j in range(INNER):
                    for k in range(w.outer):
                        dst[j, k, at:, :] = block


def ffn_backward(dr, hidden, act, slope, w, plain, r, gain, kind="none", more=()):
    rows, width = dr.shape
    inner = w.shapes[1][1]
    span = inner // w.shapes[0][0]
    steps = inner // span
    sds = jax.ShapeDtypeStruct
    once = lambda shape: pl.BlockSpec(shape, lambda i: (0,) * len(shape), pipeline_mode=pl.Buffered(1))
    by_cols = pl.BlockSpec((rows, span), lambda i: (0, i))
    extra = {"none": 0, "slot": more[0].shape[2] if kind == "slot" else 0, "gains": 16}[kind] if w.packed else 0
    if not w.packed:
        kind, more = "none", ()
    grads = w.grad_shapes(extra)
    return pl.pallas_call(
        functools.partial(ffn_bwd_kernel, gain[1], w, kind),
        grid=(steps,),
        in_specs=[once((rows, width)), once((rows, width)), by_cols, by_cols,
                  pl.BlockSpec((rows // steps, width), lambda i: (i, 0)), once(gain[0].shape),
                  pl.BlockSpec((1, width, span), lambda i: (i, 0, 0)), pl.BlockSpec((1, span, width), lambda i: (0, i, 0))]
        + [once(x.shape) for x in more] + [smem()] * len(w.place()),
        out_specs=[whole((rows, width)), whole((1, width))] + [whole(s.shape) for s in grads],
        out_shape=[sds((rows, width), F32), sds((1, width), F32)] + grads,
        scratch_shapes=[pltpu.VMEM((rows, width), BF16), pltpu.VMEM((width, rows), BF16), pltpu.VMEM((rows, width), F32),
                        pltpu.VMEM((rows, width), F32)] + w.grad_scratch(),
        compiler_params=PARAMS,
        cost_estimate=cost(16 * rows * width * inner, 25 << 20),
        name="ffn_bwd",
    )(dr, hidden, act, slope, r, gain[0], *plain, *more, *w.place())


def slot_kernel(gain, w, halo, *refs):
    n_grad = 2 if w.packed else 1
    n_join = n_grad - 1
    (len_ref, place_ref, r_ref, g_ref, cot_ref), other, halo_refs, w_refs, (out_ref, dr_ref, dg_ref), send, dw_outs, \
        w_scr, dw_scr, joined = cut(
            refs, 5, n_join, 3 if halo else 0, w.n_args(), 3, n_join, n_grad, w.n_scratch(), w.n_scratch(), n_join)
    if other:
        join(place_ref, cot_ref, other[0], joined[0])
        cot_ref = joined[0]
    length = len_ref[place_ref[3]]
    w_ref, = w.load(w_refs, w_scr, length >= 0)
    dw_ref, = dw_scr if w.packed else dw_outs
    rows, width = r_ref.shape
    gain = row_of(g_ref, gain)
    low = norm(r_ref[...], gain).astype(BF16)
    row = lax.broadcasted_iota(jnp.int32, (rows, width), 0)
    above = below = 0.0
    place = row
    if halo:
        base_ref, next_ref, prev_ref = halo_refs
        place = row + base_ref[0]
        after = norm(next_ref[...], gain).astype(BF16)
        above = nn(after, w_ref[0, width:, :])[:1, :] * base_ref[1].astype(F32)
        below = jnp.where(base_ref[0] - 1 < length - 1, prev_ref[...].astype(F32)[:1, :], 0.0)
    live = place < length - 1
    second = nn(low, w_ref[0, width:, :])
    shifted = jnp.where(row == rows - 1, above, pltpu.roll(second, rows - 1, 0))
    out_ref[...] = jnp.where(live, nn(low, w_ref[0, :width, :]) + shifted, 0.0).astype(BF16)
    if send:
        send[0][...] = other_half(place_ref, out_ref)
    g = jnp.where(live, cot_ref[...].astype(F32), 0.0)
    before = jnp.where(row == 0, below, pltpu.roll(g, 1, 0)).astype(BF16)
    g = g.astype(BF16)
    low_t = low.T
    dw_ref[0, :width, :] = nn(low_t, g).astype(BF16)
    dw_ref[0, width:, :] = nn(low_t, before).astype(BF16)
    dy = nt(g, w_ref[0, :width, :]) + nt(before, w_ref[0, width:, :])
    dr_ref[...], dg_ref[...] = norm_back(r_ref[...], gain, dy)
    w.store(w_refs[:1], [dw_ref], dw_outs, length >= 0)


def slot_step(length, r, gain, w, cot, halo):
    rows, width = r.shape
    sds = jax.ShapeDtypeStruct
    grads = w.grad_shapes()
    full = lambda x: pl.BlockSpec(x.shape, lambda i: (0,) * len(x.shape))
    outs = [sds((rows, width), BF16), sds((rows, width), F32), sds((1, width), F32)]
    outs += ([sds((rows // 2, width), BF16)] if w.packed else []) + grads
    return pl.pallas_call(
        functools.partial(slot_kernel, gain[1], w, len(halo) > 0),
        grid=(1,),
        in_specs=[smem(), smem()] + [full(x) for x in (r, gain[0], *cot)] + [smem(), *map(full, halo[1:])][:len(halo)] + w.specs(1),
        out_specs=[full(x) for x in outs],
        out_shape=outs,
        scratch_shapes=w.scratch() + w.grad_scratch() + ([pltpu.VMEM((rows, width), BF16)] if w.packed else []),
        compiler_params=PARAMS,
        cost_estimate=cost(36 * rows * width * width, 9 << 20),
        name="slot",
    )(*length, r, gain[0], *cot, *halo, *w.args())


def turn_kernel(g_in, g_out, wf, ws, *refs):
    (len_ref, place_ref, r_ref, g_ref, cot_ref, other_ref), f_refs, s_refs, \
        (out_ref, send_ref, dr_ref, dg_in_ref, dg_out_ref), dw_outs, (h_s, a_s, d_s, r_s, acc, cot_s), \
        f_scr, s_scr, f_dw, s_dw = cut(
            refs, 6, wf.n_args(), ws.n_args(), 5, 2, 6, wf.n_scratch(), ws.n_scratch(), wf.n_scratch(), ws.n_scratch())
    length = len_ref[place_ref[3]]
    always = length >= 0
    up_ref, down_ref = wf.load(f_refs, f_scr, always, True)
    slot_ref, = ws.load(s_refs, s_scr, always, True)
    join(place_ref, cot_ref, other_ref, cot_s)
    rows, width = r_ref.shape
    span = up_ref.shape[2]
    blk = math.gcd(rows, 512)
    for b in range(rows // blk):
        part = slice(b * blk, (b + 1) * blk)
        total = norm(r_ref[part, :], row_of(g_ref, g_in))
        low_in = total.astype(BF16)
        h_s[part, :] = low_in
        for c in range(up_ref.shape[0]):
            cols = slice(c * span, (c + 1) * span)
            act, slope = gelu_parts(nn(low_in, up_ref[c]))
            act = act.astype(BF16)
            a_s[part, cols] = act
            d_s[part, cols] = slope.astype(BF16)
            total = total + nn(act, down_ref[0, cols, :])
        r_s[part, :] = total

    gain = row_of(g_ref, g_out)
    row = lax.broadcasted_iota(jnp.int32, (rows, width), 0)
    live = row < length - 1
    rounded = norm(r_s[...], gain).astype(BF16)
    second = nn(rounded, slot_ref[0, width:, :])
    second = jnp.where(row == rows - 1, 0.0, pltpu.roll(second, rows - 1, 0))
    out_ref[...] = jnp.where(live, nn(rounded, slot_ref[0, :width, :]) + second, 0.0).astype(BF16)
    send_ref[...] = other_half(place_ref, out_ref)
    g = jnp.where(live, cot_s[...].astype(F32), 0.0)
    before = jnp.where(row == 0, 0.0, pltpu.roll(g, 1, 0)).astype(BF16)
    g = g.astype(BF16)
    turned = rounded.T
    s_dw[0][0, :width, :] = nn(turned, g).astype(BF16)
    s_dw[0][0, width:, :] = nn(turned, before).astype(BF16)
    dy = nt(g, slot_ref[0, :width, :]) + nt(before, slot_ref[0, width:, :])
    grad, dg_out_ref[...] = norm_back(r_s[...], gain, dy)

    acc[...] = grad
    grad = grad.astype(BF16)
    turned = h_s[...].T
    for c in range(up_ref.shape[0]):
        cols = slice(c * span, (c + 1) * span)
        f_dw[1][0, cols, :] = tn(a_s[:, cols], grad).astype(BF16)
        du = (nt(grad, down_ref[0, cols, :]) * d_s[:, cols].astype(F32)).astype(BF16)
        f_dw[0][c] = nn(turned, du).astype(BF16)
        acc[...] += nt(du, up_ref[c])
    dr_ref[...], dg_in_ref[...] = norm_back(r_ref[...], row_of(g_ref, g_in), acc[...])
    wf.store([place_ref], f_dw, dw_outs, always)

    @pl.when(always)
    def _():
        deal(Spot(place_ref, wf.outer, ws.far[1]), s_dw[0], sum(wf.share(x) for x in wf.shapes), *dw_outs)


def turn(length, r, gain_in, gain_out, wf, ws, halves):
    rows, width = r.shape
    inner = wf.shapes[1][1]
    sds = jax.ShapeDtypeStruct
    vm = pltpu.VMEM
    outs = [sds((rows, width), BF16), sds((rows // 2, width), BF16), sds((rows, width), F32), sds((1, width), F32),
            sds((1, width), F32)] + wf.grad_shapes(sum(ws.share(x) for x in ws.shapes))
    return pl.pallas_call(
        functools.partial(turn_kernel, gain_in[1], gain_out[1], wf, ws),
        in_specs=[smem(), smem()] + [vmem()] * 4 + wf.specs(0) + ws.specs(0),
        out_specs=[vmem() for _ in outs],
        out_shape=outs,
        scratch_shapes=[vm((rows, width), BF16), vm((rows, inner), BF16), vm((rows, inner), BF16), vm((rows, width), F32),
                        vm((rows, width), F32), vm((rows, width), BF16)]
        + wf.scratch() + ws.scratch() + wf.grad_scratch() + ws.grad_scratch(),
        compiler_params=PARAMS,
        cost_estimate=cost(36 * rows * width * inner, 17 << 20, rows * inner * 2),
        name="turn",
    )(*length, r, gain_in[0], *halves, *wf.args(), *ws.args())


def pack_kernel(lane_ref, gains_ref, *refs):
    *ins, first_ref, second_ref = refs
    pieces = []
    for ref in ins:
        if len(ref.shape) == 3:
            pieces += [ref[a] for a in range(ref.shape[0])]
        elif ref.shape[1] > first_ref.shape[1]:
            width = first_ref.shape[1]
            pieces += [ref[:, a * width:(a + 1) * width] for a in range(ref.shape[1] // width)]
        else:
            pieces.append(ref[...])
        if ref is ins[0]:
            count, share = gains_ref.shape
            row = lax.broadcasted_iota(jnp.int32, (share, first_ref.shape[1]), 0)
            lane = lax.broadcasted_iota(jnp.int32, (share, first_ref.shape[1]), 1)
            spread = jnp.where(lane == row + lane_ref[0], 1.0, 0.0).astype(BF16)
            gains = nn(gains_ref[...], spread).astype(BF16)
            pieces.append(jnp.concatenate([gains, jnp.zeros((16 - count, gains.shape[1]), BF16)], axis=0))
    at = 0
    dsts = [first_ref, second_ref]
    for piece in pieces:
        if at == dsts[0].shape[0]:
            at = 0
            dsts.pop(0)
        dst = dsts[0]
        dst[at:at + piece.shape[0], :] = piece
        at += piece.shape[0]


def pack(lane, gains, *groups):
    width = groups[0][0].shape[-1]
    rows = [sum(x.size for x in xs) // width for xs in groups]
    rows[0] += 16
    arrays = [x for xs in groups for x in xs]
    return pl.pallas_call(
        pack_kernel,
        in_specs=[smem()] + [vmem()] * (1 + len(arrays)),
        out_specs=[vmem() for _ in rows],
        out_shape=[jax.ShapeDtypeStruct((n, width), BF16) for n in rows],
        name="pack",
    )(lane, gains, *arrays)


def finish_kernel(shapes, terms, lane_ref, *refs):
    *ins, outs = cut(refs, *terms, len(refs) - sum(terms))
    at_out = 0
    for group, parts in zip(shapes, ins):
        total = summed([x[...] for x in parts])
        at = 0
        for stack, share in group:
            out = outs[at_out]
            width = total.shape[1]
            for a in range(stack):
                rows = total[at:at + share, :]
                at += share
                if len(out.shape) == 3:
                    out[a] = rows
                else:
                    out[:, a * width:(a + 1) * width] = rows
            at_out += 1
        if at < total.shape[0]:
            out = outs[at_out]
            count, share = out.shape
            row = lax.broadcasted_iota(jnp.int32, (width, share), 0)
            lane = lax.broadcasted_iota(jnp.int32, (width, share), 1)
            pick = jnp.where(row == lane + lane_ref[0], 1.0, 0.0).astype(BF16)
            out[...] = nn(total[at:, :].astype(BF16), pick)[:count, :]
            at_out += 1


def finish(lane, shapes, sums, more, outs):
    groups = [[x] for x in sums] + more
    arrays = [x for g in groups for x in g]
    return pl.pallas_call(
        functools.partial(finish_kernel, shapes, [len(g) for g in groups]),
        in_specs=[smem()] + [vmem()] * len(arrays),
        out_specs=[vmem() for _ in outs],
        out_shape=[jax.ShapeDtypeStruct(s, F32) for s in outs],
        name="finish",
    )(lane, *arrays)


def exchange(x, send, *during):
    count = x.shape[0]
    me = lax.axis_index("seq")
    out = x
    for k in range(1, count):
        piece = lax.dynamic_index_in_dim(x, (me + k) % count, 0, keepdims=False) if send is None else send
        piece = hold(lax.ppermute(piece, "seq", [(s, (s + k) % count) for s in range(count)]), *during)
        out = lax.dynamic_update_index_in_dim(out, piece, (me - k) % count, 0)
    return out


def to_examples(x, count):
    examples, rows, width = x.shape
    if count == examples:
        return exchange(x, None).reshape(count * rows, width)
    me = lax.axis_index("seq")
    group = count // examples
    all_rows = lax.all_gather(x, "seq", axis=1, tiled=True)
    one = lax.dynamic_index_in_dim(all_rows, me // group, 0, keepdims=False)
    return lax.dynamic_slice_in_dim(one, (me % group) * examples * rows, examples * rows, 0)


def to_positions(x, examples, count, *during, send=None):
    width = x.shape[1]
    if count == examples:
        return exchange(x.reshape(count, -1, width), send, *during)
    me = lax.axis_index("seq")
    rows = x.shape[0] // examples
    all_rows = lax.all_gather(x, "seq", axis=0, tiled=True).reshape(examples, count * rows, width)
    return lax.dynamic_slice_in_dim(all_rows, me * rows, rows, 1)


class Ring:
    def __init__(self):
        self.dp = lax.axis_size("dp")
        self.outer = self.dp // INNER
        self.columns = [[o * INNER + i for o in range(self.outer)] for i in range(INNER)]
        self.planes = [[o * INNER + i for i in range(INNER)] for o in range(self.outer)]

    def inner_step(self, x, j):
        return lax.ppermute(x, "dp", [(d, d // INNER * INNER + (d + j) % INNER) for d in range(self.dp)])

    def outer_step(self, x, k):
        return lax.ppermute(x, "dp", [(d, (d + k * INNER) % self.dp) for d in range(self.dp)])

    def swap(self, x):
        return lax.ppermute(x, "seq", [(0, 1), (1, 0)])

    def column(self, shard, *during):
        return [shard] + [hold(self.outer_step(shard, k), *during) for k in range(1, self.outer)]

    def plane(self, column, *during):
        return [column] + [hold(self.inner_step(column, j), *during) for j in range(1, INNER)]

    def far_column(self, x):
        return lax.all_gather(x, "dp", axis=0, axis_index_groups=self.columns)

    def both(self, plane):
        return plane + [self.swap(x) for x in plane]

    def pairs(self, keep, send, *during):
        other = hold(self.swap(send), *during)
        return [keep[j] + other[j] for j in range(INNER)]

    def across(self, pairs, *during):
        return low(summed([pairs[0]] + [hold(self.inner_step(pairs[j], j), *during) for j in range(1, INNER)]))

    def pair(self, keep, send):
        return keep + self.swap(send)

    def plane_sum(self, pair):
        return lax.psum_scatter(pair, "dp", scatter_dimension=0, axis_index_groups=self.planes)

    def far_sum(self, total):
        return lax.psum_scatter(total, "dp", scatter_dimension=0, axis_index_groups=self.columns)

    def near_sum(self, total):
        return [total[0]] + [self.outer_step(total[k], k) for k in range(1, self.outer)]


def low(x):
    return x.astype(BF16)


def summed(parts):
    return sum(x.astype(F32) for x in parts)


def hold(x, *after):
    return lax.optimization_barrier((x, after))[0]


def per_device(source, canvas, source_len, canvas_len, cotangent, enc_attn, enc_up, enc_down, dec_attn, cross_attn,
               dec_up, dec_down, slot_proj, norm_gains):
    examples, _, width = source.shape
    seq = lax.axis_size("seq")
    devices = lax.axis_size("dp") * seq
    group = seq // examples
    me = lax.axis_index("seq")
    rank = lax.axis_index("dp") * seq + me
    groups = [[e * group + t for t in range(group)] for e in range(examples)]
    packed = seq == SEQ and lax.axis_size("dp") % INNER == 0 and enc_up.shape[0] % 16 == 0

    def whole_keys(x):
        return lax.all_gather(x, "seq", axis=0, tiled=True, axis_index_groups=groups) if group > 1 else x

    def own_keys(x):
        if group == 1:
            return x
        return lax.psum_scatter(x, "seq", scatter_dimension=0, tiled=True, axis_index_groups=groups)

    def neighbour(x, step):
        pairs = [(s, s + step) for s in range(seq) if 0 <= s % group + step < group]
        return lax.ppermute(x, "seq", pairs)

    def chunks(up):
        rows = up.shape[0]
        return up.reshape(rows, -1, width).transpose(1, 0, 2)

    def unchunk(up):
        return up.transpose(1, 0, 2).reshape(up.shape[1], -1)

    shards = {
        "enc": enc_attn, "dec": dec_attn, "cross": cross_attn, "eup": chunks(enc_up), "edown": enc_down[None],
        "dup": chunks(dec_up), "ddown": dec_down[None], "slot": slot_proj[None],
    }
    shapes = {name: (x.shape[0], x.shape[1] * devices, width) for name, x in shards.items()}
    flat = lambda name: shards[name].reshape(-1, width)
    dp_index = lax.axis_index("dp")
    spot = jnp.stack([dp_index // INNER, dp_index % INNER, me, me // group]).astype(jnp.int32)
    if packed:
        ring = Ring()
        share = norm_gains.shape[1]
        lane = jnp.reshape(rank * share, (1,)).astype(jnp.int32)
        late, flat5 = pack(
            lane, norm_gains, [dec_attn, enc_up, enc_down, cross_attn, slot_proj], [dec_up, dec_down])
        names = ["eup", "edown", "cross", "slot", "dup", "ddown"]
        sizes = [shapes[n][0] * shapes[n][1] // devices for n in names[:4]]
        late = ring.far_column(late)
        x5 = ring.plane(flat5)
        z1 = jnp.stack(hold(ring.column(flat("enc")), *x5))
        g1 = ring.plane(z1)
        source, canvas, cotangent = hold((source, canvas, cotangent), z1)
        late = hold(late, *g1)
        x5 = ring.far_column(jnp.stack(hold(x5, *g1)))
        g1 = ring.both(g1)
        cuts = [shapes["dec"][0] * shapes["dec"][1] // devices + 16]
        cuts.append(cuts[0] + sum(sizes[:2]))
        late = [late[:, :cuts[0]], late[:, cuts[0]:cuts[1]], late[:, cuts[1]:]]

        def make(arrays, names, far=(1, 1), **more):
            return Weights(True, arrays, [shapes[n] for n in names], spot=spot, outer=ring.outer, far=far, **more)

        w_enc = make(g1, ["enc"], (0, 0))

        def fetch_dec(during):
            return make(ring.both(ring.plane(late[0], during)), ["dec"], (1, 0), tail=16)

        def fetch_effn(before, during):
            return make(ring.both(ring.plane(hold(late[1], before), during)), ["eup", "edown"])

        def fetch_cross_slot(before, during):
            arrays = ring.both(ring.plane(hold(late[2], before), during))
            return make(arrays, ["cross"]), make(arrays, ["slot"], (1, 2), at=sizes[2])

        def fetch_dffn(before, during):
            return make([x5, hold(ring.swap(hold(x5, before)), during)], ["dup", "ddown"], (1, 2), block=True)
    else:
        def fetch(*names):
            return Weights(False, [lax.all_gather(shards[n], ("dp", "seq"), axis=1, tiled=True) for n in names],
                           [shapes[n] for n in names])
        w_enc = fetch("enc")
        fetch_dec = lambda *t: fetch("dec")
        fetch_effn = lambda *t: fetch("eup", "edown")
        fetch_cross_slot = lambda *t: (fetch("cross"), fetch("slot"))
        fetch_dffn = lambda *t: fetch("dup", "ddown")
        gains = lax.all_gather(norm_gains, ("dp", "seq"), axis=1, tiled=True).astype(F32)
    s_len, c_len = (source_len, spot), (canvas_len, spot)
    if packed:
        def halves(x):
            return x, ring.swap(lax.dynamic_index_in_dim(x, 1 - me, 0, keepdims=False))
        src, can, cot = halves(source), halves(canvas), halves(cotangent)
        src = attn_forward(s_len, w_enc, halves=src)
    else:
        src, can, cot = (to_examples(x, seq) for x in (source, canvas, cotangent))
        src_all, can_all = whole_keys(src), whole_keys(can)
        src = [src, *attn_forward(s_len, w_enc, xq=src, xk=src_all)]
    src, q_a, k_a, v_a, o_a, x_a, r_a, p_enc = src
    w_dec = fetch_dec(r_a)
    can = hold(can, r_a)
    if packed:
        can = attn_forward(c_len, w_dec, halves=can)
    else:
        can = [can, *attn_forward(c_len, w_dec, xq=can, xk=can_all)]
    can, q_b, k_b, v_b, o_b, x_b, r_c, *tail, p_dec = can
    gains = tail[0] if packed else gains
    gain = [(gains, i) for i in range(5)]
    w_effn = fetch_effn(r_a, r_c)
    h_a, act_a, slope_a, r_b, *p_effn = ffn_forward(hold(r_a, r_c), gain[0], w_effn)
    w_cross, w_slot = fetch_cross_slot(r_c, r_b)
    low_one, low_enc, q_c, k_c, v_c, o_c, x_c, r_d, p_cross = attn_forward(
        s_len, w_cross, rq=r_c, rk=whole_keys(r_b), gq=gain[2], gk=gain[1])
    w_dffn = fetch_dffn(r_b, r_d)
    if packed:
        slot_out, slot_send, dr, dg3, dg4, *d_dffn = turn(c_len, r_d, gain[3], gain[4], w_dffn, w_slot, cot)
    else:
        h_b, act_b, slope_b, r_e, *p_dffn = ffn_forward(r_d, gain[3], w_dffn)
        halo = []
        if group > 1:
            place = jnp.stack([me % group * r_e.shape[0], me % group < group - 1]).astype(jnp.int32)
            halo = [place, neighbour(r_e[:8], -1), neighbour(cot[-8:][::-1], 1)]
        slot_out, dr, dg4, *d_slot = slot_step(c_len, r_e, gain[4], w_slot, [cot], halo)
        slot_send = None
        dr, dg3, *d_dffn = ffn_backward(dr, h_b, act_b, slope_b, w_dffn, p_dffn, r_d, gain[3], "slot", d_slot)
    slot_out = to_positions(slot_out, examples, seq, send=slot_send)
    if packed:
        p1 = ring.pair(*d_dffn)
        dr = hold(dr, p1)
    alone = group == 1
    norms = [(r_c, gain[2])] + ([(r_b, gain[1])] if alone else [])
    dr_c, dr_b, dg2, *rest = attn_backward(
        False, s_len, dr, w_cross, p_cross, q_c, k_c, v_c, o_c, x_c, (low_one, low_enc), norms)
    if alone:
        dg1, *d_cross = rest
    else:
        d_cross = rest
        dr_b, dg1 = norm_back(r_b, gains[1:2], own_keys(dr_b))
    if packed:
        s1 = ring.plane_sum(p1)
        dr_b = hold(dr_b, slot_out)
    dr_a, dg0, *d_effn = ffn_backward(
        dr_b, h_a, act_a, slope_a, w_effn, p_effn, r_a, gain[0], "gains", [dg1, dg2, dg3, dg4])
    if packed:
        p2 = ring.pairs(*d_cross, dr_a)
        p3 = ring.pairs(*hold(tuple(d_effn), *p2))
        dr_c = hold(dr_c, *p3)
        z1 = ring.far_sum(s1)
    sides = 1 if alone else 2
    out = attn_backward(alone, c_len, dr_c, w_dec, p_dec, q_b, k_b, v_b, o_b, x_b, [can, can if alone else can_all][:sides])
    d_can, d_dec = out[:sides], list(out[sides:])
    can_send = d_dec.pop(0) if packed else None
    canvas_grad = d_can[0] if alone else d_can[0] + own_keys(d_can[1])
    if packed:
        s2 = ring.across(p2, canvas_grad)
        s3 = ring.across(p3, canvas_grad)
        p4 = ring.pairs(*hold(tuple(d_dec), s2, s3, z1))
        dr_a = hold(dr_a, *p4)
        z23 = ring.far_sum(jnp.concatenate([s2, s3], axis=1))
        grads, *d_enc = attn_grads(s_len, dr_a, w_enc, p_enc, q_a, k_a, v_a, o_a, x_a, src)
        canvas_grad = to_positions(canvas_grad, examples, seq, grads, send=can_send)
        s4 = ring.across(p4, grads)
        d_enc = hold(tuple(d_enc), s4, z23)
        source_grad, source_send = input_grad(spot, dr_a, grads, p_enc)
        z4 = ring.near_sum(s4)
        p5 = ring.pairs(*d_enc, source_grad, *z4[1:])
        source_grad = to_positions(source_grad, examples, seq, send=hold(source_send, *p5))
        groups = [("dup", "ddown", "slot"), ("cross", "eup", "edown"), ("dec",), ("enc",)]
        rows_of = [[(shards[n].shape[0], shards[n].shape[1]) for n in names] for names in groups]
        like = {"enc": enc_attn, "eup": enc_up, "edown": enc_down, "dec": dec_attn, "cross": cross_attn, "dup": dec_up,
                "ddown": dec_down, "slot": slot_proj}
        outs = [like[n].shape for n in groups[0] + groups[1]] + [norm_gains.shape, dec_attn.shape, enc_attn.shape]
        done = finish(lane, rows_of[:2], hold([z1, z23], *p5), [], outs[:7])
        s5 = ring.across(p5, source_grad, canvas_grad, done[2])
        z5 = ring.near_sum(s5)
        t_dup, t_ddown, t_slot, t_cross, t_eup, t_edown, t_gains = done
        t_dec, t_enc = finish(lane, rows_of[2:], [], [z4, z5], outs[7:])
    else:
        def home(x):
            return lax.psum_scatter(x, ("dp", "seq"), scatter_dimension=1, tiled=True).astype(F32)
        t_dec, t_cross = home(d_dec[0]), home(d_cross[0])
        t_eup, t_edown, t_dup, t_ddown, t_slot = (home(x) for x in (*d_effn, *d_dffn, *d_slot))
        t_eup, t_edown, t_dup, t_ddown, t_slot = unchunk(t_eup), t_edown[0], unchunk(t_dup), t_ddown[0], t_slot[0]
        out = attn_backward(alone, s_len, dr_a, w_enc, p_enc, q_a, k_a, v_a, o_a, x_a, [src, src if alone else src_all][:sides])
        d_src, d_enc = out[:sides], out[sides:]
        source_grad = d_src[0] if alone else d_src[0] + own_keys(d_src[1])
        t_enc = home(d_enc[0])
        t_gains = home(jnp.concatenate([dg0, dg1, dg2, dg3, dg4], axis=0))
        source_grad = to_positions(source_grad, examples, seq)
        canvas_grad = to_positions(canvas_grad, examples, seq)

    return (
        slot_out, source_grad, canvas_grad,
        t_enc, t_eup, t_edown, t_dec, t_cross, t_dup, t_ddown, t_slot, t_gains,
    )


def solution(mesh):
    by_seq = P("dp", "seq", None)
    stack = P(None, ("dp", "seq"), None)
    by_row = P(("dp", "seq"), None)
    gains = P(None, ("dp", "seq"))
    in_specs = (by_seq, by_seq, P("dp"), P("dp"), by_seq, stack, by_row, by_row, stack, stack, by_row, by_row, by_row,
                gains)
    out_specs = (by_seq, by_seq, by_seq, stack, by_row, by_row, stack, stack, by_row, by_row, by_row, gains)
    return jax.shard_map(per_device, mesh=mesh, in_specs=in_specs, out_specs=out_specs, check_vma=False)
```

```python
import functools
import math

import jax
import jax.numpy as jnp
from jax import lax
from jax.experimental import pallas as pl
from jax.experimental.pallas import tpu as pltpu
from jax.sharding import PartitionSpec as P

F32 = jnp.float32
BF16 = jnp.bfloat16
H = 8
HD = 64
PAIR = 2 * HD
LOG2E = math.log2(math.e)
Q_SCALE = LOG2E / 8.0
K_BACK = 1.0 / LOG2E
MASKED = -1e30
VMEM_LIMIT = 58 * 1024 * 1024
PARAMS = pltpu.CompilerParams(vmem_limit_bytes=VMEM_LIMIT)


def nn(a, b):
    return lax.dot_general(a, b, (((1,), (0,)), ((), ())), preferred_element_type=F32)


def nt(a, b):
    return lax.dot_general(a, b, (((1,), (1,)), ((), ())), preferred_element_type=F32)


def tn(a, b):
    return lax.dot_general(a, b, (((0,), (0,)), ((), ())), preferred_element_type=F32)


def norm_parts(r):
    centre = r - jnp.mean(r, axis=-1, keepdims=True)
    rs = lax.rsqrt(jnp.mean(centre * centre, axis=-1, keepdims=True) + 1e-5)
    return centre * rs, rs


def norm(r, gain):
    return norm_parts(r)[0] * gain


def norm_back(r, gain, dy):
    z, rs = norm_parts(r)
    t = dy * gain
    dr = (t - jnp.mean(t, axis=-1, keepdims=True) - z * jnp.mean(t * z, axis=-1, keepdims=True)) * rs
    return dr, jnp.sum(dy * z, axis=0, keepdims=True)


def lanes(rows):
    return lax.broadcasted_iota(jnp.int32, (rows, PAIR), 1)


def key_extras(length, count):
    row = lax.broadcasted_iota(jnp.int32, (count, PAIR), 0)
    lane = lanes(count)
    bias = jnp.where(row < length, 0.0, MASKED)
    return jnp.where(lane == 3 * H, bias, jnp.where(lane < 3 * H, 1.0, 0.0)).astype(BF16)


def spread_parts(v):
    high = v.astype(BF16).astype(F32)
    rest = v - high
    middle = rest.astype(BF16).astype(F32)
    parts = high + pltpu.roll(middle, H, 1) + pltpu.roll(rest - middle, 2 * H, 1)
    return jnp.where(lanes(v.shape[0]) == 3 * H, 1.0, parts).astype(BF16)


def parts_of(parts, head):
    lane = lanes(parts.shape[0])
    mine = (lane == 3 * H) | ((lane < 3 * H) & ((lane & (H - 1)) == head))
    return jnp.where(mine, parts, 0.0)


def row_of(ref, row):
    return ref[row:row + 1, :]


def whole(shape):
    return pl.BlockSpec(shape, lambda i: (0,) * len(shape))


def smem():
    return pl.BlockSpec(memory_space=pltpu.SMEM)


def vmem():
    return pl.BlockSpec(memory_space=pltpu.VMEM)


def cost(flops, nbytes, exps=0):
    return pl.CostEstimate(flops=int(flops), bytes_accessed=int(nbytes), transcendentals=int(exps))


INNER = 4
SEQ = 2


class Spot:
    def __init__(self, ref, outer, far):
        self.outer, self.far = outer, far
        self.o, self.i, self.s = ref[0], ref[1], ref[2]

    def owner(self, c, j, k):
        o = k if self.far else lax.rem(self.o - k + self.outer, self.outer)
        i = j if self.far > 1 else lax.rem(self.i - j + INNER, INNER)
        return (o * INNER + i) * SEQ + lax.rem(self.s - c + SEQ, SEQ)

    def ahead(self, o, i):
        return (i if self.far > 1 else lax.rem(i - self.i + INNER, INNER),
                o if self.far else lax.rem(o - self.o + self.outer, self.outer))


def assemble(spot, refs, at, dst, block):
    stack, total, _ = dst.shape
    share = total // (spot.outer * INNER * SEQ)
    for c in range(SEQ):
        for j in range(INNER):
            for k in range(spot.outer):
                ref, x = (refs[c], (k, j)) if block else (refs[c * INNER + j], (k,))
                rows = pl.ds(pl.multiple_of(spot.owner(c, j, k) * share, share), share)
                for a in range(stack):
                    dst[a, rows, :] = ref[(*x, slice(at + a * share, at + (a + 1) * share))]


def deal(spot, src, at, keep, send):
    stack, total, _ = src.shape
    share = total // (spot.outer * INNER * SEQ)
    for core in range(SEQ):
        @pl.when(spot.s == core)
        def _():
            for o in range(spot.outer):
                for i in range(INNER):
                    j, k = spot.ahead(o, i)
                    for s in range(SEQ):
                        first = ((o * INNER + i) * SEQ + s) * share
                        dst = keep if s == core else send
                        for a in range(stack):
                            dst[j, k, at + a * share:at + (a + 1) * share, :] = src[a, first:first + share, :]


class Weights:
    def __init__(self, packed, arrays, shapes, at=0, spot=None, outer=0, far=(0, 0), block=False, tail=0):
        self.packed, self.arrays, self.shapes, self.at, self.spot, self.outer = packed, arrays, shapes, at, spot, outer
        self.far, self.block, self.tail = far, block, tail

    def share(self, shape):
        return shape[0] * shape[1] // (self.outer * INNER * SEQ)

    def args(self):
        return [self.spot, *self.arrays] if self.packed else list(self.arrays)

    def specs(self, dims):
        zero = lambda n: (lambda *_: (0,) * n)
        if not self.packed:
            return [pl.BlockSpec(x.shape, zero(3), pipeline_mode=pl.Buffered(1)) if dims else vmem() for x in self.arrays]
        if not dims:
            return [smem()] + [vmem() for _ in self.arrays]
        rows = sum(self.share(s) for s in self.shapes) + self.tail
        index = self.at // rows
        lead = (self.outer, INNER) if self.block else (self.outer,)
        spec = lambda: pl.BlockSpec((*lead, rows, self.shapes[0][2]), lambda *_: (*(0 for _ in lead), index, 0),
                                    **(dict(pipeline_mode=pl.Buffered(1)) if dims else {}))
        return [smem()] + [spec() for _ in self.arrays]

    def scratch(self):
        return [pltpu.VMEM(s, BF16) for s in self.shapes] if self.packed else []

    def n_args(self):
        return len(self.arrays) + 1 if self.packed else len(self.arrays)

    def n_scratch(self):
        return len(self.shapes) if self.packed else 0

    def load(self, refs, scratch, first, entire=False):
        if not self.packed:
            return list(refs)

        @pl.when(first)
        def _():
            spot = Spot(refs[0], self.outer, self.far[0])
            at = self.at if entire else 0
            for shape, dst in zip(self.shapes, scratch):
                assemble(spot, refs[1:], at, dst, self.block)
                at += self.share(shape)
        return list(scratch)

    def plain_shapes(self):
        return [jax.ShapeDtypeStruct(s, BF16) for s in self.shapes] if self.packed else []

    def plain_blocks(self, steps):
        blocks = []
        for a, m, width in self.shapes if self.packed else []:
            if a % steps == 0:
                blocks.append(((a // steps, m, width), 0))
            else:
                assert m % steps == 0
                blocks.append(((a, m // steps, width), 1))
        return blocks

    def plain_specs(self, steps):
        first, second = (lambda i: (i, 0, 0)), (lambda i: (0, i, 0))
        return [pl.BlockSpec(b, second if dim else first) for b, dim in self.plain_blocks(steps)]

    def plain_store(self, outs, scratch, steps):
        i = pl.program_id(0)
        for out, src, (block, dim) in zip(outs, scratch, self.plain_blocks(steps)):
            n = block[dim]
            part = pl.ds(pl.multiple_of(i * n, n), n)
            out[...] = src[:, part, :] if dim else src[part]

    def grad_shapes(self, extra=0):
        if not self.packed:
            return [jax.ShapeDtypeStruct(s, BF16) for s in self.shapes]
        rows = sum(self.share(s) for s in self.shapes) + extra
        return [jax.ShapeDtypeStruct((INNER, self.outer, rows, self.shapes[0][2]), BF16)] * SEQ

    def grad_scratch(self):
        return [pltpu.VMEM(s, BF16) for s in self.shapes] if self.packed else []

    def place(self):
        return [self.spot] if self.packed else []

    def store(self, place, grads, outs, last):
        if not self.packed:
            return

        @pl.when(last)
        def _():
            spot = Spot(place[0], self.outer, self.far[1])
            at = 0
            for shape, src in zip(self.shapes, grads):
                deal(spot, src, at, *outs)
                at += self.share(shape)


def other_half(place_ref, ref):
    half = ref.shape[0] // 2
    return ref[pl.ds(pl.multiple_of((1 - place_ref[2]) * half, half), half), :]


def join(place_ref, own_ref, other_ref, dst):
    half = other_ref.shape[0]
    me = place_ref[2]
    dst[pl.ds(pl.multiple_of(me * half, half), half), :] = own_ref[me]
    dst[pl.ds(pl.multiple_of((1 - me) * half, half), half), :] = other_ref[...]


def cut(refs, *counts):
    out, at = [], 0
    for n in counts:
        out.append(refs[at:at + n])
        at += n
    assert at == len(refs)
    return out


def attn_fwd_kernel(cross, joined, gq, gk, steps, w, *refs):
    n_in, n_out = (5, 8) if cross else (4, 7 if joined else 6)
    n_tail = 1 if w.tail else 0
    ins, w_refs, outs, tail, plain, (kaug, vaug), xk_s, w_scr = cut(
        refs, n_in, w.n_args(), n_out, n_tail, w.n_scratch(), 2, 1 if cross else 0, w.n_scratch())
    count = kaug.shape[1]
    i = pl.program_id(0)
    start = i == 0
    w_ref, = w.load(w_refs, w_scr, start)
    if cross:
        len_ref, place_ref, rq_ref, rk_ref, g_ref = ins
        xq_ref, xk_ref, q_ref, k_ref, v_ref, o_ref, qx_ref, r_ref = outs
    else:
        len_ref, place_ref, xq_ref, xk_ref = ins
        if joined:
            own_ref, other_ref = xq_ref, xk_ref
            xk_ref, *outs = outs
        q_ref, k_ref, v_ref, o_ref, qx_ref, r_ref = outs
    rows = r_ref.shape[0]

    @pl.when(start)
    def _():
        if w.tail:
            parts = [x[k, w.share(w.shapes[0]):, :].astype(F32) for x in w_refs[1:] for k in range(w.outer)]
            tail[0][...] = sum(parts[1:], parts[0])
        if cross:
            xk = norm(rk_ref[...], row_of(g_ref, gk)).astype(BF16)
            xk_s[0][...] = xk
        else:
            if joined:
                join(place_ref, own_ref, other_ref, xk_ref)
            xk = xk_ref[...]
        k = nn(xk, w_ref[1]).astype(BF16)
        v = nn(xk, w_ref[2]).astype(BF16)
        extras = key_extras(len_ref[place_ref[3]], count)
        ones = jnp.ones((count, PAIR), BF16)
        for p in range(H // 2):
            kaug[p, :, :PAIR] = k[:, p * PAIR:(p + 1) * PAIR]
            kaug[p, :, PAIR:] = extras
            vaug[p, :, :PAIR] = v[:, p * PAIR:(p + 1) * PAIR]
            vaug[p, :, PAIR:] = ones
        k_ref[...] = k
        v_ref[...] = v

    w.plain_store(plain, w_scr, steps)
    if cross:
        xk_ref[...] = xk_s[0][pl.ds(pl.multiple_of(i * (count // steps), count // steps), count // steps), :]
        resid = norm(rq_ref[...], row_of(g_ref, gq))
        xq = resid.astype(BF16)
        xq_ref[...] = xq
    else:
        xq = xk_ref[pl.ds(pl.multiple_of(i * rows, rows), rows), :] if joined else xq_ref[...]
        resid = xq.astype(F32)
    q = nn(xq, w_ref[0]) * Q_SCALE
    q_ref[...] = q.astype(BF16)
    lane = lanes(rows)
    first = lane < HD
    extra = jnp.where(lane == 3 * H, 1.0, 0.0).astype(BF16)

    def score(h):
        p = h // 2
        mine = first if h % 2 == 0 else lane >= HD
        qm = jnp.where(mine, q[:, p * PAIR:(p + 1) * PAIR], 0.0).astype(BF16)
        return nt(jnp.concatenate([qm, extra], axis=1), kaug[p])

    halves = []
    sums = jnp.zeros((rows, PAIR), F32)
    ahead = score(0)
    for h in range(H):
        s = ahead
        if h + 1 < H:
            ahead = score(h + 1)
        m = jnp.max(s, axis=1, keepdims=True)
        o = nn(jnp.exp2(s - m).astype(BF16), vaug[h // 2])
        total = o[:, PAIR:]
        halves.append(o[:, :PAIR] / total)
        sums = jnp.where(lane == h, -(m + jnp.log2(total)), sums)
    qx_ref[...] = spread_parts(sums)
    blended = [jnp.where(first, halves[2 * p], halves[2 * p + 1]).astype(BF16) for p in range(H // 2)]
    o_all = jnp.concatenate(blended, axis=1)
    o_ref[...] = o_all
    r_ref[...] = resid + nn(o_all, w_ref[3])


def attn_forward(length, w, xq=None, xk=None, rq=None, rk=None, gq=None, gk=None, halves=None):
    cross, joined = rq is not None, halves is not None
    if joined:
        rows, width = 2 * halves[1].shape[0], halves[1].shape[1]
        count = rows
    else:
        rows, width = (rq if cross else xq).shape
        count = (rk if cross else xk).shape[0]
    blk = math.gcd(rows, 512)
    steps = rows // blk
    sds = jax.ShapeDtypeStruct
    by_rows = pl.BlockSpec((blk, width), lambda i: (i, 0))
    by_keys = pl.BlockSpec((count // steps, width), lambda i: (i, 0))
    outs = [
        sds((rows, width), BF16), sds((count, width), BF16), sds((count, width), BF16),
        sds((rows, width), BF16), sds((rows, PAIR), BF16), sds((rows, width), F32),
    ]
    out_specs = [by_rows, whole((count, width)), whole((count, width)), by_rows, pl.BlockSpec((blk, PAIR), lambda i: (i, 0)), by_rows]
    if cross:
        args = [*length, rq, rk, gq[0]]
        in_specs = [smem(), smem(), by_rows, whole((count, width)), whole(gq[0].shape)]
        outs = [sds((rows, width), BF16), sds((count, width), BF16)] + outs
        out_specs = [by_rows, by_keys] + out_specs
    elif joined:
        args = [*length, *halves]
        in_specs = [smem(), smem(), *(whole(x.shape) for x in halves)]
        outs = [sds((rows, width), BF16)] + outs
        out_specs = [whole((rows, width))] + out_specs
    else:
        args = [*length, xq, xk]
        in_specs = [smem(), smem(), by_rows, whole((count, width))]
    if w.tail:
        outs.append(sds((w.tail, width), F32))
        out_specs.append(whole((w.tail, width)))
    out = pl.pallas_call(
        functools.partial(attn_fwd_kernel, cross, joined, *((gq[1], gk[1]) if cross else (0, 0)), steps, w),
        grid=(steps,),
        in_specs=in_specs + w.specs(1),
        out_specs=out_specs + w.plain_specs(steps),
        out_shape=outs + w.plain_shapes(),
        scratch_shapes=[pltpu.VMEM((H // 2, count, 2 * PAIR), BF16)] * 2
        + ([pltpu.VMEM((count, width), BF16)] if cross else []) + w.scratch(),
        compiler_params=PARAMS,
        cost_estimate=cost(rows * count * 5 * 512 * H, 14 << 20, rows * count * H),
        name="cross_fwd" if cross else "self_fwd",
    )(*args, *w.args())
    return out if w.packed else [*out, *w.arrays]


def pair_back(p, k_ref, v_ref, q_ref, qx_ref, o, do, kaug, vaug, qaug, oaug, kt, dqt):
    count, rows = kaug.shape[0], o.shape[0]
    blk = math.gcd(count, 512)
    kaug[:, :PAIR] = k_ref[...]
    vaug[:, :PAIR] = v_ref[...]
    kt[...] = k_ref[...].T
    lane = lanes(rows)
    inner = -(o.astype(F32) * do.astype(F32))
    high = inner.astype(BF16).astype(F32)
    rest = pltpu.roll(inner - high, HD, 1)
    q, do, parts = q_ref[...].astype(F32), do.astype(F32), qx_ref[...].astype(F32)
    for h in range(2):
        mine = lane < HD if h == 0 else lane >= HD
        qaug[h, :, :PAIR] = jnp.where(mine, q, 0.0).astype(BF16)
        qaug[h, :, PAIR:] = parts_of(parts, 2 * p + h).astype(BF16)
        oaug[h, :, :PAIR] = jnp.where(mine, do, 0.0).astype(BF16)
        oaug[h, :, PAIR:] = jnp.where(mine, high, rest).astype(BF16)
    for j in range(count // blk):
        keys = slice(j * blk, (j + 1) * blk)
        dv_sum = dk_sum = None
        for h in range(2):
            pt = jnp.exp2(nt(kaug[keys, :], qaug[h]))
            dpt = nt(vaug[keys, :], oaug[h])
            ptb = pt.astype(BF16)
            dst = (pt * dpt).astype(BF16)
            dv_h = nn(ptb, oaug[h, :, :PAIR])
            dk_h = nn(dst, qaug[h, :, :PAIR])
            dq_h = nn(kt[h * HD:(h + 1) * HD, keys], dst)
            dv_sum = dv_h if h == 0 else dv_sum + dv_h
            dk_sum = dk_h if h == 0 else dk_sum + dk_h
            if j == 0:
                dqt[h * HD:(h + 1) * HD, :] = dq_h
            else:
                dqt[h * HD:(h + 1) * HD, :] += dq_h
        yield keys, (dk_sum * K_BACK).astype(BF16), dv_sum.astype(BF16)


def attn_bwd_kernel(gains, same, w, *refs):
    norms = len(gains)
    n_out = 1 if same else 2
    n_dg = 0 if same else norms
    n_send = 1 if same and w.packed else 0
    n_grad = 2 if w.packed else 1
    (len_ref, place_ref, dr_ref, w3_ref, w_ref, q_ref, k_ref, v_ref, o_ref, qx_ref), x_refs, n_refs, place, outs, send, dg_refs, dw_outs, \
        (dab, do_s, kaug, vaug, qaug, oaug, kt, ot, dqt, grads_q, grads_k, w_all), xts, dw_scr = cut(
            refs, 10, n_out, 2 * norms, len(w.place()), n_out, n_send, n_dg, n_grad, 12, n_out, w.n_scratch())
    dw_ref, = dw_scr if w.packed else dw_outs
    count = kaug.shape[0]
    rows, width = dab.shape
    p = pl.program_id(0)

    @pl.when(p == 0)
    def _():
        dab[...] = dr_ref[...].astype(BF16)
        kaug[:, PAIR:] = key_extras(len_ref[place_ref[3]], count)
        vaug[:, PAIR:] = jnp.ones((count, PAIR), BF16)
        do = nt(dab[...], w3_ref[0]).astype(BF16)
        for n in range(H // 2):
            do_s[n] = do[:, n * PAIR:(n + 1) * PAIR]

    @pl.when(p < 3)
    def _():
        w_all[:, pl.ds(pl.multiple_of(p * width, PAIR), width)] = w_ref[0]

    own = pl.ds(pl.multiple_of(p * PAIR, PAIR), PAIR)
    behind = pl.ds(pl.multiple_of(width + p * PAIR, PAIR), PAIR)
    o, do = o_ref[...], do_s[p]
    ot[own, :] = o.T
    for x, xt in zip(x_refs, xts):
        xt[own, :] = x[...].T
    for keys, dk, dv in pair_back(p, k_ref, v_ref, q_ref, qx_ref, o, do, kaug, vaug, qaug, oaug, kt, dqt):
        grads_k[keys, own] = dk
        grads_k[keys, behind] = dv
    grads_q[:, own] = (dqt[...].T * 0.125).astype(BF16)
    last = p == pl.num_programs(0) - 1

    @pl.when(last)
    def _():
        dw_ref[0] = nn(xts[0][...], grads_q[...]).astype(BF16)
        both = nn(xts[-1][...], grads_k[...]).astype(BF16)
        dw_ref[1] = both[:, :width]
        dw_ref[2] = both[:, width:]
        dw_ref[3] = nn(ot[...], dab[...]).astype(BF16)
        dxq = dr_ref[...] + nt(grads_q[...], w_all[:, :width])
        dxk = nt(grads_k[...], w_all[:, width:])
        if same:
            outs[0][...] = dxq + dxk
            if n_send:
                send[0][...] = other_half(place_ref, outs[0])
        else:
            for n, value in enumerate((dxq, dxk)):
                if n < norms:
                    gain = row_of(n_refs[2 * n + 1], gains[n])
                    value, dg_refs[n][...] = norm_back(n_refs[2 * n][...], gain, value)
                outs[n][...] = value

    w.store(place, [dw_ref], dw_outs, last)


def attn_backward(same, length, dr, w, plain, q, k, v, o, qx, xs, norms=()):
    rows, width = dr.shape
    count = k.shape[0]
    sds = jax.ShapeDtypeStruct
    pair_of = lambda n: pl.BlockSpec((n, PAIR), lambda i: (0, i))
    once = lambda shape, index=None: pl.BlockSpec(
        shape, lambda i: index or (0,) * len(shape), pipeline_mode=pl.Buffered(1))
    in_specs = [
        smem(), smem(), once((rows, width)), once((1, width, width), (3, 0, 0)),
        pl.BlockSpec((1, width, width), lambda i: (jnp.minimum(i, 2), 0, 0)),
        pair_of(rows), pair_of(count), pair_of(count), pair_of(rows),
        once((rows, PAIR)),
    ] + [pair_of(x.shape[0]) for x in xs]
    norm_args = []
    for r, g in norms:
        norm_args += [r, g[0]]
        in_specs += [once(r.shape), once(g[0].shape)]
    outs = [sds((rows, width), F32)]
    if not same:
        outs += [sds((count, width), F32)] + [sds((1, width), F32)] * len(norms)
    elif w.packed:
        outs.append(sds((rows // 2, width), F32))
    outs += w.grad_shapes()
    vm = pltpu.VMEM
    return pl.pallas_call(
        functools.partial(attn_bwd_kernel, [g[1] for _, g in norms], same, w),
        grid=(H // 2,),
        in_specs=in_specs + [smem()] * len(w.place()),
        out_specs=[whole(s.shape) for s in outs],
        out_shape=outs,
        scratch_shapes=[
            vm((rows, width), BF16), vm((H // 2, rows, PAIR), BF16),
            vm((count, 2 * PAIR), BF16), vm((count, 2 * PAIR), BF16),
            vm((2, rows, 2 * PAIR), BF16), vm((2, rows, 2 * PAIR), BF16), vm((PAIR, count), BF16), vm((width, rows), BF16),
            vm((PAIR, rows), F32), vm((rows, width), BF16), vm((count, 2 * width), BF16), vm((width, 3 * width), BF16),
        ] + [vm((width, x.shape[0]), BF16) for x in xs] + w.grad_scratch(),
        compiler_params=PARAMS,
        cost_estimate=cost(rows * count * 9 * 512 * H, 20 << 20, rows * count * H),
        name="self_bwd" if same else "cross_bwd",
    )(*length, dr, plain, plain, q, k, v, o, qx, *xs, *norm_args, *w.place())


def attn_grads_kernel(w, len_ref, place_ref, dr_ref, w3_ref, q_ref, k_ref, v_ref, o_ref, qx_ref, x_ref, grads_ref, *refs):
    dw_outs, (dab, do_s, kaug, vaug, qaug, oaug, kt, ot, xt, dqt), (dw_ref,) = cut(refs, 2, 10, 1)
    count = kaug.shape[0]
    width = dab.shape[1]
    p = pl.program_id(0)

    @pl.when(p == 0)
    def _():
        dab[...] = dr_ref[...].astype(BF16)
        kaug[:, PAIR:] = key_extras(len_ref[place_ref[3]], count)
        vaug[:, PAIR:] = jnp.ones((count, PAIR), BF16)
        do = nt(dab[...], w3_ref[0]).astype(BF16)
        for n in range(H // 2):
            do_s[n] = do[:, n * PAIR:(n + 1) * PAIR]

    own = pl.ds(pl.multiple_of(p * PAIR, PAIR), PAIR)
    part = lambda n: pl.ds(pl.multiple_of(n * width + p * PAIR, PAIR), PAIR)
    o, do = o_ref[...], do_s[p]
    ot[own, :] = o.T
    xt[own, :] = x_ref[...].T
    for keys, dk, dv in pair_back(p, k_ref, v_ref, q_ref, qx_ref, o, do, kaug, vaug, qaug, oaug, kt, dqt):
        grads_ref[keys, part(1)] = dk
        grads_ref[keys, part(2)] = dv
    grads_ref[:, part(0)] = (dqt[...].T * 0.125).astype(BF16)
    last = p == pl.num_programs(0) - 1

    @pl.when(last)
    def _():
        dw = nn(xt[...], grads_ref[...]).astype(BF16)
        for n in range(3):
            dw_ref[n] = dw[:, n * width:(n + 1) * width]
        dw_ref[3] = nn(ot[...], dab[...]).astype(BF16)

    w.store([place_ref], [dw_ref], dw_outs, last)


def attn_grads(length, dr, w, plain, q, k, v, o, qx, x):
    rows, width = dr.shape
    sds = jax.ShapeDtypeStruct
    vm = pltpu.VMEM
    once = lambda shape, index=None: pl.BlockSpec(
        shape, lambda i: index or (0,) * len(shape), pipeline_mode=pl.Buffered(1))
    pair = pl.BlockSpec((rows, PAIR), lambda i: (0, i))
    outs = [sds((rows, 3 * width), BF16)] + w.grad_shapes()
    return pl.pallas_call(
        functools.partial(attn_grads_kernel, w),
        grid=(H // 2,),
        in_specs=[smem(), smem(), once((rows, width)), once((1, width, width), (3, 0, 0))] + [pair] * 4
        + [once((rows, PAIR)), pair],
        out_specs=[whole(x.shape) for x in outs],
        out_shape=outs,
        scratch_shapes=[
            vm((rows, width), BF16), vm((H // 2, rows, PAIR), BF16), vm((rows, 2 * PAIR), BF16), vm((rows, 2 * PAIR), BF16),
            vm((2, rows, 2 * PAIR), BF16), vm((2, rows, 2 * PAIR), BF16), vm((PAIR, rows), BF16), vm((width, rows), BF16),
            vm((width, rows), BF16), vm((PAIR, rows), F32),
        ] + w.grad_scratch(),
        compiler_params=PARAMS,
        cost_estimate=cost(rows * rows * 9 * 512 * H, 14 << 20, rows * rows * H),
        name="grads_bwd",
    )(*length, dr, plain, q, k, v, o, qx, x)


def input_grad_kernel(place_ref, dr_ref, grads_ref, *refs):
    *w_refs, out_ref, send_ref = refs
    out_ref[...] = dr_ref[...] + nt(grads_ref[...], jnp.concatenate([w[0] for w in w_refs], axis=1))

    @pl.when(pl.program_id(0) != place_ref[2])
    def _():
        send_ref[...] = out_ref[...]


def input_grad(place, dr, grads, plain):
    rows, width = dr.shape
    blk = rows // SEQ
    by_rows = lambda x: pl.BlockSpec((blk, x.shape[1]), lambda i: (i, 0))
    matrix = lambda n: pl.BlockSpec((1, width, width), lambda i: (n, 0, 0))
    return pl.pallas_call(
        input_grad_kernel,
        grid=(rows // blk,),
        in_specs=[smem(), by_rows(dr), by_rows(grads)] + [matrix(n) for n in range(3)],
        out_specs=[by_rows(dr), whole((blk, width))],
        out_shape=[jax.ShapeDtypeStruct(dr.shape, F32), jax.ShapeDtypeStruct((blk, width), F32)],
        compiler_params=PARAMS,
        cost_estimate=cost(6 * rows * width * width, 9 << 20),
        name="input_grad",
    )(place, dr, grads, plain, plain, plain)


def gelu_parts(u):
    phi = 0.5 + 0.5 * lax.erf(u * math.sqrt(0.5))
    return u * phi, phi + u * jnp.exp2(u * u * (-0.5 * LOG2E)) * (1.0 / math.sqrt(2.0 * math.pi))


def ffn_fwd_kernel(gain, steps, w, *refs):
    (r_ref, g_ref), w_refs, (h_ref, a_ref, d_ref, out_ref), plain, w_scr = cut(
        refs, 2, w.n_args(), 4, w.n_scratch(), w.n_scratch())
    up_ref, down_ref = w.load(w_refs, w_scr, pl.program_id(0) == 0)
    w.plain_store(plain, w_scr, steps)
    hidden = norm(r_ref[...], row_of(g_ref, gain))
    low = hidden.astype(BF16)
    h_ref[...] = low
    total = hidden
    span = up_ref.shape[2]
    for c in range(up_ref.shape[0]):
        cols = slice(c * span, (c + 1) * span)
        act, slope = gelu_parts(nn(low, up_ref[c]))
        act = act.astype(BF16)
        a_ref[:, cols] = act
        d_ref[:, cols] = slope.astype(BF16)
        total = total + nn(act, down_ref[0, cols, :])
    out_ref[...] = total


def ffn_forward(r, gain, w):
    rows, width = r.shape
    inner = w.shapes[1][1]
    blk = math.gcd(rows, 512)
    steps = rows // blk
    sds = jax.ShapeDtypeStruct
    by_rows = lambda n: pl.BlockSpec((blk, n), lambda i: (i, 0))
    out = pl.pallas_call(
        functools.partial(ffn_fwd_kernel, gain[1], steps, w),
        grid=(steps,),
        in_specs=[by_rows(width), whole(gain[0].shape)] + w.specs(1),
        out_specs=[by_rows(width), by_rows(inner), by_rows(inner), by_rows(width)] + w.plain_specs(steps),
        out_shape=[sds((rows, width), BF16), sds((rows, inner), BF16), sds((rows, inner), BF16), sds((rows, width), F32)]
        + w.plain_shapes(),
        scratch_shapes=w.scratch(),
        compiler_params=PARAMS,
        cost_estimate=cost(12 * rows * width * inner, 17 << 20, rows * inner * 2),
        name="ffn_fwd",
    )(r, gain[0], *w.args())
    return out if w.packed else [*out, *w.arrays]


def ffn_bwd_kernel(gain, w, kind, *refs):
    n_more = {"none": 0, "slot": 2, "gains": 4}[kind]
    (dr_ref, h_ref, a_ref, d_ref, r_ref, g_ref, up_ref, down_ref), more, place, (dout_ref, dg_ref), dw_outs, \
        (low, ht, acc, r_s), dw_scr = cut(refs, 8, n_more, len(w.place()), 2, 2, 4, w.n_scratch())
    n = pl.program_id(0)
    dup_ref, ddown_ref = dw_scr if w.packed else dw_outs

    @pl.when(n == 0)
    def _():
        grad = dr_ref[...]
        acc[...] = grad
        low[...] = grad.astype(BF16)
        ht[...] = h_ref[...].T

    grad = low[...]
    some = r_ref.shape[0]
    r_s[pl.ds(pl.multiple_of(n * some, some), some), :] = r_ref[...]
    span = up_ref.shape[2]
    rows = pl.ds(pl.multiple_of(n * span, span), span)
    ddown_ref[0, rows, :] = tn(a_ref[...], grad).astype(BF16)
    du = (nt(grad, down_ref[0]) * d_ref[...].astype(F32)).astype(BF16)
    dup_ref[n] = nn(ht[...], du).astype(BF16)
    acc[...] += nt(du, up_ref[0])
    last = n == pl.num_programs(0) - 1

    @pl.when(last)
    def _():
        dout_ref[...], dg_ref[...] = norm_back(r_s[...], row_of(g_ref, gain), acc[...])

    w.store(place, [dup_ref, ddown_ref], dw_outs, last)
    if not w.packed or kind == "none":
        return
    at = sum(w.share(s) for s in w.shapes)

    @pl.when(last)
    def _():
        if kind == "slot":
            for src, dst in zip(more, dw_outs):
                dst[:, :, at:, :] = src[...]
        else:
            gains = [dg_ref] + list(more)
            row = lax.broadcasted_iota(jnp.int32, (16, dg_ref.shape[1]), 0)
            block = jnp.zeros((16, dg_ref.shape[1]), F32)
            for x, ref in enumerate(gains):
                block = jnp.where(row == x, ref[...], block)
            block = block.astype(BF16)
            for dst in dw_outs:
                for j in range(INNER):
                    for k in range(w.outer):
                        dst[j, k, at:, :] = block


def ffn_backward(dr, hidden, act, slope, w, plain, r, gain, kind="none", more=()):
    rows, width = dr.shape
    inner = w.shapes[1][1]
    span = inner // w.shapes[0][0]
    steps = inner // span
    sds = jax.ShapeDtypeStruct
    once = lambda shape: pl.BlockSpec(shape, lambda i: (0,) * len(shape), pipeline_mode=pl.Buffered(1))
    by_cols = pl.BlockSpec((rows, span), lambda i: (0, i))
    extra = {"none": 0, "slot": more[0].shape[2] if kind == "slot" else 0, "gains": 16}[kind] if w.packed else 0
    if not w.packed:
        kind, more = "none", ()
    grads = w.grad_shapes(extra)
    return pl.pallas_call(
        functools.partial(ffn_bwd_kernel, gain[1], w, kind),
        grid=(steps,),
        in_specs=[once((rows, width)), once((rows, width)), by_cols, by_cols,
                  pl.BlockSpec((rows // steps, width), lambda i: (i, 0)), once(gain[0].shape),
                  pl.BlockSpec((1, width, span), lambda i: (i, 0, 0)), pl.BlockSpec((1, span, width), lambda i: (0, i, 0))]
        + [once(x.shape) for x in more] + [smem()] * len(w.place()),
        out_specs=[whole((rows, width)), whole((1, width))] + [whole(s.shape) for s in grads],
        out_shape=[sds((rows, width), F32), sds((1, width), F32)] + grads,
        scratch_shapes=[pltpu.VMEM((rows, width), BF16), pltpu.VMEM((width, rows), BF16), pltpu.VMEM((rows, width), F32),
                        pltpu.VMEM((rows, width), F32)] + w.grad_scratch(),
        compiler_params=PARAMS,
        cost_estimate=cost(16 * rows * width * inner, 25 << 20),
        name="ffn_bwd",
    )(dr, hidden, act, slope, r, gain[0], *plain, *more, *w.place())


def slot_kernel(gain, w, halo, *refs):
    n_grad = 2 if w.packed else 1
    n_join = n_grad - 1
    (len_ref, place_ref, r_ref, g_ref, cot_ref), other, halo_refs, w_refs, (out_ref, dr_ref, dg_ref), send, dw_outs, \
        w_scr, dw_scr, joined = cut(
            refs, 5, n_join, 3 if halo else 0, w.n_args(), 3, n_join, n_grad, w.n_scratch(), w.n_scratch(), n_join)
    if other:
        join(place_ref, cot_ref, other[0], joined[0])
        cot_ref = joined[0]
    length = len_ref[place_ref[3]]
    w_ref, = w.load(w_refs, w_scr, length >= 0)
    dw_ref, = dw_scr if w.packed else dw_outs
    rows, width = r_ref.shape
    gain = row_of(g_ref, gain)
    low = norm(r_ref[...], gain).astype(BF16)
    row = lax.broadcasted_iota(jnp.int32, (rows, width), 0)
    above = below = 0.0
    place = row
    if halo:
        base_ref, next_ref, prev_ref = halo_refs
        place = row + base_ref[0]
        after = norm(next_ref[...], gain).astype(BF16)
        above = nn(after, w_ref[0, width:, :])[:1, :] * base_ref[1].astype(F32)
        below = jnp.where(base_ref[0] - 1 < length - 1, prev_ref[...].astype(F32)[:1, :], 0.0)
    live = place < length - 1
    second = nn(low, w_ref[0, width:, :])
    shifted = jnp.where(row == rows - 1, above, pltpu.roll(second, rows - 1, 0))
    out_ref[...] = jnp.where(live, nn(low, w_ref[0, :width, :]) + shifted, 0.0).astype(BF16)
    if send:
        send[0][...] = other_half(place_ref, out_ref)
    g = jnp.where(live, cot_ref[...].astype(F32), 0.0)
    before = jnp.where(row == 0, below, pltpu.roll(g, 1, 0)).astype(BF16)
    g = g.astype(BF16)
    low_t = low.T
    dw_ref[0, :width, :] = nn(low_t, g).astype(BF16)
    dw_ref[0, width:, :] = nn(low_t, before).astype(BF16)
    dy = nt(g, w_ref[0, :width, :]) + nt(before, w_ref[0, width:, :])
    dr_ref[...], dg_ref[...] = norm_back(r_ref[...], gain, dy)
    w.store(w_refs[:1], [dw_ref], dw_outs, length >= 0)


def slot_step(length, r, gain, w, cot, halo):
    rows, width = r.shape
    sds = jax.ShapeDtypeStruct
    grads = w.grad_shapes()
    full = lambda x: pl.BlockSpec(x.shape, lambda i: (0,) * len(x.shape))
    outs = [sds((rows, width), BF16), sds((rows, width), F32), sds((1, width), F32)]
    outs += ([sds((rows // 2, width), BF16)] if w.packed else []) + grads
    return pl.pallas_call(
        functools.partial(slot_kernel, gain[1], w, len(halo) > 0),
        grid=(1,),
        in_specs=[smem(), smem()] + [full(x) for x in (r, gain[0], *cot)] + [smem(), *map(full, halo[1:])][:len(halo)] + w.specs(1),
        out_specs=[full(x) for x in outs],
        out_shape=outs,
        scratch_shapes=w.scratch() + w.grad_scratch() + ([pltpu.VMEM((rows, width), BF16)] if w.packed else []),
        compiler_params=PARAMS,
        cost_estimate=cost(36 * rows * width * width, 9 << 20),
        name="slot",
    )(*length, r, gain[0], *cot, *halo, *w.args())


def turn_kernel(g_in, g_out, wf, ws, *refs):
    (len_ref, place_ref, r_ref, g_ref, cot_ref, other_ref), f_refs, s_refs, \
        (out_ref, send_ref, dr_ref, dg_in_ref, dg_out_ref), dw_outs, (h_s, a_s, d_s, r_s, acc, cot_s), \
        f_scr, s_scr, f_dw, s_dw = cut(
            refs, 6, wf.n_args(), ws.n_args(), 5, 2, 6, wf.n_scratch(), ws.n_scratch(), wf.n_scratch(), ws.n_scratch())
    length = len_ref[place_ref[3]]
    always = length >= 0
    up_ref, down_ref = wf.load(f_refs, f_scr, always, True)
    slot_ref, = ws.load(s_refs, s_scr, always, True)
    join(place_ref, cot_ref, other_ref, cot_s)
    rows, width = r_ref.shape
    span = up_ref.shape[2]
    blk = math.gcd(rows, 512)
    for b in range(rows // blk):
        part = slice(b * blk, (b + 1) * blk)
        total = norm(r_ref[part, :], row_of(g_ref, g_in))
        low_in = total.astype(BF16)
        h_s[part, :] = low_in
        for c in range(up_ref.shape[0]):
            cols = slice(c * span, (c + 1) * span)
            act, slope = gelu_parts(nn(low_in, up_ref[c]))
            act = act.astype(BF16)
            a_s[part, cols] = act
            d_s[part, cols] = slope.astype(BF16)
            total = total + nn(act, down_ref[0, cols, :])
        r_s[part, :] = total

    gain = row_of(g_ref, g_out)
    row = lax.broadcasted_iota(jnp.int32, (rows, width), 0)
    live = row < length - 1
    rounded = norm(r_s[...], gain).astype(BF16)
    second = nn(rounded, slot_ref[0, width:, :])
    second = jnp.where(row == rows - 1, 0.0, pltpu.roll(second, rows - 1, 0))
    out_ref[...] = jnp.where(live, nn(rounded, slot_ref[0, :width, :]) + second, 0.0).astype(BF16)
    send_ref[...] = other_half(place_ref, out_ref)
    g = jnp.where(live, cot_s[...].astype(F32), 0.0)
    before = jnp.where(row == 0, 0.0, pltpu.roll(g, 1, 0)).astype(BF16)
    g = g.astype(BF16)
    turned = rounded.T
    s_dw[0][0, :width, :] = nn(turned, g).astype(BF16)
    s_dw[0][0, width:, :] = nn(turned, before).astype(BF16)
    dy = nt(g, slot_ref[0, :width, :]) + nt(before, slot_ref[0, width:, :])
    grad, dg_out_ref[...] = norm_back(r_s[...], gain, dy)

    acc[...] = grad
    grad = grad.astype(BF16)
    turned = h_s[...].T
    for c in range(up_ref.shape[0]):
        cols = slice(c * span, (c + 1) * span)
        f_dw[1][0, cols, :] = tn(a_s[:, cols], grad).astype(BF16)
        du = (nt(grad, down_ref[0, cols, :]) * d_s[:, cols].astype(F32)).astype(BF16)
        f_dw[0][c] = nn(turned, du).astype(BF16)
        acc[...] += nt(du, up_ref[c])
    dr_ref[...], dg_in_ref[...] = norm_back(r_ref[...], row_of(g_ref, g_in), acc[...])
    wf.store([place_ref], f_dw, dw_outs, always)

    @pl.when(always)
    def _():
        deal(Spot(place_ref, wf.outer, ws.far[1]), s_dw[0], sum(wf.share(x) for x in wf.shapes), *dw_outs)


def turn(length, r, gain_in, gain_out, wf, ws, halves):
    rows, width = r.shape
    inner = wf.shapes[1][1]
    sds = jax.ShapeDtypeStruct
    vm = pltpu.VMEM
    outs = [sds((rows, width), BF16), sds((rows // 2, width), BF16), sds((rows, width), F32), sds((1, width), F32),
            sds((1, width), F32)] + wf.grad_shapes(sum(ws.share(x) for x in ws.shapes))
    return pl.pallas_call(
        functools.partial(turn_kernel, gain_in[1], gain_out[1], wf, ws),
        in_specs=[smem(), smem()] + [vmem()] * 4 + wf.specs(0) + ws.specs(0),
        out_specs=[vmem() for _ in outs],
        out_shape=outs,
        scratch_shapes=[vm((rows, width), BF16), vm((rows, inner), BF16), vm((rows, inner), BF16), vm((rows, width), F32),
                        vm((rows, width), F32), vm((rows, width), BF16)]
        + wf.scratch() + ws.scratch() + wf.grad_scratch() + ws.grad_scratch(),
        compiler_params=PARAMS,
        cost_estimate=cost(36 * rows * width * inner, 17 << 20, rows * inner * 2),
        name="turn",
    )(*length, r, gain_in[0], *halves, *wf.args(), *ws.args())


def pack_kernel(lane_ref, gains_ref, *refs):
    *ins, first_ref, second_ref = refs
    pieces = []
    for ref in ins:
        if len(ref.shape) == 3:
            pieces += [ref[a] for a in range(ref.shape[0])]
        elif ref.shape[1] > first_ref.shape[1]:
            width = first_ref.shape[1]
            pieces += [ref[:, a * width:(a + 1) * width] for a in range(ref.shape[1] // width)]
        else:
            pieces.append(ref[...])
        if ref is ins[0]:
            count, share = gains_ref.shape
            row = lax.broadcasted_iota(jnp.int32, (share, first_ref.shape[1]), 0)
            lane = lax.broadcasted_iota(jnp.int32, (share, first_ref.shape[1]), 1)
            spread = jnp.where(lane == row + lane_ref[0], 1.0, 0.0).astype(BF16)
            gains = nn(gains_ref[...], spread).astype(BF16)
            pieces.append(jnp.concatenate([gains, jnp.zeros((16 - count, gains.shape[1]), BF16)], axis=0))
    at = 0
    dsts = [first_ref, second_ref]
    for piece in pieces:
        if at == dsts[0].shape[0]:
            at = 0
            dsts.pop(0)
        dst = dsts[0]
        dst[at:at + piece.shape[0], :] = piece
        at += piece.shape[0]


def pack(lane, gains, *groups):
    width = groups[0][0].shape[-1]
    rows = [sum(x.size for x in xs) // width for xs in groups]
    rows[0] += 16
    arrays = [x for xs in groups for x in xs]
    return pl.pallas_call(
        pack_kernel,
        in_specs=[smem()] + [vmem()] * (1 + len(arrays)),
        out_specs=[vmem() for _ in rows],
        out_shape=[jax.ShapeDtypeStruct((n, width), BF16) for n in rows],
        name="pack",
    )(lane, gains, *arrays)


def finish_kernel(shapes, terms, lane_ref, *refs):
    *ins, outs = cut(refs, *terms, len(refs) - sum(terms))
    at_out = 0
    for group, parts in zip(shapes, ins):
        total = summed([x[...] for x in parts])
        at = 0
        for stack, share in group:
            out = outs[at_out]
            width = total.shape[1]
            for a in range(stack):
                rows = total[at:at + share, :]
                at += share
                if len(out.shape) == 3:
                    out[a] = rows
                else:
                    out[:, a * width:(a + 1) * width] = rows
            at_out += 1
        if at < total.shape[0]:
            out = outs[at_out]
            count, share = out.shape
            row = lax.broadcasted_iota(jnp.int32, (width, share), 0)
            lane = lax.broadcasted_iota(jnp.int32, (width, share), 1)
            pick = jnp.where(row == lane + lane_ref[0], 1.0, 0.0).astype(BF16)
            out[...] = nn(total[at:, :].astype(BF16), pick)[:count, :]
            at_out += 1


def finish(lane, shapes, sums, more, outs):
    groups = [[x] for x in sums] + more
    arrays = [x for g in groups for x in g]
    return pl.pallas_call(
        functools.partial(finish_kernel, shapes, [len(g) for g in groups]),
        in_specs=[smem()] + [vmem()] * len(arrays),
        out_specs=[vmem() for _ in outs],
        out_shape=[jax.ShapeDtypeStruct(s, F32) for s in outs],
        name="finish",
    )(lane, *arrays)


def exchange(x, send, *during):
    count = x.shape[0]
    me = lax.axis_index("seq")
    out = x
    for k in range(1, count):
        piece = lax.dynamic_index_in_dim(x, (me + k) % count, 0, keepdims=False) if send is None else send
        piece = hold(lax.ppermute(piece, "seq", [(s, (s + k) % count) for s in range(count)]), *during)
        out = lax.dynamic_update_index_in_dim(out, piece, (me - k) % count, 0)
    return out


def to_examples(x, count):
    examples, rows, width = x.shape
    if count == examples:
        return exchange(x, None).reshape(count * rows, width)
    me = lax.axis_index("seq")
    group = count // examples
    all_rows = lax.all_gather(x, "seq", axis=1, tiled=True)
    one = lax.dynamic_index_in_dim(all_rows, me // group, 0, keepdims=False)
    return lax.dynamic_slice_in_dim(one, (me % group) * examples * rows, examples * rows, 0)


def to_positions(x, examples, count, *during, send=None):
    width = x.shape[1]
    if count == examples:
        return exchange(x.reshape(count, -1, width), send, *during)
    me = lax.axis_index("seq")
    rows = x.shape[0] // examples
    all_rows = lax.all_gather(x, "seq", axis=0, tiled=True).reshape(examples, count * rows, width)
    return lax.dynamic_slice_in_dim(all_rows, me * rows, rows, 1)


class Ring:
    def __init__(self):
        self.dp = lax.axis_size("dp")
        self.outer = self.dp // INNER
        self.columns = [[o * INNER + i for o in range(self.outer)] for i in range(INNER)]
        self.planes = [[o * INNER + i for i in range(INNER)] for o in range(self.outer)]

    def inner_step(self, x, j):
        return lax.ppermute(x, "dp", [(d, d // INNER * INNER + (d + j) % INNER) for d in range(self.dp)])

    def outer_step(self, x, k):
        return lax.ppermute(x, "dp", [(d, (d + k * INNER) % self.dp) for d in range(self.dp)])

    def swap(self, x):
        return lax.ppermute(x, "seq", [(0, 1), (1, 0)])

    def column(self, shard, *during):
        return [shard] + [hold(self.outer_step(shard, k), *during) for k in range(1, self.outer)]

    def plane(self, column, *during):
        return [column] + [hold(self.inner_step(column, j), *during) for j in range(1, INNER)]

    def far_column(self, x):
        return lax.all_gather(x, "dp", axis=0, axis_index_groups=self.columns)

    def both(self, plane):
        return plane + [self.swap(x) for x in plane]

    def pairs(self, keep, send, *during):
        other = hold(self.swap(send), *during)
        return [keep[j] + other[j] for j in range(INNER)]

    def across(self, pairs, *during):
        return low(summed([pairs[0]] + [hold(self.inner_step(pairs[j], j), *during) for j in range(1, INNER)]))

    def pair(self, keep, send):
        return keep + self.swap(send)

    def plane_sum(self, pair):
        return lax.psum_scatter(pair, "dp", scatter_dimension=0, axis_index_groups=self.planes)

    def far_sum(self, total):
        return lax.psum_scatter(total, "dp", scatter_dimension=0, axis_index_groups=self.columns)

    def near_sum(self, total):
        return [total[0]] + [self.outer_step(total[k], k) for k in range(1, self.outer)]


def low(x):
    return x.astype(BF16)


def summed(parts):
    return sum(x.astype(F32) for x in parts)


def hold(x, *after):
    return lax.optimization_barrier((x, after))[0]


def per_device(source, canvas, source_len, canvas_len, cotangent, enc_attn, enc_up, enc_down, dec_attn, cross_attn,
               dec_up, dec_down, slot_proj, norm_gains):
    examples, _, width = source.shape
    seq = lax.axis_size("seq")
    devices = lax.axis_size("dp") * seq
    group = seq // examples
    me = lax.axis_index("seq")
    rank = lax.axis_index("dp") * seq + me
    groups = [[e * group + t for t in range(group)] for e in range(examples)]
    packed = seq == SEQ and lax.axis_size("dp") % INNER == 0 and enc_up.shape[0] % 16 == 0

    def whole_keys(x):
        return lax.all_gather(x, "seq", axis=0, tiled=True, axis_index_groups=groups) if group > 1 else x

    def own_keys(x):
        if group == 1:
            return x
        return lax.psum_scatter(x, "seq", scatter_dimension=0, tiled=True, axis_index_groups=groups)

    def neighbour(x, step):
        pairs = [(s, s + step) for s in range(seq) if 0 <= s % group + step < group]
        return lax.ppermute(x, "seq", pairs)

    def chunks(up):
        rows = up.shape[0]
        return up.reshape(rows, -1, width).transpose(1, 0, 2)

    def unchunk(up):
        return up.transpose(1, 0, 2).reshape(up.shape[1], -1)

    shards = {
        "enc": enc_attn, "dec": dec_attn, "cross": cross_attn, "eup": chunks(enc_up), "edown": enc_down[None],
        "dup": chunks(dec_up), "ddown": dec_down[None], "slot": slot_proj[None],
    }
    shapes = {name: (x.shape[0], x.shape[1] * devices, width) for name, x in shards.items()}
    flat = lambda name: shards[name].reshape(-1, width)
    dp_index = lax.axis_index("dp")
    spot = jnp.stack([dp_index // INNER, dp_index % INNER, me, me // group]).astype(jnp.int32)
    if packed:
        ring = Ring()
        share = norm_gains.shape[1]
        lane = jnp.reshape(rank * share, (1,)).astype(jnp.int32)
        late, flat5 = pack(
            lane, norm_gains, [dec_attn, enc_up, enc_down, cross_attn, slot_proj], [dec_up, dec_down])
        names = ["eup", "edown", "cross", "slot", "dup", "ddown"]
        sizes = [shapes[n][0] * shapes[n][1] // devices for n in names[:4]]
        late = ring.far_column(late)
        x5 = ring.plane(flat5)
        z1 = jnp.stack(hold(ring.column(flat("enc")), *x5))
        g1 = ring.plane(z1)
        source, canvas, cotangent = hold((source, canvas, cotangent), z1)
        late = hold(late, *g1)
        x5 = ring.far_column(jnp.stack(hold(x5, *g1)))
        g1 = ring.both(g1)
        cuts = [shapes["dec"][0] * shapes["dec"][1] // devices + 16]
        cuts.append(cuts[0] + sum(sizes[:2]))
        late = [late[:, :cuts[0]], late[:, cuts[0]:cuts[1]], late[:, cuts[1]:]]

        def make(arrays, names, far=(1, 1), **more):
            return Weights(True, arrays, [shapes[n] for n in names], spot=spot, outer=ring.outer, far=far, **more)

        w_enc = make(g1, ["enc"], (0, 0))

        def fetch_dec(during):
            return make(ring.both(ring.plane(late[0], during)), ["dec"], (1, 0), tail=16)

        def fetch_effn(before, during):
            return make(ring.both(ring.plane(hold(late[1], before), during)), ["eup", "edown"])

        def fetch_cross_slot(before, during):
            arrays = ring.both(ring.plane(hold(late[2], before), during))
            return make(arrays, ["cross"]), make(arrays, ["slot"], (1, 2), at=sizes[2])

        def fetch_dffn(before, during):
            return make([x5, hold(ring.swap(hold(x5, before)), during)], ["dup", "ddown"], (1, 2), block=True)
    else:
        def fetch(*names):
            return Weights(False, [lax.all_gather(shards[n], ("dp", "seq"), axis=1, tiled=True) for n in names],
                           [shapes[n] for n in names])
        w_enc = fetch("enc")
        fetch_dec = lambda *t: fetch("dec")
        fetch_effn = lambda *t: fetch("eup", "edown")
        fetch_cross_slot = lambda *t: (fetch("cross"), fetch("slot"))
        fetch_dffn = lambda *t: fetch("dup", "ddown")
        gains = lax.all_gather(norm_gains, ("dp", "seq"), axis=1, tiled=True).astype(F32)
    s_len, c_len = (source_len, spot), (canvas_len, spot)
    if packed:
        def halves(x):
            return x, ring.swap(lax.dynamic_index_in_dim(x, 1 - me, 0, keepdims=False))
        src, can, cot = halves(source), halves(canvas), halves(cotangent)
        src = attn_forward(s_len, w_enc, halves=src)
    else:
        src, can, cot = (to_examples(x, seq) for x in (source, canvas, cotangent))
        src_all, can_all = whole_keys(src), whole_keys(can)
        src = [src, *attn_forward(s_len, w_enc, xq=src, xk=src_all)]
    src, q_a, k_a, v_a, o_a, x_a, r_a, p_enc = src
    w_dec = fetch_dec(r_a)
    can = hold(can, r_a)
    if packed:
        can = attn_forward(c_len, w_dec, halves=can)
    else:
        can = [can, *attn_forward(c_len, w_dec, xq=can, xk=can_all)]
    can, q_b, k_b, v_b, o_b, x_b, r_c, *tail, p_dec = can
    gains = tail[0] if packed else gains
    gain = [(gains, i) for i in range(5)]
    w_effn = fetch_effn(r_a, r_c)
    h_a, act_a, slope_a, r_b, *p_effn = ffn_forward(hold(r_a, r_c), gain[0], w_effn)
    w_cross, w_slot = fetch_cross_slot(r_c, r_b)
    low_one, low_enc, q_c, k_c, v_c, o_c, x_c, r_d, p_cross = attn_forward(
        s_len, w_cross, rq=r_c, rk=whole_keys(r_b), gq=gain[2], gk=gain[1])
    w_dffn = fetch_dffn(r_b, r_d)
    if packed:
        slot_out, slot_send, dr, dg3, dg4, *d_dffn = turn(c_len, r_d, gain[3], gain[4], w_dffn, w_slot, cot)
    else:
        h_b, act_b, slope_b, r_e, *p_dffn = ffn_forward(r_d, gain[3], w_dffn)
        halo = []
        if group > 1:
            place = jnp.stack([me % group * r_e.shape[0], me % group < group - 1]).astype(jnp.int32)
            halo = [place, neighbour(r_e[:8], -1), neighbour(cot[-8:][::-1], 1)]
        slot_out, dr, dg4, *d_slot = slot_step(c_len, r_e, gain[4], w_slot, [cot], halo)
        slot_send = None
        dr, dg3, *d_dffn = ffn_backward(dr, h_b, act_b, slope_b, w_dffn, p_dffn, r_d, gain[3], "slot", d_slot)
    if not packed:
        slot_out = to_positions(slot_out, examples, seq)
    if packed:
        p1 = ring.pair(*d_dffn)
        dr = hold(dr, p1)
    alone = group == 1
    norms = [(r_c, gain[2])] + ([(r_b, gain[1])] if alone else [])
    dr_c, dr_b, dg2, *rest = attn_backward(
        False, s_len, dr, w_cross, p_cross, q_c, k_c, v_c, o_c, x_c, (low_one, low_enc), norms)
    if alone:
        dg1, *d_cross = rest
    else:
        d_cross = rest
        dr_b, dg1 = norm_back(r_b, gains[1:2], own_keys(dr_b))
    if packed:
        s1 = ring.plane_sum(p1)
    dr_a, dg0, *d_effn = ffn_backward(
        dr_b, h_a, act_a, slope_a, w_effn, p_effn, r_a, gain[0], "gains", [dg1, dg2, dg3, dg4])
    if packed:
        p2 = ring.pairs(*d_cross, dr_a)
        p3 = ring.pairs(*hold(tuple(d_effn), *p2))
        dr_c = hold(dr_c, *p3)
        z1 = ring.far_sum(s1)
    sides = 1 if alone else 2
    out = attn_backward(alone, c_len, dr_c, w_dec, p_dec, q_b, k_b, v_b, o_b, x_b, [can, can if alone else can_all][:sides])
    d_can, d_dec = out[:sides], list(out[sides:])
    can_send = d_dec.pop(0) if packed else None
    canvas_grad = d_can[0] if alone else d_can[0] + own_keys(d_can[1])
    if packed:
        s2 = ring.across(p2, canvas_grad)
        s3 = ring.across(p3, canvas_grad)
        p4 = ring.pairs(*hold(tuple(d_dec), s2, s3, z1))
        dr_a = hold(dr_a, *p4)
        z23 = ring.far_sum(jnp.concatenate([s2, s3], axis=1))
        grads, *d_enc = attn_grads(s_len, dr_a, w_enc, p_enc, q_a, k_a, v_a, o_a, x_a, src)
        canvas_grad = to_positions(canvas_grad, examples, seq, grads, send=can_send)
        slot_out = to_positions(slot_out, examples, seq, grads, send=slot_send)
        s4 = ring.across(p4, grads)
        d_enc = hold(tuple(d_enc), s4, z23)
        source_grad, source_send = input_grad(spot, dr_a, grads, p_enc)
        z4 = ring.near_sum(s4)
        p5 = ring.pairs(*d_enc, source_grad, *z4[1:])
        source_grad = to_positions(source_grad, examples, seq, send=hold(source_send, *p5))
        groups = [("dup", "ddown", "slot"), ("cross", "eup", "edown"), ("dec",), ("enc",)]
        rows_of = [[(shards[n].shape[0], shards[n].shape[1]) for n in names] for names in groups]
        like = {"enc": enc_attn, "eup": enc_up, "edown": enc_down, "dec": dec_attn, "cross": cross_attn, "dup": dec_up,
                "ddown": dec_down, "slot": slot_proj}
        outs = [like[n].shape for n in groups[0] + groups[1]] + [norm_gains.shape, dec_attn.shape, enc_attn.shape]
        done = finish(lane, rows_of[:2], hold([z1, z23], *p5), [], outs[:7])
        s5 = ring.across(p5, source_grad, canvas_grad, done[2])
        z5 = ring.near_sum(s5)
        t_dup, t_ddown, t_slot, t_cross, t_eup, t_edown, t_gains = done
        t_dec, t_enc = finish(lane, rows_of[2:], [], [z4, z5], outs[7:])
    else:
        def home(x):
            return lax.psum_scatter(x, ("dp", "seq"), scatter_dimension=1, tiled=True).astype(F32)
        t_dec, t_cross = home(d_dec[0]), home(d_cross[0])
        t_eup, t_edown, t_dup, t_ddown, t_slot = (home(x) for x in (*d_effn, *d_dffn, *d_slot))
        t_eup, t_edown, t_dup, t_ddown, t_slot = unchunk(t_eup), t_edown[0], unchunk(t_dup), t_ddown[0], t_slot[0]
        out = attn_backward(alone, s_len, dr_a, w_enc, p_enc, q_a, k_a, v_a, o_a, x_a, [src, src if alone else src_all][:sides])
        d_src, d_enc = out[:sides], out[sides:]
        source_grad = d_src[0] if alone else d_src[0] + own_keys(d_src[1])
        t_enc = home(d_enc[0])
        t_gains = home(jnp.concatenate([dg0, dg1, dg2, dg3, dg4], axis=0))
        source_grad = to_positions(source_grad, examples, seq)
        canvas_grad = to_positions(canvas_grad, examples, seq)

    return (
        slot_out, source_grad, canvas_grad,
        t_enc, t_eup, t_edown, t_dec, t_cross, t_dup, t_ddown, t_slot, t_gains,
    )


def solution(mesh):
    by_seq = P("dp", "seq", None)
    stack = P(None, ("dp", "seq"), None)
    by_row = P(("dp", "seq"), None)
    gains = P(None, ("dp", "seq"))
    in_specs = (by_seq, by_seq, P("dp"), P("dp"), by_seq, stack, by_row, by_row, stack, stack, by_row, by_row, by_row,
                gains)
    out_specs = (by_seq, by_seq, by_seq, stack, by_row, by_row, stack, stack, by_row, by_row, by_row, gains)
    return jax.shard_map(per_device, mesh=mesh, in_specs=in_specs, out_specs=out_specs, check_vma=False)
```
